32 devices in a mesh: seq: 4 (over y, core), item: 8 (over z, x).
Axes of the slice: x: 2, y: 2, z: 4, core: 2. Of those that a mesh axis runs over, the one named last changes fastest.
Arguments:
- events: float32 [8, 512, 512], P('item', 'seq'), may hold values from -6 to 6
- w_uvqk: float32 [512, 2048], replicated, may hold values from -0.25 to 0.25
- out_gain: float32 [512], replicated, may hold values from 0.5 to 1.5
- w_out: float32 [512, 512], replicated, may hold values from -0.25 to 0.25
- item_table: float32 [8192, 512], P('item'), may hold values from -0.25 to 0.25
- user_lengths: int32 [8, 4], P('item'), may hold values from 1 to 256, 512 in all within a row
- neg_ids: int32 [4, 512], replicated, may hold values from 0 to 1023
- panel_owner: int32 [4], replicated, may hold values from 0 to 7
- block_mask: int32 [8, 4], P('item', 'seq'), may hold values from 1 to 65535
- targets: int32 [8, 512], P('item', 'seq'), may hold values from 0 to 2047
Outputs:
- mean_loss: float32 [], replicated
- event_grad: float32 [8, 512, 512], P('item', 'seq')
- table_grad: float32 [8192, 512], P('item')
The draws below stay inside these ranges and needn't reach their ends.
Inputs may be any that keep to these rules, and one draw needn't show every extreme that they name: `user_lengths`: the 4 lengths of a group sum to 512, the longest is exactly 256. `neg_ids`: rows may repeat within and across panels. `panel_owner`: several panels may have one owner. `block_mask`: bit k of an entry admits negative columns 128 k to 128 k + 127 for the 128 events of that block.
All inputs are finite; a program needn't handle non-finite values.
Results may differ from the reference program's by a relative error of at most 0.0003.
Values sent between devices are 32-bit elements; how exact they have to be, the bound alone decides.
No kernel may reach another device: no remote copies, remote signals or barrier semaphores. Data moves between devices by JAX's collectives and lax.ppermute only.
A program may use at most 64 MiB of HBM per device.

```python
import math
import jax
import jax.numpy as jnp
import numpy as np
from jax import lax

D = 512
H = 16
USERS = 4
PANELS = 4
PANEL = 512
CAND_DEV = 1024
GROUP = 512
USER_MOST = 256
GROUPS = 8
TOKENS = 4096
NEG = 2048
ITEMS = 8192
N_ITEM = 8


def with_ends(result, rng, low, high):
    extent = result.shape
    spot = [jax.random.randint(jax.random.fold_in(rng, axis), (), 0, extent[axis]) for axis in range(len(extent))]
    result = result.at[tuple(spot)].set(low)
    longest = extent.index(max(extent))
    spot[longest] = (spot[longest] + 1) % extent[longest]
    return result.at[tuple(spot)].set(high)


def block_scale(stream_key, dims, shards, smallest, high):
    level, own = 1.0, jax.random.fold_in(stream_key, 6)
    for dim, parts in shards:
        heights = jnp.exp(jax.random.uniform(jax.random.fold_in(own, dim), (parts,), jnp.float32, smallest / len(shards), high / len(shards)))
        level = level * jnp.repeat(heights, dims[dim] // parts).reshape([-1 if axis == dim else 1 for axis in range(len(dims))])
    return level


def split_up(number_of, total, bound, lean):
    weights = [(1 << 20) // math.isqrt(standing ** lean) + 1 for standing in range(2, number_of + 1)]
    surplus, given = total - bound - (number_of - 1), [1] * (number_of - 1)
    while surplus > 0:
        movable = [i for i in range(number_of - 1) if given[i] < bound]
        mass, left = sum([weights[i] for i in movable]), surplus
        for i in movable:
            extra = min(bound - given[i], max(1, left * weights[i] // mass), surplus)
            given[i] = given[i] + extra
            surplus = surplus - extra
    return np.array([bound] + given)


def ragged_sizes(stream_key, count, total, limit, skew):
    if count == 2:
        one = jax.random.randint(stream_key, (), max(1, total - limit), min(limit, total - 1) + 1)
        return jnp.stack([one, total - one])
    sizes = jnp.asarray(split_up(count, total, limit, skew), jnp.int32)
    pairs = (count - 1) // 2
    giver, receiver = sizes[1:1 + 2 * pairs:2], sizes[2:2 + 2 * pairs:2]
    slack = jnp.minimum(giver - 1, limit - receiver)
    moved = jax.random.randint(jax.random.fold_in(stream_key, 1), (pairs,), 0, 1 << 20) % (slack + 1)
    sizes = sizes.at[1:1 + 2 * pairs:2].set(giver - moved).at[2:2 + 2 * pairs:2].set(receiver + moved)
    return sizes[jax.random.permutation(jax.random.fold_in(stream_key, 2), count)]


def centred(key, shape, deviation, bound, cuts=(), kind=jnp.bfloat16):
    entries = deviation * jax.random.normal(key, shape, jnp.float32)
    if cuts:
        entries = entries * block_scale(key, shape, cuts, -0.22, 0.18)
    return jnp.clip(entries, -bound, bound).astype(kind)


def setup_inputs(seed: int = 0) -> dict:
    keys = jax.random.split(jax.random.key(seed), 11)
    events = centred(keys[0], (GROUPS, GROUP, D), 1.0, 6.0, ((0, 8), (1, 4)), jnp.float32)
    w_uvqk = centred(keys[1], (D, 4 * D), D ** -0.5, 0.25, (), jnp.float32)
    out_gain = jnp.clip(1.0 + 0.1 * jax.random.normal(keys[2], (D,), jnp.float32), 0.5, 1.5)
    w_out = centred(keys[3], (D, D), D ** -0.5, 0.25, (), jnp.float32)
    item_table = centred(keys[4], (ITEMS, D), D ** -0.5, 0.25, ((0, 8),), jnp.float32)
    user_lengths = jax.vmap(lambda own: ragged_sizes(own, USERS, GROUP, USER_MOST, 2))(jax.random.split(keys[5], GROUPS)).reshape((GROUPS, USERS)).astype(jnp.int32)
    neg_ids = with_ends(jax.random.randint(keys[6], (PANELS, PANEL), 0, CAND_DEV), jax.random.fold_in(keys[6], 1), 0, CAND_DEV - 1).astype(jnp.int32)
    panel_owner = with_ends(jax.random.randint(keys[7], (PANELS,), 0, N_ITEM), jax.random.fold_in(keys[7], 1), 0, N_ITEM - 1).astype(jnp.int32)
    block_mask = with_ends(jax.random.randint(keys[8], (GROUPS, GROUP // 128), 1, 2 ** (NEG // 128)), jax.random.fold_in(keys[8], 1), 1, (2 ** (NEG // 128)) - 1).astype(jnp.int32)
    targets = with_ends(jax.random.randint(keys[9], (GROUPS, GROUP), 0, NEG), jax.random.fold_in(keys[9], 1), 0, NEG - 1).astype(jnp.int32)
    return dict(events=events, w_uvqk=w_uvqk, out_gain=out_gain, w_out=w_out, item_table=item_table, user_lengths=user_lengths, neg_ids=neg_ids, panel_owner=panel_owner, block_mask=block_mask, targets=targets)


highest = lax.Precision.HIGHEST
beta_weight = 0.75
epsilon = 1e-05

def user_index(lengths, positions):
    user_ends = jnp.cumsum(lengths).astype(jnp.int32)
    return lax.optimization_barrier(jnp.sum((positions[:, None] >= user_ends[None, :]).astype(jnp.int32), axis=1))

def loss_terms(outputs, negatives, mask_words, target_cols):
    logits = jnp.einsum('td,nd->tn', outputs, negatives, precision=highest)
    columns = jnp.arange(negatives.shape[0], dtype=jnp.int32)
    mask_bits = jnp.repeat(mask_words, 128)
    live_cols = jnp.bitwise_and(jnp.right_shift(mask_bits[:, None], columns[None, :] // 128), 1).astype(logits.dtype)
    is_target = (columns[None, :] == target_cols[:, None]).astype(logits.dtype)
    neg_weight = live_cols * (1.0 - is_target)
    loss_part = jnp.sum(beta_weight * is_target * jax.nn.softplus(-logits) + neg_weight * jax.nn.softplus(logits))
    grad_logits = neg_weight * jax.nn.sigmoid(logits) - beta_weight * is_target * jax.nn.sigmoid(-logits)
    grad_rows = jnp.dot(grad_logits, negatives, precision=highest)
    panel_part = jnp.einsum('tn,td->nd', grad_logits, outputs, precision=highest)
    return (loss_part, grad_rows, panel_part)

def hstu_group(rows_in, lengths, w_uvqk, out_gain, w_out):
    group_len, width = rows_in.shape
    projected = jax.nn.silu(jnp.dot(rows_in, w_uvqk, precision=highest))
    gates_u = projected[:, :width]
    packed = projected[:, width:].reshape(group_len, 3, H, width // H)
    positions = jnp.arange(group_len, dtype=jnp.int32)
    user_ids = user_index(lengths, positions)
    allowed = ((user_ids[:, None] == user_ids[None, :]) & (positions[:, None] >= positions[None, :])).astype(rows_in.dtype)

    def one_head(stacked):
        scores = jnp.dot(stacked[:, 1], stacked[:, 2].T, precision=highest)
        return jnp.dot(jax.nn.silu(scores) * allowed, stacked[:, 0], precision=highest)
    attended = lax.map(one_head, jnp.transpose(packed, (2, 0, 1, 3)))
    attended = jnp.transpose(attended, (1, 0, 2)).reshape(group_len, width)
    row_mean = lax.optimization_barrier(jnp.mean(attended, axis=1, keepdims=True))
    centered = attended - row_mean
    variance = lax.optimization_barrier(jnp.mean(centered * centered, axis=1, keepdims=True))
    normed = centered * lax.rsqrt(variance + epsilon) * out_gain
    return rows_in + jnp.dot(normed * gates_u, w_out, precision=highest)

def reference(events, w_uvqk, out_gain, w_out, item_table, user_lengths, neg_ids, panel_owner, block_mask, targets):
    table_rows = (panel_owner[:, None] * CAND_DEV + neg_ids).reshape(-1).astype(jnp.int32)
    negatives = item_table[table_rows]

    def group_step(running, group_args):
        loss_sum, panel_sum = running
        rows_in, lengths, mask_words, target_cols = group_args
        outputs = hstu_group(rows_in, lengths, w_uvqk, out_gain, w_out)
        loss_part, grad_rows, panel_part = loss_terms(outputs, negatives, mask_words, target_cols)
        return ((loss_sum + loss_part, panel_sum + panel_part), grad_rows)
    start_carry = (jnp.zeros((), jnp.float32), jnp.zeros(negatives.shape, jnp.float32))
    (loss_total, panel_total), event_grad = lax.scan(group_step, start_carry, (events, user_lengths, block_mask, targets))
    table_grad = jnp.zeros_like(item_table).at[table_rows].add(panel_total)
    return (loss_total / TOKENS, event_grad, table_grad)
```

```python
import jax
import jax.numpy as jnp
from jax import lax
from jax.sharding import PartitionSpec as P

H = 16


high = lax.Precision.HIGH
beta_weight = 0.75
epsilon = 1e-05


def swap(block, axis, bit):
    size = lax.axis_size(axis)
    return lax.ppermute(block, axis, [(i, i ^ (1 << bit)) for i in range(size)])


def bits_of(size):
    return list(range(size.bit_length() - 1))[::-1]


def gather_steps(block, axis, bits):
    stacked, order = block[None], [0]
    for bit in bits:
        stacked = jnp.concatenate([stacked, swap(stacked, axis, bit)], axis=0)
        order = order + [r ^ (1 << bit) for r in order]
    return stacked, order


def reduce_steps(stacked, axis, bits):
    for bit in bits:
        half = stacked.shape[0] // 2
        stacked = stacked[:half] + swap(stacked[half:], axis, bit)
    return stacked[0]


def orders(bits):
    order = [0]
    for bit in bits:
        order = order + [r ^ (1 << bit) for r in order]
    return order


def per_device(
    events,
    w_uvqk,
    out_gain,
    w_out,
    item_table,
    user_lengths,
    neg_ids,
    panel_owner,
    block_mask,
    targets,
):
    rows_in = events[0]
    tok, width = rows_in.shape
    n_seq, n_item = lax.axis_size("seq"), lax.axis_size("item")
    s, i = lax.axis_index("seq"), lax.axis_index("item")
    group_len = tok * n_seq
    head_size = width // H
    seq_bits, item_bits = bits_of(n_seq), bits_of(n_item)
    seq_order, item_order = orders(seq_bits), orders(item_bits)
    seq_rel = s ^ jnp.array(seq_order, jnp.int32)
    item_rel = i ^ jnp.array(item_order, jnp.int32)

    flat_ids = neg_ids.reshape(-1)
    n_neg = flat_ids.shape[0] // n_seq
    per_panel = neg_ids.shape[1] // n_neg
    n_part = n_neg // n_item
    ids_by_seq = flat_ids.reshape(n_seq, n_neg)
    own_ids = ids_by_seq[s]
    root = panel_owner[s // per_panel]
    ids_rel = own_ids.reshape(n_item, n_part)[item_rel]
    part = item_table[ids_rel.reshape(-1)].reshape(n_item, n_part, width)
    for bit in item_bits[::-1]:
        half = part.shape[0] // 2
        other = swap(part[half:], "item", bit)
        part = jnp.where(((i ^ root) >> bit) & 1 == 0, part[:half], other)
    negatives, _ = gather_steps(part[0], "item", item_bits)
    negatives = negatives[item_rel_inverse(item_order, i)].reshape(n_neg, width)

    extra = jnp.zeros((8, width), jnp.float32)
    extra = extra.at[0, :tok].set(targets[0].astype(jnp.float32))
    extra = extra.at[1, : block_mask.shape[1]].set(block_mask[0].astype(jnp.float32))
    with_extra = jnp.concatenate([rows_in, extra], axis=0)
    group, _ = gather_steps(with_extra, "seq", seq_bits)
    group_events = group[:, :tok].reshape(group_len, width)
    group_targets = group[:, tok, :tok].astype(jnp.int32).reshape(-1)
    mask_words = group[:, tok + 1, : block_mask.shape[1]].astype(jnp.int32).reshape(-1)

    positions = (seq_rel[:, None] * tok + jnp.arange(tok, dtype=jnp.int32)[None, :]).reshape(-1)
    user_ends = jnp.cumsum(user_lengths[0])
    user_ids = jnp.sum((positions[:, None] >= user_ends[None, :]).astype(jnp.int32), axis=1)

    own = jax.nn.silu(
        jnp.dot(
            rows_in,
            jnp.concatenate([w_uvqk[:, :width], w_uvqk[:, 2 * width : 3 * width]], axis=1),
            precision=high,
        )
    )
    gates_u, queries = own[:, :width], own[:, width:].reshape(tok, H, head_size)
    values = jax.nn.silu(jnp.dot(group_events, w_uvqk[:, width : 2 * width], precision=high))
    keys = jax.nn.silu(jnp.dot(group_events, w_uvqk[:, 3 * width :], precision=high))
    values = values.reshape(group_len, H, head_size)
    keys = keys.reshape(group_len, H, head_size)
    scores = jnp.einsum("qhd,khd->hqk", queries, keys, precision=high)
    allowed = (user_ids[:tok, None] == user_ids[None, :]) & (
        positions[:tok, None] >= positions[None, :]
    )
    weights = jax.nn.silu(scores) * allowed[None, :, :].astype(jnp.float32)
    attended = jnp.einsum("hqk,khd->qhd", weights, values, precision=high).reshape(tok, width)
    row_mean = jnp.mean(attended, axis=1, keepdims=True)
    centered = attended - row_mean
    variance = jnp.mean(centered * centered, axis=1, keepdims=True)
    normed = centered * lax.rsqrt(variance + epsilon) * out_gain
    own_outputs = rows_in + jnp.dot(normed * gates_u, w_out, precision=high)
    outputs, _ = gather_steps(own_outputs, "seq", seq_bits)
    outputs = outputs.reshape(group_len, width)

    logits = jnp.einsum("td,nd->tn", outputs, negatives, precision=high)
    columns = s * n_neg + jnp.arange(n_neg, dtype=jnp.int32)
    mask_bits = jnp.repeat(mask_words, 128)
    live_cols = jnp.bitwise_and(
        jnp.right_shift(mask_bits[:, None], columns[None, :] // 128), 1
    ).astype(jnp.float32)
    is_target = (columns[None, :] == group_targets[:, None]).astype(jnp.float32)
    neg_weight = live_cols * (1.0 - is_target)
    loss_part = jnp.sum(
        beta_weight * is_target * jax.nn.softplus(-logits) + neg_weight * jax.nn.softplus(logits)
    )
    grad_logits = neg_weight * jax.nn.sigmoid(logits) - beta_weight * is_target * jax.nn.sigmoid(
        -logits
    )
    panel_part = jnp.einsum("td,tn->dn", outputs, grad_logits, precision=high)
    grad_rows = jnp.dot(grad_logits, negatives, precision=high)
    event_grad = reduce_steps(grad_rows.reshape(n_seq, tok, width), "seq", seq_bits[::-1])

    n_dim = width // (n_seq * n_item)
    panel_part = panel_part.reshape(n_seq, n_item, n_dim, n_neg)
    panel_part = panel_part.transpose(1, 0, 2, 3)[item_rel]
    panel_sum = reduce_steps(panel_part, "item", item_bits[::-1])
    panel_sum = panel_sum[seq_rel]
    moved = panel_sum[:, None]
    for bit in seq_bits[::-1]:
        half = moved.shape[0] // 2
        moved = jnp.concatenate([moved[:half], swap(moved[half:], "seq", bit)], axis=1)
    moved = moved[0]
    moved_order = orders(seq_bits[::-1])
    source_seq = s ^ jnp.array(moved_order, jnp.int32)
    rows = jnp.arange(item_table.shape[0], dtype=jnp.int32)
    hot = (ids_by_seq[source_seq][:, :, None] == rows[None, None, :]).astype(jnp.float32)
    spread = jnp.einsum("pdc,pcr->pdr", moved, hot, precision=high)
    owner = panel_owner[source_seq // per_panel]
    mine = (owner[None, :] == jnp.arange(n_item, dtype=jnp.int32)[:, None]).astype(jnp.float32)
    sent = jnp.sum(mine[:, :, None, None] * spread[None], axis=1)
    taken = lax.all_to_all(sent, "item", split_axis=0, concat_axis=0, tiled=True)
    quarter = taken.reshape(n_item * n_dim, -1).T
    table, _ = gather_steps(quarter, "seq", seq_bits)
    table_grad = jnp.concatenate(
        [table[k] for k in range(n_seq)], axis=1
    ).reshape(-1, n_seq, n_item * n_dim)[:, item_rel_inverse(seq_order, s)].reshape(-1, width)

    losses = lax.all_gather(jnp.full((8, 128), loss_part), ("seq", "item"))
    loss_total = jnp.sum(losses[:, 0, 0])
    return (loss_total / (group_len * n_item), event_grad[None], table_grad)


def item_rel_inverse(order, index):
    place = [0] * len(order)
    for k, r in enumerate(order):
        place[r] = k
    return jnp.array(place, jnp.int32)[index ^ jnp.arange(len(order), dtype=jnp.int32)]


def solution(mesh):
    placed = (
        P("item", "seq", None),
        P(),
        P(),
        P(),
        P("item", None),
        P("item", None),
        P(),
        P(),
        P("item", "seq"),
        P("item", "seq"),
    )
    return jax.shard_map(
        per_device,
        mesh=mesh,
        in_specs=placed,
        out_specs=(P(), P("item", "seq", None), P("item", None)),
        check_vma=False,
    )
```

```python
import jax
import jax.numpy as jnp
from jax import lax
from jax.sharding import PartitionSpec as P

H = 16


high = lax.Precision.HIGH
beta_weight = 0.75
epsilon = 1e-05


def swap(block, axis, bit):
    size = lax.axis_size(axis)
    return lax.ppermute(block, axis, [(i, i ^ (1 << bit)) for i in range(size)])


def bits_of(size):
    return list(range(size.bit_length() - 1))[::-1]


def two_orders(size):
    up = bits_of(size)
    return [up, up[:-2] + up[:-3:-1]]


def gather_steps(block, axis, bits):
    stacked, order = block[None], [0]
    for bit in bits:
        stacked = jnp.concatenate([stacked, swap(stacked, axis, bit)], axis=0)
        order = order + [r ^ (1 << bit) for r in order]
    return stacked, order


def reduce_steps(stacked, axis, bits):
    for bit in bits:
        half = stacked.shape[0] // 2
        stacked = stacked[:half] + swap(stacked[half:], axis, bit)
    return stacked[0]


def orders(bits):
    order = [0]
    for bit in bits:
        order = order + [r ^ (1 << bit) for r in order]
    return order


def per_device(
    events,
    w_uvqk,
    out_gain,
    w_out,
    item_table,
    user_lengths,
    neg_ids,
    panel_owner,
    block_mask,
    targets,
):
    rows_in = events[0]
    tok, width = rows_in.shape
    n_seq, n_item = lax.axis_size("seq"), lax.axis_size("item")
    s, i = lax.axis_index("seq"), lax.axis_index("item")
    group_len = tok * n_seq
    head_size = width // H
    seq_bits = bits_of(n_seq)
    seq_order = orders(seq_bits)
    seq_rel = s ^ jnp.array(seq_order, jnp.int32)

    flat_ids = neg_ids.reshape(-1)
    n_neg = flat_ids.shape[0] // n_seq
    per_panel = neg_ids.shape[1] // n_neg
    n_part = n_neg // (2 * n_item)
    ids_by_seq = flat_ids.reshape(n_seq, n_neg)
    own_ids = ids_by_seq[s].reshape(2, n_item, n_part)
    root = panel_owner[s // per_panel]
    bit_lists = two_orders(n_item)
    negatives = []
    for half, bits in enumerate(bit_lists):
        order = orders(bits)
        rel = i ^ jnp.array(order, jnp.int32)
        part = item_table[own_ids[half][rel].reshape(-1)].reshape(n_item, n_part, width)
        for bit in bits[:0:-1]:
            cut = part.shape[0] // 2
            other = swap(part[cut:], "item", bit)
            part = jnp.where(((i ^ root) >> bit) & 1 == 0, part[:cut], other)
        other = swap(part, "item", bits[0])
        same = ((i ^ root) >> bits[0]) & 1 == 0
        part = jnp.where(same, part, jnp.concatenate([other[1:], other[:1]], axis=0))
        for bit in bits[1:]:
            part = jnp.concatenate([part, swap(part, "item", bit)], axis=0)
        negatives.append(part[item_rel_inverse(order, i)].reshape(n_neg // 2, width))
    negatives = jnp.concatenate(negatives, axis=0)

    extra = jnp.zeros((8, width), jnp.float32)
    extra = extra.at[0, :tok].set(targets[0].astype(jnp.float32))
    extra = extra.at[1, : block_mask.shape[1]].set(block_mask[0].astype(jnp.float32))
    with_extra = jnp.concatenate([rows_in, extra], axis=0)
    group, _ = gather_steps(with_extra, "seq", seq_bits)
    group_events = group[:, :tok].reshape(group_len, width)
    group_targets = group[:, tok, :tok].astype(jnp.int32).reshape(-1)
    mask_words = group[:, tok + 1, : block_mask.shape[1]].astype(jnp.int32).reshape(-1)

    positions = (seq_rel[:, None] * tok + jnp.arange(tok, dtype=jnp.int32)[None, :]).reshape(-1)
    user_ends = jnp.cumsum(user_lengths[0])
    user_ids = jnp.sum((positions[:, None] >= user_ends[None, :]).astype(jnp.int32), axis=1)

    own = jax.nn.silu(
        jnp.dot(
            rows_in,
            jnp.concatenate([w_uvqk[:, :width], w_uvqk[:, 2 * width : 3 * width]], axis=1),
            precision=high,
        )
    )
    gates_u, queries = own[:, :width], own[:, width:].reshape(tok, H, head_size)
    values = jax.nn.silu(jnp.dot(group_events, w_uvqk[:, width : 2 * width], precision=high))
    keys = jax.nn.silu(jnp.dot(group_events, w_uvqk[:, 3 * width :], precision=high))
    values = values.reshape(group_len, H, head_size)
    keys = keys.reshape(group_len, H, head_size)
    scores = jnp.einsum("qhd,khd->hqk", queries, keys, precision=high)
    allowed = (user_ids[:tok, None] == user_ids[None, :]) & (
        positions[:tok, None] >= positions[None, :]
    )
    weights = jax.nn.silu(scores) * allowed[None, :, :].astype(jnp.float32)
    attended = jnp.einsum("hqk,khd->qhd", weights, values, precision=high).reshape(tok, width)
    row_mean = jnp.mean(attended, axis=1, keepdims=True)
    centered = attended - row_mean
    variance = jnp.mean(centered * centered, axis=1, keepdims=True)
    normed = centered * lax.rsqrt(variance + epsilon) * out_gain
    own_outputs = rows_in + jnp.dot(normed * gates_u, w_out, precision=high)
    outputs, _ = gather_steps(own_outputs, "seq", seq_bits)
    outputs = outputs.reshape(group_len, width)

    logits = jnp.einsum("td,nd->tn", outputs, negatives, precision=high)
    columns = s * n_neg + jnp.arange(n_neg, dtype=jnp.int32)
    mask_bits = jnp.repeat(mask_words, 128)
    live_cols = jnp.bitwise_and(
        jnp.right_shift(mask_bits[:, None], columns[None, :] // 128), 1
    ).astype(jnp.float32)
    is_target = (columns[None, :] == group_targets[:, None]).astype(jnp.float32)
    neg_weight = live_cols * (1.0 - is_target)
    loss_part = jnp.sum(
        beta_weight * is_target * jax.nn.softplus(-logits) + neg_weight * jax.nn.softplus(logits)
    )
    grad_logits = neg_weight * jax.nn.sigmoid(logits) - beta_weight * is_target * jax.nn.sigmoid(
        -logits
    )
    panel_part = jnp.einsum("td,tn->dn", outputs, grad_logits, precision=high)
    grad_rows = jnp.dot(grad_logits, negatives, precision=high)
    event_grad = reduce_steps(grad_rows.reshape(n_seq, tok, width), "seq", seq_bits[::-1])

    n_dim = width // (n_seq * n_item)
    panel_part = panel_part.reshape(n_seq, n_item, 2, n_dim // 2, n_neg).transpose(2, 1, 0, 3, 4)
    sums = []
    for half, bits in enumerate(bit_lists):
        rel = i ^ jnp.array(orders(bits), jnp.int32)
        sums.append(reduce_steps(panel_part[half][rel], "item", bits[::-1]))
    panel_sum = jnp.concatenate(sums, axis=1)
    panel_sum = panel_sum[seq_rel]
    moved = panel_sum[:, None]
    for bit in seq_bits[::-1]:
        half = moved.shape[0] // 2
        moved = jnp.concatenate([moved[:half], swap(moved[half:], "seq", bit)], axis=1)
    moved = moved[0]
    moved_order = orders(seq_bits[::-1])
    source_seq = s ^ jnp.array(moved_order, jnp.int32)
    rows = jnp.arange(item_table.shape[0], dtype=jnp.int32)
    hot = (ids_by_seq[source_seq][:, :, None] == rows[None, None, :]).astype(jnp.float32)
    spread = jnp.einsum("pdc,pcr->pdr", moved, hot, precision=high)
    owner = panel_owner[source_seq // per_panel]
    mine = (owner[None, :] == jnp.arange(n_item, dtype=jnp.int32)[:, None]).astype(jnp.float32)
    sent = jnp.sum(mine[:, :, None, None] * spread[None], axis=1)
    taken = lax.all_to_all(sent, "item", split_axis=0, concat_axis=0, tiled=True)
    quarter = taken.reshape(n_item * n_dim, -1).T
    table, _ = gather_steps(quarter, "seq", seq_bits)
    table_grad = jnp.concatenate(
        [table[k] for k in range(n_seq)], axis=1
    ).reshape(-1, n_seq, n_item * n_dim)[:, item_rel_inverse(seq_order, s)].reshape(-1, width)

    loss_total = jnp.full((8, 128), loss_part)
    for axis, size in (("seq", n_seq), ("item", n_item)):
        for bit in bits_of(size):
            loss_total = loss_total + swap(loss_total, axis, bit)
    loss_total = loss_total[0, 0]
    return (loss_total / (group_len * n_item), event_grad[None], table_grad)


def item_rel_inverse(order, index):
    place = [0] * len(order)
    for k, r in enumerate(order):
        place[r] = k
    return jnp.array(place, jnp.int32)[index ^ jnp.arange(len(order), dtype=jnp.int32)]


def solution(mesh):
    placed = (
        P("item", "seq", None),
        P(),
        P(),
        P(),
        P("item", None),
        P("item", None),
        P(),
        P(),
        P("item", "seq"),
        P("item", "seq"),
    )
    return jax.shard_map(
        per_device,
        mesh=mesh,
        in_specs=placed,
        out_specs=(P(), P("item", "seq", None), P("item", None)),
        check_vma=False,
    )
```

```python
import functools

import jax
import jax.numpy as jnp
from jax import lax
from jax.experimental import pallas as pl
from jax.experimental.pallas import tpu as pltpu
from jax.sharding import PartitionSpec as P

H = 16
LANES = 128
EXTRA = 8

beta_weight = 0.75
epsilon = 1e-05

f32, bf16, i32 = jnp.float32, jnp.bfloat16, jnp.int32
high = lax.Precision.HIGH
NN, NT = ((1,), (0,)), ((1,), (1,))
params = pltpu.CompilerParams(vmem_limit_bytes=40 * 2**20)


def swap(block, axis, bit):
    size = lax.axis_size(axis)
    return lax.ppermute(block, axis, [(i, i ^ (1 << bit)) for i in range(size)])


def bits_of(size):
    return list(range(size.bit_length() - 1))[::-1]


def two_orders(size):
    up = bits_of(size)
    return [up, up[:-2] + up[:-3:-1]]


def orders(bits):
    order = [0]
    for bit in bits:
        order = order + [r ^ (1 << bit) for r in order]
    return order


def gather_pieces(block, axis, bits):
    pieces = [block]
    for bit in bits:
        pieces = pieces + [swap(piece, axis, bit) for piece in pieces]
    return pieces


def reduce_steps(kept, sent, axis, bits):
    for n, bit in enumerate(bits):
        got = swap(sent, axis, bit)
        if n == len(bits) - 1:
            return (kept + got)[0]
        half = kept.shape[0] // 2
        sent = kept[half:] + got[half:]
        kept = kept[:half] + got[:half]


def true_order(stacked, order, index):
    place = [0] * len(order)
    for k, r in enumerate(order):
        place[r] = k
    return stacked[jnp.array(place, i32)[index ^ jnp.arange(len(order), dtype=i32)]]


def split(x):
    top = x.astype(bf16)
    return top, (x - top.astype(f32)).astype(bf16)


def dot(a, b, dims):
    return lax.dot_general(a, b, (dims, ((), ())), preferred_element_type=f32)


def dot3(a, b, dims):
    return dot(a[0], b[0], dims) + (dot(a[0], b[1], dims) + dot(a[1], b[0], dims))


def silu(x):
    return x / (1.0 + jnp.exp(jnp.minimum(-x, 87.0)))


def prepare_kernel(x_ref, u_ref, v_ref, q_ref, k_ref, wo_ref, gates_ref, queries_ref, vk_hi, vk_lo, wo_hi, wo_lo):
    x = split(x_ref[...])
    uq = split(jnp.concatenate([u_ref[...], q_ref[...]], axis=1))
    both = silu(dot3(x, uq, NN))
    gates_ref[...] = both[:, :LANES]
    queries_ref[...] = both[:, LANES:]
    vk_hi[0], vk_lo[0] = split(jnp.concatenate([v_ref[...], k_ref[...]], axis=1))
    wo_hi[...], wo_lo[...] = split(wo_ref[...])


def prepare(rows_in, w_uvqk, w_out):
    tok, width = rows_in.shape
    n = width // LANES

    def column(part):
        return pl.BlockSpec((width, LANES), lambda j: (0, part * n + j))

    own = pl.BlockSpec((tok, LANES), lambda j: (0, j))
    pair = pl.BlockSpec((1, width, 2 * LANES), lambda j: (j, 0, 0))
    rows = pl.BlockSpec((LANES, width), lambda j: (j, 0))
    return pl.pallas_call(
        prepare_kernel,
        grid=(n,),
        in_specs=[pl.BlockSpec((tok, width), lambda j: (0, 0)), *[column(p) for p in range(4)], rows],
        out_specs=[own, own, pair, pair, rows, rows],
        out_shape=[jax.ShapeDtypeStruct((tok, width), f32)] * 2
        + [jax.ShapeDtypeStruct((n, width, 2 * LANES), bf16)] * 2
        + [jax.ShapeDtypeStruct((width, width), bf16)] * 2,
        compiler_params=params,
        cost_estimate=pl.CostEstimate(flops=8 * tok * width * width, bytes_accessed=6 * width * width * 4, transcendentals=0),
        name="prepare",
    )(rows_in, w_uvqk, w_uvqk, w_uvqk, w_uvqk, w_out)


def attend_kernel(order, n_seq, meta, *refs):
    x_refs, (q_ref, vk_hi, vk_lo, out_ref, x_hi, x_lo, allowed) = refs[:n_seq], refs[n_seq:]
    tok = q_ref.shape[0]
    head = x_hi.shape[1] // H

    @pl.when(pl.program_id(0) == 0)
    def _():
        me = meta[0]
        q_pos = me * tok + lax.broadcasted_iota(i32, (tok, tok), 0)
        col = lax.broadcasted_iota(i32, (tok, tok), 1)

        def user(pos):
            ids, end = jnp.zeros_like(pos), 0
            for k in range(meta.shape[0] - 1):
                end = end + meta[1 + k]
                ids = ids + (pos >= end).astype(i32)
            return ids

        q_user = user(q_pos)
        for n in range(n_seq):
            span = pl.ds(n * tok, tok)
            x_hi[span], x_lo[span] = split(x_refs[n][...])
            k_pos = (me ^ order[n]) * tok + col
            seen = (q_user == user(k_pos)) & (q_pos >= k_pos)
            allowed[:, span] = seen.astype(f32)

    x = (x_hi[...], x_lo[...])
    vk = silu(dot3(x, (vk_hi[0], vk_lo[0]), NN))
    v_hi, v_lo = split(vk[:, :LANES])
    k_hi, k_lo = split(vk[:, LANES:])
    k_both = jnp.concatenate([k_hi, k_lo], axis=1)
    v_both = jnp.concatenate([v_hi, v_lo], axis=1)
    queries = q_ref[...]
    of_head = lax.broadcasted_iota(i32, (tok, LANES), 1) // head
    total = jnp.zeros((tok, LANES), f32)
    for h in range(LANES // head):
        q_hi, q_lo = split(jnp.where(of_head == h, queries, 0.0))
        scores = dot(jnp.concatenate([q_hi, q_hi], axis=1), k_both, NT) + dot(q_lo, k_hi, NT)
        w_hi, w_lo = split(silu(scores) * allowed[...])
        wide = dot(w_hi, v_both, NN)
        mine = wide[:, :LANES] + wide[:, LANES:] + dot(w_lo, v_hi, NN)
        total = jnp.where(of_head == h, mine, total)
    out_ref[...] = total


def attend(meta, pieces, order, queries, vk_hi, vk_lo, first, count):
    tok, width = pieces[0].shape
    n_seq = len(pieces)
    whole = pl.BlockSpec((tok, width), lambda j: (0, 0))
    pair = pl.BlockSpec((1, width, 2 * LANES), lambda j: (first + j, 0, 0))
    return pl.pallas_call(
        functools.partial(attend_kernel, order, n_seq),
        grid=(count,),
        in_specs=[pl.BlockSpec(memory_space=pltpu.SMEM)]
        + [whole] * n_seq
        + [pl.BlockSpec((tok, LANES), lambda j: (0, first + j)), pair, pair],
        out_specs=pl.BlockSpec((tok, LANES), lambda j: (0, j)),
        out_shape=jax.ShapeDtypeStruct((tok, count * LANES), f32),
        scratch_shapes=[
            pltpu.VMEM((n_seq * tok, width), bf16),
            pltpu.VMEM((n_seq * tok, width), bf16),
            pltpu.VMEM((tok, n_seq * tok), f32),
        ],
        compiler_params=params,
        cost_estimate=pl.CostEstimate(flops=count * 2000000000, bytes_accessed=2 * width * width * 4, transcendentals=0),
        name="attend",
    )(meta, *pieces, queries, vk_hi, vk_lo)


def project_kernel(n_parts, words, *refs):
    parts, (gates, gain, wo_hi, wo_lo, rows_in, targets, out_ref) = refs[:n_parts], refs[n_parts:]
    tok, width = rows_in.shape
    attended = jnp.concatenate([p[...] for p in parts], axis=1)
    centered = attended - jnp.mean(attended, axis=1, keepdims=True)
    variance = jnp.mean(centered * centered, axis=1, keepdims=True)
    normed = centered * lax.rsqrt(variance + epsilon) * gain[...]
    gated = split(normed * gates[...])
    out_ref[:tok] = rows_in[...] + dot3(gated, (wo_hi[...], wo_lo[...]), NN)
    out_ref[tok:] = jnp.zeros((EXTRA, width), f32)
    out_ref[tok : tok + 1, :tok] = targets[...].astype(f32)
    for k in range(words.shape[1]):
        out_ref[tok + 1 : tok + 2, k * LANES : (k + 1) * LANES] = jnp.full((1, LANES), words[0, k].astype(f32))


def project(words, parts, gates, gain, wo_hi, wo_lo, rows_in, targets):
    tok, width = rows_in.shape
    return pl.pallas_call(
        lambda words, *refs: project_kernel(len(parts), words, *refs),
        in_specs=[pl.BlockSpec(memory_space=pltpu.SMEM)] + [pl.BlockSpec(memory_space=pltpu.VMEM)] * (len(parts) + 6),
        out_specs=pl.BlockSpec(memory_space=pltpu.VMEM),
        out_shape=jax.ShapeDtypeStruct((tok + EXTRA, width), f32),
        compiler_params=params,
        cost_estimate=pl.CostEstimate(flops=6 * tok * width * width, bytes_accessed=2 * width * width * 4, transcendentals=0),
        name="project",
    )(words, *parts, gates, gain, wo_hi, wo_lo, rows_in, targets)


def loss_kernel(plan, meta, *refs):
    n_seq, n_item, seq_order, item_orders, aligned = plan
    o_refs, refs = refs[:n_seq], refs[n_seq:]
    n_refs, refs = refs[: 4 if aligned else 1], refs[4 if aligned else 1 :]
    n_out = 4 if aligned else 1
    panel_refs, (kept_rows, sent_rows, loss_ref, n_hi, n_lo, o_hi, o_lo, g_hi, g_lo, panel) = refs[:n_out], refs[n_out:]
    me, item = meta[0], meta[1]
    n_neg, width = n_hi.shape
    tok = o_refs[0].shape[0] - EXTRA

    if aligned:
        n_part = n_neg // (2 * n_item)
        for half in range(2):
            for m, r in enumerate(item_orders[half]):
                source = n_refs[2 * half + m // (n_item // 2)]
                rows = source[pl.ds((m % (n_item // 2)) * n_part, n_part)]
                place = pl.ds(pl.multiple_of(half * (n_neg // 2) + (item ^ r) * n_part, n_part), n_part)
                n_hi[place], n_lo[place] = split(rows)
    else:
        n_hi[...], n_lo[...] = split(n_refs[0][...])

    negatives = (n_hi[...], n_lo[...])
    loss = jnp.zeros((1, 2 * tok), f32)
    columns = me * n_neg + lax.broadcasted_iota(i32, (n_neg, 2 * tok), 0)
    for p in range(n_seq // 2):
        both = o_refs[2 * p], o_refs[2 * p + 1]
        span = pl.ds(2 * p * tok, 2 * tok)
        outputs = split(jnp.concatenate([b[:tok] for b in both], axis=0).T)
        o_hi[:, span], o_lo[:, span] = outputs
        target = jnp.concatenate([b[tok : tok + 1, :tok] for b in both], axis=1).astype(i32)
        words = jnp.concatenate([b[tok + 1 : tok + 2, :tok] for b in both], axis=1).astype(i32)
        logits = dot3(negatives, outputs, NN)
        is_target = columns == target
        live = jnp.bitwise_and(jnp.right_shift(jnp.broadcast_to(words, columns.shape), columns // LANES), 1).astype(f32)
        weight = jnp.where(is_target, beta_weight, live)
        signed = jnp.where(is_target, -logits, logits)
        small = jnp.exp(-jnp.abs(logits))
        loss = loss + jnp.sum(weight * (jnp.maximum(signed, 0.0) + jnp.log1p(small)), axis=0, keepdims=True)
        chance = jnp.where(signed >= 0.0, 1.0, small) / (1.0 + small)
        grad = jnp.where(is_target, -weight, weight) * chance
        g_hi[:, span], g_lo[:, span] = split(grad)
        rows = dot3(split(grad.T), negatives, NN)
        for k in range(2):
            n = 2 * p + k
            target_ref = kept_rows if n < n_seq // 2 else sent_rows
            target_ref[n % (n_seq // 2)] = rows[k * tok : (k + 1) * tok]
    loss_ref[...] = jnp.full((8, LANES), jnp.sum(loss))
    whole = dot3((o_hi[...], o_lo[...]), (g_hi[...], g_lo[...]), NT)
    if not aligned:
        panel_refs[0][...] = whole
        return
    panel[...] = whole
    n_dim = width // (n_seq * n_item)
    part = n_dim // 2
    for half in range(2):
        for m, r in enumerate(item_orders[half]):
            out = panel_refs[2 * half + m // (n_item // 2)]
            for n, q in enumerate(seq_order):
                first = (me ^ q) * (n_item * n_dim) + (item ^ r) * n_dim + half * part
                out[m % (n_item // 2), n] = panel[pl.ds(pl.multiple_of(first, part), part)]


def loss_terms(meta, outputs, negatives, plan, n_neg):
    n_seq, n_item, _, _, aligned = plan
    tok, width = outputs[0].shape[0] - EXTRA, outputs[0].shape[1]
    group_len = tok * n_seq
    vmem = pl.BlockSpec(memory_space=pltpu.VMEM)
    if aligned:
        panel = [jax.ShapeDtypeStruct((n_item // 2, n_seq, width // (2 * n_seq * n_item), n_neg), f32)] * 4
    else:
        panel = [jax.ShapeDtypeStruct((width, n_neg), f32)]
    rows = [jax.ShapeDtypeStruct((n_seq // 2, tok, width), f32)] * 2
    out_shape = panel + rows + [jax.ShapeDtypeStruct((8, LANES), f32)]
    return pl.pallas_call(
        functools.partial(loss_kernel, plan),
        in_specs=[pl.BlockSpec(memory_space=pltpu.SMEM)] + [vmem] * (n_seq + len(negatives)),
        out_specs=[vmem] * len(out_shape),
        out_shape=out_shape,
        scratch_shapes=[pltpu.VMEM((n_neg, width), bf16)] * 2
        + [pltpu.VMEM((width, group_len), bf16)] * 2
        + [pltpu.VMEM((n_neg, group_len), bf16)] * 2
        + [pltpu.VMEM((width, n_neg), f32)],
        compiler_params=params,
        cost_estimate=pl.CostEstimate(flops=18 * group_len * width * n_neg, bytes_accessed=16 * n_neg * width, transcendentals=0),
        name="loss_terms",
    )(meta, *outputs, *negatives)


def spread_kernel(owner, moved, ids, out_ref):
    n_src, n_dim, n_neg = moved.shape
    n_item, _, n_rows = out_ref.shape
    row = lax.broadcasted_iota(i32, (n_rows, n_neg), 0)
    spread = []
    for p in range(n_src):
        hot = jnp.where(row == ids[p : p + 1], 1.0, 0.0).astype(bf16)
        both = dot(jnp.concatenate(split(moved[p]), axis=0), hot, NT)
        spread.append(both[:n_dim] + both[n_dim:])
    for j in range(n_item):
        total = jnp.where(owner[0] == j, spread[0], 0.0)
        for p in range(1, n_src):
            total = total + jnp.where(owner[p] == j, spread[p], 0.0)
        out_ref[j] = total


def spread_rows(owner, moved, ids, n_item, n_rows):
    vmem = pl.BlockSpec(memory_space=pltpu.VMEM)
    return pl.pallas_call(
        spread_kernel,
        in_specs=[pl.BlockSpec(memory_space=pltpu.SMEM), vmem, vmem],
        out_specs=vmem,
        out_shape=jax.ShapeDtypeStruct((n_item, moved.shape[1], n_rows), f32),
        compiler_params=params,
        cost_estimate=pl.CostEstimate(flops=4 * moved.size * n_rows, bytes_accessed=2**21, transcendentals=0),
        name="spread_rows",
    )(owner, moved, ids)


def assemble_kernel(order, meta, *refs):
    pieces, out_ref = refs[:-1], refs[-1]
    cols = pieces[0].shape[0]
    for piece, r in zip(pieces, order):
        place = pl.ds(pl.multiple_of((meta[0] ^ r) * cols, cols), cols)
        out_ref[:, place] = piece[...].T


def assemble(meta, pieces, order):
    cols, n_rows = pieces[0].shape
    width = cols * len(pieces)
    step = min(n_rows, 256)
    return pl.pallas_call(
        functools.partial(assemble_kernel, order),
        grid=(n_rows // step,),
        in_specs=[pl.BlockSpec(memory_space=pltpu.SMEM)] + [pl.BlockSpec((cols, step), lambda j: (0, j))] * len(pieces),
        out_specs=pl.BlockSpec((step, width), lambda j: (j, 0)),
        out_shape=jax.ShapeDtypeStruct((n_rows, width), f32),
        compiler_params=params,
        cost_estimate=pl.CostEstimate(flops=0, bytes_accessed=8 * n_rows * width, transcendentals=0),
        name="assemble",
    )(meta, *pieces)


def per_device(
    events,
    w_uvqk,
    out_gain,
    w_out,
    item_table,
    user_lengths,
    neg_ids,
    panel_owner,
    block_mask,
    targets,
):
    rows_in = events[0]
    tok, width = rows_in.shape
    n_rows = item_table.shape[0]
    n_seq, n_item = lax.axis_size("seq"), lax.axis_size("item")
    s, i = lax.axis_index("seq").astype(i32), lax.axis_index("item").astype(i32)
    group_len = tok * n_seq
    seq_bits = bits_of(n_seq)
    seq_order = orders(seq_bits)
    bit_lists = two_orders(n_item)
    item_orders = [orders(bits) for bits in bit_lists]
    flat_ids = neg_ids.reshape(-1)
    n_neg = flat_ids.shape[0] // n_seq
    per_panel = neg_ids.shape[1] // n_neg
    n_part = n_neg // (2 * n_item)
    n_dim = width // (n_seq * n_item)
    aligned = n_part % 16 == 0 and n_dim % 16 == 0 and (n_item * n_dim) % LANES == 0
    plan = (n_seq, n_item, tuple(seq_order), tuple(tuple(o) for o in item_orders), aligned)

    rel = i ^ jnp.array(item_orders, i32)
    spot = s * n_neg + rel[:, :, None] * n_part + jnp.arange(n_part, dtype=i32)
    spot = spot + jnp.array([0, n_neg // 2], i32)[:, None, None]
    own_ids = flat_ids.at[spot.reshape(2, -1)].get(mode="promise_in_bounds")
    root = panel_owner[s // per_panel]
    parts = [
        item_table.at[own_ids[half]].get(mode="promise_in_bounds").reshape(n_item, n_part, width) for half in range(2)
    ]
    for step in range(len(bit_lists[0]) - 1):
        for half, bits in enumerate(bit_lists):
            bit, part = bits[-1 - step], parts[half]
            cut = part.shape[0] // 2
            other = swap(part[cut:], "item", bit)
            parts[half] = jnp.where(((i ^ root) >> bit) & 1 == 0, part[:cut], other)
    for half, bits in enumerate(bit_lists):
        other = swap(parts[half], "item", bits[0])
        same = ((i ^ root) >> bits[0]) & 1 == 0
        parts[half] = jnp.where(same, parts[half], jnp.concatenate([other[1:], other[:1]], axis=0))
    for step in range(1, len(bit_lists[0]) - 1):
        for half, bits in enumerate(bit_lists):
            parts[half] = jnp.concatenate([parts[half], swap(parts[half], "item", bits[step])], axis=0)
    negatives = []
    for half, bits in enumerate(bit_lists):
        negatives += [parts[half], swap(parts[half], "item", bits[-1])]
    if aligned:
        negatives = [n.reshape(-1, width) for n in negatives]
    else:
        negatives = [
            true_order(jnp.concatenate(negatives[2 * half : 2 * half + 2], axis=0), item_orders[half], i)
            for half in range(2)
        ]
        negatives = [jnp.concatenate([n.reshape(-1, width) for n in negatives], axis=0)]

    meta = jnp.concatenate([s[None], user_lengths[0]])
    pieces = gather_pieces(rows_in, "seq", seq_bits)
    gates, queries, vk_hi, vk_lo, wo_hi, wo_lo = prepare(rows_in, w_uvqk, w_out)
    groups = width // LANES
    attended = [attend(meta, pieces, seq_order, queries, vk_hi, vk_lo, 0, groups)]
    own_outputs = project(block_mask, attended, gates, out_gain[None], wo_hi, wo_lo, rows_in, targets)
    outputs = gather_pieces(own_outputs, "seq", seq_bits)

    place = jnp.stack([s, i])
    *panel, kept_rows, sent_rows, loss_total = loss_terms(place, outputs, negatives, plan, n_neg)
    if not aligned:
        blocks = panel[0].reshape(n_seq, n_item, 2, n_dim // 2, n_neg).transpose(2, 1, 0, 3, 4)
        panel = []
        for half in range(2):
            mine = blocks[half][rel[half]][:, s ^ jnp.array(seq_order, i32)]
            panel += [mine[: n_item // 2], mine[n_item // 2 :]]
    event_grad = reduce_steps(kept_rows, sent_rows, "seq", seq_bits[::-1])
    for axis, size in (("seq", n_seq), ("item", n_item)):
        for bit in bits_of(size):
            loss_total = loss_total + swap(loss_total, axis, bit)
    loss_total = loss_total[0, 0]

    sums = [
        reduce_steps(panel[2 * half], panel[2 * half + 1], "item", bits[::-1]) for half, bits in enumerate(bit_lists)
    ]
    moved = jnp.concatenate(sums, axis=1)[:, None]
    for bit in seq_bits[::-1]:
        half = moved.shape[0] // 2
        moved = jnp.concatenate([moved[:half], swap(moved[half:], "seq", bit)], axis=1)
    moved = moved[0]
    source = s ^ jnp.array(orders(seq_bits[::-1]), i32)
    ids = flat_ids.reshape(n_seq, n_neg)[source]
    owner = panel_owner[source // per_panel]
    if aligned:
        sent = spread_rows(owner, moved, ids, n_item, n_rows)
    else:
        hot = (ids[:, :, None] == jnp.arange(n_rows, dtype=i32)).astype(f32)
        spread = jnp.einsum("pdc,pcr->pdr", moved, hot, precision=high)
        mine = (owner[None, :] == jnp.arange(n_item, dtype=i32)[:, None]).astype(f32)
        sent = jnp.sum(mine[:, :, None, None] * spread[None], axis=1)
    taken = lax.all_to_all(sent, "item", split_axis=0, concat_axis=0, tiled=True)
    table = gather_pieces(taken.reshape(n_item * n_dim, n_rows), "seq", seq_bits)
    if aligned:
        table_grad = assemble(place, table, seq_order)
    else:
        table_grad = true_order(jnp.stack(table), seq_order, s).reshape(width, n_rows).T
    return (loss_total / (group_len * n_item), event_grad[None], table_grad)


def solution(mesh):
    placed = (
        P("item", "seq", None),
        P(),
        P(),
        P(),
        P("item", None),
        P("item", None),
        P(),
        P(),
        P("item", "seq"),
        P("item", "seq"),
    )
    return jax.shard_map(
        per_device,
        mesh=mesh,
        in_specs=placed,
        out_specs=(P(), P("item", "seq", None), P("item", None)),
        check_vma=False,
    )
```

```python
import functools

import jax
import jax.numpy as jnp
from jax import lax
from jax.experimental import pallas as pl
from jax.experimental.pallas import tpu as pltpu
from jax.sharding import PartitionSpec as P

H = 16
LANES = 128
EXTRA = 8

beta_weight = 0.75
epsilon = 1e-05

f32, bf16, i32 = jnp.float32, jnp.bfloat16, jnp.int32
high = lax.Precision.HIGH
NN, NT = ((1,), (0,)), ((1,), (1,))
params = pltpu.CompilerParams(vmem_limit_bytes=40 * 2**20)
alone = pltpu.CompilerParams(vmem_limit_bytes=62 * 2**20)


def swap(block, axis, bit):
    size = lax.axis_size(axis)
    return lax.ppermute(block, axis, [(i, i ^ (1 << bit)) for i in range(size)])


def send(block, axis, r):
    size = lax.axis_size(axis)
    return lax.ppermute(block, axis, [(i, i ^ r) for i in range(size)])


def bits_of(size):
    return list(range(size.bit_length() - 1))[::-1]


def two_orders(size):
    up = bits_of(size)
    return [up, up[:-2] + up[:-3:-1]]


def orders(bits):
    order = [0]
    for bit in bits:
        order = order + [r ^ (1 << bit) for r in order]
    return order


def gather_pieces(block, axis, bits):
    pieces = [block]
    for bit in bits:
        pieces = pieces + [swap(piece, axis, bit) for piece in pieces]
    return pieces


def reduce_steps(kept, sent, axis, bits):
    for n, bit in enumerate(bits):
        got = swap(sent, axis, bit)
        if n == len(bits) - 1:
            return (kept + got)[0]
        half = kept.shape[0] // 2
        sent = kept[half:] + got[half:]
        kept = kept[:half] + got[:half]


def true_order(stacked, order, index):
    place = [0] * len(order)
    for k, r in enumerate(order):
        place[r] = k
    return stacked[jnp.array(place, i32)[index ^ jnp.arange(len(order), dtype=i32)]]


def split(x):
    top = x.astype(bf16)
    return top, (x - top.astype(f32)).astype(bf16)


def dot(a, b, dims):
    return lax.dot_general(a, b, (dims, ((), ())), preferred_element_type=f32)


def dot3(a, b, dims):
    return dot(a[0], b[0], dims) + (dot(a[0], b[1], dims) + dot(a[1], b[0], dims))


def silu(x):
    return x / (1.0 + jnp.exp(jnp.minimum(-x, 87.0)))


def pick_kernel(plan, ids_hbm, table_hbm, *refs):
    _, n_item, _, item_orders, _ = plan
    outs, (ids, table, picked, sems) = refs[:4], refs[4:]
    n_neg = ids.shape[1]
    n_step, step = table.shape[:2]
    me, item = lax.axis_index("seq"), lax.axis_index("item")
    copies = [pltpu.make_async_copy(ids_hbm, ids, sems.at[n_step])]
    copies += [
        pltpu.make_async_copy(table_hbm.at[pl.ds(k * step, step)], table.at[k], sems.at[k]) for k in range(n_step)
    ]
    for copy in copies:
        copy.start()
    copies[0].wait()
    row = ids[pl.ds(me, 1), :].astype(f32)
    col = jnp.broadcast_to(row, (LANES, n_neg)).T
    lane = lax.broadcasted_iota(i32, (n_neg, LANES), 1)
    for k in range(n_step):
        hot = [
            jnp.where(col == (lane + (k * step + c)).astype(f32), 1.0, 0.0).astype(bf16) for c in range(0, step, LANES)
        ]
        hot = jnp.concatenate(hot, axis=1)
        copies[1 + k].wait()
        t_hi, t_lo = split(table[k])
        part = dot(hot, t_hi, NN) + dot(hot, t_lo, NN)
        picked[...] = part if k == 0 else picked[...] + part
    n_part = n_neg // (2 * n_item)
    for half in range(2):
        for m, r in enumerate(item_orders[half]):
            first = half * (n_neg // 2) + (item ^ r) * n_part
            out = outs[2 * half + m // (n_item // 2)]
            out[m % (n_item // 2)] = picked[pl.ds(pl.multiple_of(first, n_part), n_part)]


def pick_rows(plan, ids, table):
    n_rows, width = table.shape
    n_item, n_neg = plan[1], ids.shape[1]
    step = 256
    out = (n_item // 2, n_neg // (2 * n_item), width)
    return pl.pallas_call(
        functools.partial(pick_kernel, plan),
        in_specs=[pl.BlockSpec(memory_space=pltpu.HBM)] * 2,
        out_specs=[pl.BlockSpec(memory_space=pltpu.VMEM)] * 4,
        out_shape=[jax.ShapeDtypeStruct(out, f32)] * 4,
        scratch_shapes=[
            pltpu.VMEM(ids.shape, i32),
            pltpu.VMEM((n_rows // step, step, width), f32),
            pltpu.VMEM((n_neg, width), f32),
            pltpu.SemaphoreType.DMA((n_rows // step + 1,)),
        ],
        compiler_params=alone,
        cost_estimate=pl.CostEstimate(flops=4 * n_neg * n_rows * width, bytes_accessed=4 * n_rows * width, transcendentals=0),
        name="pick_rows",
    )(ids, table)


def prepare_kernel(x_ref, w_hbm, wo_hbm, gates_ref, queries_ref, vk_hi, vk_lo, wo_hi, wo_lo, w_buf, wo_buf, w_sems, wo_sem):
    n = w_buf.shape[0]
    copies = [
        [
            pltpu.make_async_copy(
                w_hbm.at[:, pl.ds((part * n + j) * LANES, LANES)], w_buf.at[j, part], w_sems.at[j, part]
            )
            for part in range(4)
        ]
        for j in range(n)
    ]
    last = pltpu.make_async_copy(wo_hbm, wo_buf, wo_sem)
    for copy in sum(copies, []) + [last]:
        copy.start()
    x = split(x_ref[...])
    for j in range(n):
        for copy in copies[j]:
            copy.wait()
        span = pl.ds(j * LANES, LANES)
        uq = split(jnp.concatenate([w_buf[j, 0], w_buf[j, 2]], axis=1))
        both = silu(dot3(x, uq, NN))
        gates_ref[:, span] = both[:, :LANES]
        queries_ref[:, span] = both[:, LANES:]
        vk_hi[j], vk_lo[j] = split(jnp.concatenate([w_buf[j, 1], w_buf[j, 3]], axis=1))
    last.wait()
    wo_hi[...], wo_lo[...] = split(wo_buf[...])


def prepare(rows_in, w_uvqk, w_out):
    tok, width = rows_in.shape
    n = width // LANES
    hbm, vmem = pl.BlockSpec(memory_space=pltpu.HBM), pl.BlockSpec(memory_space=pltpu.VMEM)
    return pl.pallas_call(
        prepare_kernel,
        in_specs=[vmem, hbm, hbm],
        out_specs=[vmem] * 6,
        out_shape=[jax.ShapeDtypeStruct((tok, width), f32)] * 2
        + [jax.ShapeDtypeStruct((n, width, 2 * LANES), bf16)] * 2
        + [jax.ShapeDtypeStruct((width, width), bf16)] * 2,
        scratch_shapes=[
            pltpu.VMEM((n, 4, width, LANES), f32),
            pltpu.VMEM((width, width), f32),
            pltpu.SemaphoreType.DMA((n, 4)),
            pltpu.SemaphoreType.DMA,
        ],
        compiler_params=params,
        cost_estimate=pl.CostEstimate(flops=8 * tok * width * width, bytes_accessed=6 * width * width * 4, transcendentals=0),
        name="prepare",
    )(rows_in, w_uvqk, w_out)


def attend_kernel(order, n_seq, lengths, *refs):
    x_refs, (q_ref, vk_hi, vk_lo, out_ref, x_hi, x_lo, allowed) = refs[:n_seq], refs[n_seq:]
    tok = q_ref.shape[0]
    head = x_hi.shape[1] // H

    @pl.when(pl.program_id(0) == 0)
    def _():
        me = lax.axis_index("seq")
        q_pos = me * tok + lax.broadcasted_iota(i32, (tok, tok), 0)
        col = lax.broadcasted_iota(i32, (tok, tok), 1)

        def user(pos):
            ids, end = jnp.zeros_like(pos), 0
            for k in range(lengths.shape[1]):
                end = end + lengths[0, k]
                ids = ids + (pos >= end).astype(i32)
            return ids

        q_user = user(q_pos)
        for n in range(n_seq):
            span = pl.ds(n * tok, tok)
            x_hi[span], x_lo[span] = split(x_refs[n][...])
            k_pos = (me ^ order[n]) * tok + col
            seen = (q_user == user(k_pos)) & (q_pos >= k_pos)
            allowed[:, span] = seen.astype(f32)

    x = (x_hi[...], x_lo[...])
    vk = silu(dot3(x, (vk_hi[0], vk_lo[0]), NN))
    v_hi, v_lo = split(vk[:, :LANES])
    k_hi, k_lo = split(vk[:, LANES:])
    k_both = jnp.concatenate([k_hi, k_lo], axis=1)
    v_both = jnp.concatenate([v_hi, v_lo], axis=1)
    queries = q_ref[...]
    n_heads = LANES // head
    of_head = lax.broadcasted_iota(i32, (tok, LANES), 1) // head
    stacked = jnp.concatenate([jnp.where(of_head == h, queries, 0.0) for h in range(n_heads)], axis=0)
    q_hi, q_lo = split(stacked)
    scores = dot(jnp.concatenate([q_hi, q_hi], axis=1), k_both, NT) + dot(q_lo, k_hi, NT)
    seen = allowed[...]
    weights = silu(scores) * jnp.concatenate([seen] * n_heads, axis=0)
    w_hi, w_lo = split(weights)
    wide = dot(w_hi, v_both, NN)
    mine = wide[:, :LANES] + wide[:, LANES:] + dot(w_lo, v_hi, NN)
    total = mine[:tok]
    for h in range(1, n_heads):
        total = jnp.where(of_head == h, mine[h * tok : (h + 1) * tok], total)
    out_ref[...] = total


def attend(lengths, pieces, order, queries, vk_hi, vk_lo, first, count):
    tok, width = pieces[0].shape
    n_seq = len(pieces)
    whole = pl.BlockSpec((tok, width), lambda j: (0, 0))
    pair = pl.BlockSpec((1, width, 2 * LANES), lambda j: (first + j, 0, 0))
    return pl.pallas_call(
        functools.partial(attend_kernel, order, n_seq),
        grid=(count,),
        in_specs=[pl.BlockSpec(memory_space=pltpu.SMEM)]
        + [whole] * n_seq
        + [pl.BlockSpec((tok, LANES), lambda j: (0, first + j)), pair, pair],
        out_specs=pl.BlockSpec((tok, LANES), lambda j: (0, j)),
        out_shape=jax.ShapeDtypeStruct((tok, count * LANES), f32),
        scratch_shapes=[
            pltpu.VMEM((n_seq * tok, width), bf16),
            pltpu.VMEM((n_seq * tok, width), bf16),
            pltpu.VMEM((tok, n_seq * tok), f32),
        ],
        compiler_params=params,
        cost_estimate=pl.CostEstimate(flops=count * 2000000000, bytes_accessed=2 * width * width * 4, transcendentals=0),
        name="attend",
    )(lengths, *pieces, queries, vk_hi, vk_lo)


def project_kernel(n_parts, words, *refs):
    parts, (gates, gain, wo_hi, wo_lo, rows_in, targets, out_ref) = refs[:n_parts], refs[n_parts:]
    tok, width = rows_in.shape
    attended = jnp.concatenate([p[...] for p in parts], axis=1)
    centered = attended - jnp.mean(attended, axis=1, keepdims=True)
    variance = jnp.mean(centered * centered, axis=1, keepdims=True)
    normed = centered * lax.rsqrt(variance + epsilon) * gain[...]
    gated = split(normed * gates[...])
    out_ref[:tok] = rows_in[...] + dot3(gated, (wo_hi[...], wo_lo[...]), NN)
    out_ref[tok:] = jnp.zeros((EXTRA, width), f32)
    out_ref[tok : tok + 1, :tok] = targets[...].astype(f32)
    for k in range(words.shape[1]):
        out_ref[tok + 1 : tok + 2, k * LANES : (k + 1) * LANES] = jnp.full((1, LANES), words[0, k].astype(f32))


def project(words, parts, gates, gain, wo_hi, wo_lo, rows_in, targets):
    tok, width = rows_in.shape
    return pl.pallas_call(
        lambda words, *refs: project_kernel(len(parts), words, *refs),
        in_specs=[pl.BlockSpec(memory_space=pltpu.SMEM)] + [pl.BlockSpec(memory_space=pltpu.VMEM)] * (len(parts) + 6),
        out_specs=pl.BlockSpec(memory_space=pltpu.VMEM),
        out_shape=jax.ShapeDtypeStruct((tok + EXTRA, width), f32),
        compiler_params=params,
        cost_estimate=pl.CostEstimate(flops=6 * tok * width * width, bytes_accessed=2 * width * width * 4, transcendentals=0),
        name="project",
    )(words, *parts, gates, gain, wo_hi, wo_lo, rows_in, targets)


def loss_kernel(plan, *refs):
    n_seq, n_item, seq_order, item_orders, aligned = plan
    o_refs, refs = refs[:n_seq], refs[n_seq:]
    n_refs, refs = refs[: 4 if aligned else 1], refs[4 if aligned else 1 :]
    n_out = 4 if aligned else 2
    panel_refs, (kept_rows, sent_rows, n_hi, n_lo, o_hi, o_lo, g_hi, g_lo, panel) = refs[:n_out], refs[n_out:]
    me, item = lax.axis_index("seq"), lax.axis_index("item")
    n_neg, width = n_hi.shape
    tok = o_refs[0].shape[0] - EXTRA

    if aligned:
        n_part = n_neg // (2 * n_item)
        for half in range(2):
            for m, r in enumerate(item_orders[half]):
                source = n_refs[2 * half + m // (n_item // 2)]
                rows = source[pl.ds((m % (n_item // 2)) * n_part, n_part)]
                place = pl.ds(pl.multiple_of(half * (n_neg // 2) + (item ^ r) * n_part, n_part), n_part)
                n_hi[place], n_lo[place] = split(rows)
    else:
        n_hi[...], n_lo[...] = split(n_refs[0][...])

    negatives = (n_hi[...], n_lo[...])
    loss = jnp.zeros((1, 2 * tok), f32)
    columns = me * n_neg + lax.broadcasted_iota(i32, (n_neg, 2 * tok), 0)
    for p in range(n_seq // 2):
        both = o_refs[2 * p], o_refs[2 * p + 1]
        span = pl.ds(2 * p * tok, 2 * tok)
        outputs = split(jnp.concatenate([b[:tok] for b in both], axis=0).T)
        o_hi[:, span], o_lo[:, span] = outputs
        target = jnp.concatenate([b[tok : tok + 1, :tok] for b in both], axis=1).astype(i32)
        words = jnp.concatenate([b[tok + 1 : tok + 2, :tok] for b in both], axis=1).astype(i32)
        logits = dot3(negatives, outputs, NN)
        is_target = columns == target
        live = jnp.bitwise_and(jnp.right_shift(jnp.broadcast_to(words, columns.shape), columns // LANES), 1).astype(f32)
        weight = jnp.where(is_target, beta_weight, live)
        signed = jnp.where(is_target, -logits, logits)
        small = jnp.exp(-jnp.abs(logits))
        loss = loss + jnp.sum(weight * (jnp.maximum(signed, 0.0) + jnp.log1p(small)), axis=0, keepdims=True)
        chance = jnp.where(signed >= 0.0, 1.0, small) / (1.0 + small)
        grad = jnp.where(is_target, -weight, weight) * chance
        g_hi[:, span], g_lo[:, span] = split(grad)
        rows = dot3(split(grad.T), negatives, NN)
        for k in range(2):
            n = 2 * p + k
            target_ref = kept_rows if n < n_seq // 2 else sent_rows
            target_ref[n % (n_seq // 2)] = rows[k * tok : (k + 1) * tok]
    loss = jnp.full((EXTRA, n_neg), jnp.sum(loss))
    whole = dot3((o_hi[...], o_lo[...]), (g_hi[...], g_lo[...]), NT)
    if not aligned:
        panel_refs[0][...] = whole
        panel_refs[1][...] = loss
        return
    panel[...] = whole
    n_dim = width // (n_seq * n_item)
    part = n_dim // 2
    for half in range(2):
        for m, r in enumerate(item_orders[half]):
            out = panel_refs[2 * half + m // (n_item // 2)]
            k = m % (n_item // 2)
            for n, q in enumerate(seq_order):
                first = (me ^ q) * (n_item * n_dim) + (item ^ r) * n_dim + half * part
                out[k, n * part : (n + 1) * part] = panel[pl.ds(pl.multiple_of(first, part), part)]
            if half == 0:
                out[k, n_seq * part :] = loss


def loss_terms(outputs, negatives, plan, n_neg):
    n_seq, n_item, _, _, aligned = plan
    tok, width = outputs[0].shape[0] - EXTRA, outputs[0].shape[1]
    group_len = tok * n_seq
    vmem = pl.BlockSpec(memory_space=pltpu.VMEM)
    if aligned:
        part = width // (2 * n_item)
        panel = [jax.ShapeDtypeStruct((n_item // 2, part + e, n_neg), f32) for e in (EXTRA, EXTRA, 0, 0)]
    else:
        panel = [jax.ShapeDtypeStruct((width, n_neg), f32), jax.ShapeDtypeStruct((EXTRA, n_neg), f32)]
    rows = [jax.ShapeDtypeStruct((n_seq // 2, tok, width), f32)] * 2
    out_shape = panel + rows
    return pl.pallas_call(
        functools.partial(loss_kernel, plan),
        in_specs=[vmem] * (n_seq + len(negatives)),
        out_specs=[vmem] * len(out_shape),
        out_shape=out_shape,
        scratch_shapes=[pltpu.VMEM((n_neg, width), bf16)] * 2
        + [pltpu.VMEM((width, group_len), bf16)] * 2
        + [pltpu.VMEM((n_neg, group_len), bf16)] * 2
        + [pltpu.VMEM((width, n_neg), f32)],
        compiler_params=params,
        cost_estimate=pl.CostEstimate(flops=18 * group_len * width * n_neg, bytes_accessed=16 * n_neg * width, transcendentals=0),
        name="loss_terms",
    )(*outputs, *negatives)


def spread_kernel(order, per_panel, n_item, owner, ids, *refs):
    moved, (*outs, loss_ref) = refs[: len(order)], refs[len(order) :]
    n_dim, n_rows = outs[0].shape
    n_neg = ids.shape[1]
    me, item = lax.axis_index("seq"), lax.axis_index("item")
    row = lax.broadcasted_iota(i32, (n_rows, n_neg), 0)
    spread, owners = [], []
    for p, r in enumerate(order):
        source = me ^ r
        owners.append(owner[source // per_panel])
        hot = jnp.where(row == ids[pl.ds(source, 1), :], 1.0, 0.0).astype(bf16)
        both = dot(jnp.concatenate(split(moved[p][:n_dim]), axis=0), hot, NT)
        spread.append(both[:n_dim] + both[n_dim:])
    for r in range(n_item):
        total = jnp.where(owners[0] == item ^ r, spread[0], 0.0)
        for p in range(1, len(order)):
            total = total + jnp.where(owners[p] == item ^ r, spread[p], 0.0)
        outs[r][...] = total
    loss_ref[...] = sum(m[n_dim:, :LANES] for m in moved)


def spread_rows(order, per_panel, owner, moved, ids, n_item, n_rows):
    vmem = pl.BlockSpec(memory_space=pltpu.VMEM)
    smem = pl.BlockSpec(memory_space=pltpu.SMEM)
    n_dim = moved[0].shape[0] - EXTRA
    return pl.pallas_call(
        functools.partial(spread_kernel, order, per_panel, n_item),
        in_specs=[smem, vmem] + [vmem] * len(moved),
        out_specs=[vmem] * (n_item + 1),
        out_shape=[jax.ShapeDtypeStruct((n_dim, n_rows), f32)] * n_item + [jax.ShapeDtypeStruct((EXTRA, LANES), f32)],
        compiler_params=params,
        cost_estimate=pl.CostEstimate(flops=4 * len(moved) * moved[0].size * n_rows, bytes_accessed=2**21, transcendentals=0),
        name="spread_rows",
    )(owner, ids, *moved)


def assemble_kernel(order, n_item, *refs):
    n_seq = len(order)
    near, far, (out_ref, quarter) = refs[:n_seq], refs[n_seq : 2 * n_seq], refs[2 * n_seq :]
    me, item = lax.axis_index("seq"), lax.axis_index("item")
    cols = quarter.shape[0]
    part = cols // n_item
    for k, q in enumerate(order):
        for r in range(n_item):
            source = near[k] if r < n_item // 2 else far[k]
            rows = source[pl.ds(r % (n_item // 2) * part, part)]
            quarter[pl.ds(pl.multiple_of((item ^ r) * part, part), part)] = rows
        out_ref[:, pl.ds(pl.multiple_of((me ^ q) * cols, cols), cols)] = quarter[...].T


def assemble(table, order, n_item):
    half, n_rows = table[0][0].shape
    cols = 2 * half
    width = cols * len(order)
    step = min(n_rows, 256)
    pieces = table[0] + table[1]
    return pl.pallas_call(
        functools.partial(assemble_kernel, order, n_item),
        grid=(n_rows // step,),
        in_specs=[pl.BlockSpec((half, step), lambda j: (0, j))] * len(pieces),
        out_specs=pl.BlockSpec((step, width), lambda j: (j, 0)),
        out_shape=jax.ShapeDtypeStruct((n_rows, width), f32),
        scratch_shapes=[pltpu.VMEM((cols, step), f32)],
        compiler_params=params,
        cost_estimate=pl.CostEstimate(flops=0, bytes_accessed=8 * n_rows * width, transcendentals=0),
        name="assemble",
    )(*pieces)


def per_device(
    events,
    w_uvqk,
    out_gain,
    w_out,
    item_table,
    user_lengths,
    neg_ids,
    panel_owner,
    block_mask,
    targets,
):
    rows_in = events[0]
    tok, width = rows_in.shape
    n_rows = item_table.shape[0]
    n_seq, n_item = lax.axis_size("seq"), lax.axis_size("item")
    s, i = lax.axis_index("seq").astype(i32), lax.axis_index("item").astype(i32)
    group_len = tok * n_seq
    seq_bits = bits_of(n_seq)
    seq_order = orders(seq_bits)
    bit_lists = two_orders(n_item)
    shared = bit_lists[0][:-2]
    item_orders = [orders(bits) for bits in bit_lists]
    flat_ids = neg_ids.reshape(-1)
    n_neg = flat_ids.shape[0] // n_seq
    per_panel = neg_ids.shape[1] // n_neg
    n_part = n_neg // (2 * n_item)
    n_dim = width // (n_seq * n_item)
    aligned = n_part % 16 == 0 and n_dim % 16 == 0 and (n_item * n_dim) % LANES == 0
    plan = (n_seq, n_item, tuple(seq_order), tuple(tuple(o) for o in item_orders), aligned)

    ids_by_seq = flat_ids.reshape(n_seq, n_neg)
    rel = i ^ jnp.array(item_orders, i32)
    root = panel_owner[s // per_panel]
    if aligned:
        parts = pick_rows(plan, ids_by_seq, item_table)
        parts = [parts[:2], parts[2:]]
    else:
        spot = s * n_neg + rel[:, :, None] * n_part + jnp.arange(n_part, dtype=i32)
        spot = spot + jnp.array([0, n_neg // 2], i32)[:, None, None]
        rows = item_table[flat_ids[spot.reshape(-1)]].reshape(2, n_item, n_part, width)
        parts = [(part[: n_item // 2], part[n_item // 2 :]) for part in rows]
    for step in range(2):
        for half, bits in enumerate(bit_lists):
            bit, (kept, sent) = bits[-1 - step], parts[half]
            other = swap(sent, "item", bit)
            same = ((i ^ root) >> bit) & 1 == 0
            cut = kept.shape[0] if step == 1 else kept.shape[0] // 2
            parts[half] = (jnp.where(same, kept[:cut], other[:cut]), jnp.where(same, kept[cut:], other[cut:]))
    both = jnp.stack([part[0] for part in parts])
    for bit in shared[:0:-1]:
        cut = both.shape[1] // 2
        other = swap(both[:, cut:], "item", bit)
        both = jnp.where(((i ^ root) >> bit) & 1 == 0, both[:, :cut], other)
    other = swap(both, "item", shared[0])
    same = ((i ^ root) >> shared[0]) & 1 == 0
    parts = [
        jnp.where(same, both[half], jnp.concatenate([other[half, 1:], other[half, :1]], axis=0)) for half in range(2)
    ]
    for step in range(1, len(bit_lists[0]) - 1):
        for half, bits in enumerate(bit_lists):
            parts[half] = jnp.concatenate([parts[half], swap(parts[half], "item", bits[step])], axis=0)
    negatives = []
    for half, bits in enumerate(bit_lists):
        negatives += [parts[half], swap(parts[half], "item", bits[-1])]
    if aligned:
        negatives = [n.reshape(-1, width) for n in negatives]
    else:
        negatives = [
            true_order(jnp.concatenate(negatives[2 * half : 2 * half + 2], axis=0), item_orders[half], i)
            for half in range(2)
        ]
        negatives = [jnp.concatenate([n.reshape(-1, width) for n in negatives], axis=0)]

    pieces = gather_pieces(rows_in, "seq", seq_bits)
    gates, queries, vk_hi, vk_lo, wo_hi, wo_lo = prepare(rows_in, w_uvqk, w_out)
    groups = width // LANES
    calls = 2
    attended = [
        attend(user_lengths, pieces, seq_order, queries, vk_hi, vk_lo, c * groups // calls, groups // calls)
        for c in range(calls)
    ]
    own_outputs = project(block_mask, attended, gates, out_gain[None], wo_hi, wo_lo, rows_in, targets)
    outputs = gather_pieces(own_outputs, "seq", seq_bits)

    *panel, kept_rows, sent_rows = loss_terms(outputs, negatives, plan, n_neg)
    if not aligned:
        blocks = panel[0].reshape(n_seq, n_item, 2, n_dim // 2, n_neg).transpose(2, 1, 0, 3, 4)
        loss = jnp.broadcast_to(panel[1], (n_item, EXTRA, n_neg))
        panel = []
        for half in range(2):
            mine = blocks[half][rel[half]][:, s ^ jnp.array(seq_order, i32)].reshape(n_item, -1, n_neg)
            if half == 0:
                mine = jnp.concatenate([mine, loss], axis=1)
            panel += [mine[: n_item // 2], mine[n_item // 2 :]]
    event_grad = reduce_steps(kept_rows, sent_rows, "seq", seq_bits[::-1])

    kept, sent = [], []
    for half, bits in enumerate(bit_lists):
        k, t = panel[2 * half], panel[2 * half + 1]
        for bit in bits[:-3:-1]:
            got = swap(t, "item", bit)
            cut = k.shape[0] // 2
            k, t = k[:cut] + got[:cut], k[cut:] + got[cut:]
        kept.append(k)
        sent.append(t)
    total = reduce_steps(jnp.concatenate(kept, axis=1), jnp.concatenate(sent, axis=1), "item", shared[::-1])
    total, event_grad = lax.optimization_barrier((total, event_grad))
    part = n_dim // 2
    loss = total[n_seq * part : n_seq * part + EXTRA]
    halves = total[: n_seq * part], total[n_seq * part + EXTRA :]
    moved = []
    for k, r in enumerate(seq_order):
        block = jnp.concatenate([half[k * part : (k + 1) * part] for half in halves] + [loss], axis=0)
        moved.append(send(block, "seq", r) if r else block)
    if aligned:
        *sent, loss_total = spread_rows(seq_order, per_panel, panel_owner, moved, ids_by_seq, n_item, n_rows)
    else:
        source = s ^ jnp.array(seq_order, i32)
        ids, owner = ids_by_seq[source], panel_owner[source // per_panel]
        hot = (ids[:, :, None] == jnp.arange(n_rows, dtype=i32)).astype(f32)
        moved = jnp.stack(moved)
        loss_total = jnp.sum(moved[:, n_dim:], axis=0)
        spread = jnp.einsum("pdc,pcr->pdr", moved[:, :n_dim], hot, precision=high)
        mine = (owner[None, :] == (i ^ jnp.arange(n_item, dtype=i32))[:, None]).astype(f32)
        sent = jnp.sum(mine[:, :, None, None] * spread[None], axis=1)
        sent = [sent[r] for r in range(n_item)]

    taken = {r: send(sent[r], "item", r) if r else sent[r] for r in list(range(n_item // 2, n_item)) + list(range(n_item // 2))}
    table = []
    for first in (0, n_item // 2):
        group = jnp.concatenate([taken[r] for r in range(first, first + n_item // 2)], axis=0)
        table.append([group, swap(group, "seq", seq_bits[0])])
    for bit in seq_bits[1:]:
        table = [group + [swap(piece, "seq", bit) for piece in group] for group in table]
    if aligned:
        table_grad = assemble(table, seq_order, n_item)
    else:
        table = jnp.stack([jnp.concatenate([near, far], axis=0) for near, far in zip(*table)])
        table = table.reshape(n_seq, n_item, n_dim, n_rows)[:, i ^ jnp.arange(n_item, dtype=i32)]
        table_grad = true_order(table, seq_order, s).reshape(width, n_rows).T
    return (loss_total[0, 0] / (group_len * n_item), event_grad[None], table_grad)


def solution(mesh):
    placed = (
        P("item", "seq", None),
        P(),
        P(),
        P(),
        P("item", None),
        P("item", None),
        P(),
        P(),
        P("item", "seq"),
        P("item", "seq"),
    )
    return jax.shard_map(
        per_device,
        mesh=mesh,
        in_specs=placed,
        out_specs=(P(), P("item", "seq", None), P("item", None)),
        check_vma=False,
    )
```

```python
import functools

import jax
import jax.numpy as jnp
from jax import lax
from jax.experimental import pallas as pl
from jax.experimental.pallas import tpu as pltpu
from jax.sharding import PartitionSpec as P

H = 16
LANES = 128
EXTRA = 8

beta_weight = 0.75
epsilon = 1e-05

f32, bf16, i32 = jnp.float32, jnp.bfloat16, jnp.int32
high = lax.Precision.HIGH
NN, NT = ((1,), (0,)), ((1,), (1,))
params = pltpu.CompilerParams(vmem_limit_bytes=40 * 2**20)
almost = pltpu.CompilerParams(vmem_limit_bytes=55 * 2**20)
alone = pltpu.CompilerParams(vmem_limit_bytes=62 * 2**20)


def swap(block, axis, bit):
    size = lax.axis_size(axis)
    return lax.ppermute(block, axis, [(i, i ^ (1 << bit)) for i in range(size)])


def send(block, axis, r):
    size = lax.axis_size(axis)
    return lax.ppermute(block, axis, [(i, i ^ r) for i in range(size)])


def bits_of(size):
    return list(range(size.bit_length() - 1))[::-1]


def two_orders(size):
    up = bits_of(size)
    return [up, up[:-2] + up[:-3:-1]]


def orders(bits):
    order = [0]
    for bit in bits:
        order = order + [r ^ (1 << bit) for r in order]
    return order


def gather_pieces(block, axis, bits):
    pieces = [block]
    for bit in bits:
        pieces = pieces + [swap(piece, axis, bit) for piece in pieces]
    return pieces


def reduce_steps(kept, sent, axis, bits):
    for n, bit in enumerate(bits):
        got = swap(sent, axis, bit)
        if n == len(bits) - 1:
            return (kept + got)[0]
        half = kept.shape[0] // 2
        sent = kept[half:] + got[half:]
        kept = kept[:half] + got[:half]


def true_order(stacked, order, index):
    place = [0] * len(order)
    for k, r in enumerate(order):
        place[r] = k
    return stacked[jnp.array(place, i32)[index ^ jnp.arange(len(order), dtype=i32)]]


def split(x):
    top = x.astype(bf16)
    return top, (x - top.astype(f32)).astype(bf16)


def dot(a, b, dims):
    return lax.dot_general(a, b, (dims, ((), ())), preferred_element_type=f32)


def dot3(a, b, dims):
    return dot(a[0], b[0], dims) + (dot(a[0], b[1], dims) + dot(a[1], b[0], dims))


def silu(x):
    return x / (1.0 + jnp.exp(jnp.minimum(-x, 87.0)))


def pick_kernel(plan, ids_hbm, table_hbm, *refs):
    _, n_item, _, item_orders, _ = plan
    outs, (ids, table, picked, sems) = refs[:4], refs[4:]
    n_neg = ids.shape[1]
    n_step, step = table.shape[:2]
    me, item = lax.axis_index("seq"), lax.axis_index("item")
    copies = [pltpu.make_async_copy(ids_hbm, ids, sems.at[n_step])]
    copies += [
        pltpu.make_async_copy(table_hbm.at[pl.ds(k * step, step)], table.at[k], sems.at[k]) for k in range(n_step)
    ]
    for copy in copies:
        copy.start()
    copies[0].wait()
    row = ids[pl.ds(me, 1), :].astype(f32)
    col = jnp.broadcast_to(row, (LANES, n_neg)).T
    lane = lax.broadcasted_iota(i32, (n_neg, LANES), 1)
    for k in range(n_step):
        hot = [
            jnp.where(col == (lane + (k * step + c)).astype(f32), 1.0, 0.0).astype(bf16) for c in range(0, step, LANES)
        ]
        hot = jnp.concatenate(hot, axis=1)
        copies[1 + k].wait()
        t_hi, t_lo = split(table[k])
        part = dot(hot, t_hi, NN) + dot(hot, t_lo, NN)
        picked[...] = part if k == 0 else picked[...] + part
    n_part = n_neg // (2 * n_item)
    for half in range(2):
        for m, r in enumerate(item_orders[half]):
            first = half * (n_neg // 2) + (item ^ r) * n_part
            out = outs[2 * half + m // (n_item // 2)]
            out[m % (n_item // 2)] = picked[pl.ds(pl.multiple_of(first, n_part), n_part)]


def pick_rows(plan, ids, table):
    n_rows, width = table.shape
    n_item, n_neg = plan[1], ids.shape[1]
    step = 256
    out = (n_item // 2, n_neg // (2 * n_item), width)
    return pl.pallas_call(
        functools.partial(pick_kernel, plan),
        in_specs=[pl.BlockSpec(memory_space=pltpu.HBM)] * 2,
        out_specs=[pl.BlockSpec(memory_space=pltpu.VMEM)] * 4,
        out_shape=[jax.ShapeDtypeStruct(out, f32)] * 4,
        scratch_shapes=[
            pltpu.VMEM(ids.shape, i32),
            pltpu.VMEM((n_rows // step, step, width), f32),
            pltpu.VMEM((n_neg, width), f32),
            pltpu.SemaphoreType.DMA((n_rows // step + 1,)),
        ],
        compiler_params=alone,
        cost_estimate=pl.CostEstimate(flops=4 * n_neg * n_rows * width, bytes_accessed=4 * n_rows * width, transcendentals=0),
        name="pick_rows",
    )(ids, table)


def prepare_kernel(x_ref, w_hbm, wo_hbm, gates_ref, queries_ref, vk_hi, vk_lo, wo_hi, wo_lo, w_buf, wo_buf, sems):
    n, depth, _ = w_buf.shape
    width = x_ref.shape[1]
    copies = [pltpu.make_async_copy(w_hbm.at[pl.ds(k * depth, depth)], w_buf.at[k], sems.at[k]) for k in range(n)]
    copies.append(pltpu.make_async_copy(wo_hbm, wo_buf, sems.at[n]))
    for copy in copies:
        copy.start()
    x = split(x_ref[...])
    gates = queries = 0.0
    for k in range(n):
        copies[k].wait()
        span = pl.ds(k * depth, depth)
        mine = x[0][:, k * depth : (k + 1) * depth], x[1][:, k * depth : (k + 1) * depth]
        w = w_buf[k]
        gates = gates + dot3(mine, split(w[:, :width]), NN)
        queries = queries + dot3(mine, split(w[:, 2 * width : 3 * width]), NN)
        for j in range(width // LANES):
            v = w[:, width + j * LANES : width + (j + 1) * LANES]
            key = w[:, 3 * width + j * LANES : 3 * width + (j + 1) * LANES]
            vk_hi[j, span], vk_lo[j, span] = split(jnp.concatenate([v, key], axis=1))
    gates_ref[...] = silu(gates)
    queries_ref[...] = silu(queries)
    copies[n].wait()
    wo_hi[...], wo_lo[...] = split(wo_buf[...])


def prepare(rows_in, w_uvqk, w_out):
    tok, width = rows_in.shape
    n, depth = width // LANES, 256
    hbm, vmem = pl.BlockSpec(memory_space=pltpu.HBM), pl.BlockSpec(memory_space=pltpu.VMEM)
    return pl.pallas_call(
        prepare_kernel,
        in_specs=[vmem, hbm, hbm],
        out_specs=[vmem] * 6,
        out_shape=[jax.ShapeDtypeStruct((tok, width), f32)] * 2
        + [jax.ShapeDtypeStruct((n, width, 2 * LANES), bf16)] * 2
        + [jax.ShapeDtypeStruct((width, width), bf16)] * 2,
        scratch_shapes=[
            pltpu.VMEM((width // depth, depth, w_uvqk.shape[1]), f32),
            pltpu.VMEM((width, width), f32),
            pltpu.SemaphoreType.DMA((width // depth + 1,)),
        ],
        compiler_params=almost,
        cost_estimate=pl.CostEstimate(flops=8 * tok * width * width, bytes_accessed=6 * width * width * 4, transcendentals=0),
        name="prepare",
    )(rows_in, w_uvqk, w_out)


def attend_kernel(order, n_seq, lengths, *refs):
    x_refs, (q_ref, vk_hi, vk_lo, out_ref, x_hi, x_lo, allowed) = refs[:n_seq], refs[n_seq:]
    tok = q_ref.shape[0]
    head = x_hi.shape[1] // H

    @pl.when(pl.program_id(0) == 0)
    def _():
        me = lax.axis_index("seq")
        q_pos = me * tok + lax.broadcasted_iota(i32, (tok, tok), 0)
        col = lax.broadcasted_iota(i32, (tok, tok), 1)

        def user(pos):
            ids, end = jnp.zeros_like(pos), 0
            for k in range(lengths.shape[1]):
                end = end + lengths[0, k]
                ids = ids + (pos >= end).astype(i32)
            return ids

        q_user = user(q_pos)
        for n in range(n_seq):
            span = pl.ds(n * tok, tok)
            x_hi[span], x_lo[span] = split(x_refs[n][...])
            k_pos = (me ^ order[n]) * tok + col
            seen = (q_user == user(k_pos)) & (q_pos >= k_pos)
            allowed[:, span] = seen.astype(f32)

    x = (x_hi[...], x_lo[...])
    vk = silu(dot3(x, (vk_hi[0], vk_lo[0]), NN))
    v_hi, v_lo = split(vk[:, :LANES])
    k_hi, k_lo = split(vk[:, LANES:])
    k_both = jnp.concatenate([k_hi, k_lo], axis=1)
    v_both = jnp.concatenate([v_hi, v_lo], axis=1)
    queries = q_ref[...]
    n_heads = LANES // head
    of_head = lax.broadcasted_iota(i32, (tok, LANES), 1) // head
    stacked = jnp.concatenate([jnp.where(of_head == h, queries, 0.0) for h in range(n_heads)], axis=0)
    q_hi, q_lo = split(stacked)
    scores = dot(jnp.concatenate([q_hi, q_hi], axis=1), k_both, NT) + dot(q_lo, k_hi, NT)
    seen = allowed[...]
    weights = silu(scores) * jnp.concatenate([seen] * n_heads, axis=0)
    w_hi, w_lo = split(weights)
    wide = dot(w_hi, v_both, NN)
    mine = wide[:, :LANES] + wide[:, LANES:] + dot(w_lo, v_hi, NN)
    total = mine[:tok]
    for h in range(1, n_heads):
        total = jnp.where(of_head == h, mine[h * tok : (h + 1) * tok], total)
    out_ref[...] = total


def attend(lengths, pieces, order, queries, vk_hi, vk_lo, first, count):
    tok, width = pieces[0].shape
    n_seq = len(pieces)
    whole = pl.BlockSpec((tok, width), lambda j: (0, 0))
    pair = pl.BlockSpec((1, width, 2 * LANES), lambda j: (first + j, 0, 0))
    return pl.pallas_call(
        functools.partial(attend_kernel, order, n_seq),
        grid=(count,),
        in_specs=[pl.BlockSpec(memory_space=pltpu.SMEM)]
        + [whole] * n_seq
        + [pl.BlockSpec((tok, LANES), lambda j: (0, first + j)), pair, pair],
        out_specs=pl.BlockSpec((tok, LANES), lambda j: (0, j)),
        out_shape=jax.ShapeDtypeStruct((tok, count * LANES), f32),
        scratch_shapes=[
            pltpu.VMEM((n_seq * tok, width), bf16),
            pltpu.VMEM((n_seq * tok, width), bf16),
            pltpu.VMEM((tok, n_seq * tok), f32),
        ],
        compiler_params=params,
        cost_estimate=pl.CostEstimate(flops=count * 2000000000, bytes_accessed=2 * width * width * 4, transcendentals=0),
        name="attend",
    )(lengths, *pieces, queries, vk_hi, vk_lo)


def project_kernel(n_parts, words, *refs):
    parts, (gates, gain, wo_hi, wo_lo, rows_in, targets, out_ref) = refs[:n_parts], refs[n_parts:]
    tok, width = rows_in.shape
    attended = jnp.concatenate([p[...] for p in parts], axis=1)
    centered = attended - jnp.mean(attended, axis=1, keepdims=True)
    variance = jnp.mean(centered * centered, axis=1, keepdims=True)
    normed = centered * lax.rsqrt(variance + epsilon) * gain[...]
    gated = split(normed * gates[...])
    out_ref[:tok] = rows_in[...] + dot3(gated, (wo_hi[...], wo_lo[...]), NN)
    out_ref[tok:] = jnp.zeros((EXTRA, width), f32)
    out_ref[tok : tok + 1, :tok] = targets[...].astype(f32)
    for k in range(words.shape[1]):
        out_ref[tok + 1 : tok + 2, k * LANES : (k + 1) * LANES] = jnp.full((1, LANES), words[0, k].astype(f32))


def project(words, parts, gates, gain, wo_hi, wo_lo, rows_in, targets):
    tok, width = rows_in.shape
    return pl.pallas_call(
        lambda words, *refs: project_kernel(len(parts), words, *refs),
        in_specs=[pl.BlockSpec(memory_space=pltpu.SMEM)] + [pl.BlockSpec(memory_space=pltpu.VMEM)] * (len(parts) + 6),
        out_specs=pl.BlockSpec(memory_space=pltpu.VMEM),
        out_shape=jax.ShapeDtypeStruct((tok + EXTRA, width), f32),
        compiler_params=params,
        cost_estimate=pl.CostEstimate(flops=6 * tok * width * width, bytes_accessed=2 * width * width * 4, transcendentals=0),
        name="project",
    )(words, *parts, gates, gain, wo_hi, wo_lo, rows_in, targets)


def loss_kernel(plan, *refs):
    n_seq, n_item, seq_order, item_orders, aligned = plan
    o_refs, refs = refs[:n_seq], refs[n_seq:]
    n_refs, refs = refs[: 4 if aligned else 1], refs[4 if aligned else 1 :]
    n_out = 4 if aligned else 1
    panel_refs, (kept_rows, sent_rows, loss_ref, n_hi, n_lo, o_hi, o_lo, g_hi, g_lo, panel) = refs[:n_out], refs[n_out:]
    me, item = lax.axis_index("seq"), lax.axis_index("item")
    n_neg, width = n_hi.shape
    tok = o_refs[0].shape[0] - EXTRA

    if aligned:
        n_part = n_neg // (2 * n_item)
        for half in range(2):
            for m, r in enumerate(item_orders[half]):
                source = n_refs[2 * half + m // (n_item // 2)]
                rows = source[pl.ds((m % (n_item // 2)) * n_part, n_part)]
                place = pl.ds(pl.multiple_of(half * (n_neg // 2) + (item ^ r) * n_part, n_part), n_part)
                n_hi[place], n_lo[place] = split(rows)
    else:
        n_hi[...], n_lo[...] = split(n_refs[0][...])

    negatives = (n_hi[...], n_lo[...])
    loss = jnp.zeros((1, 2 * tok), f32)
    columns = me * n_neg + lax.broadcasted_iota(i32, (n_neg, 2 * tok), 0)
    for p in range(n_seq // 2):
        both = o_refs[2 * p], o_refs[2 * p + 1]
        span = pl.ds(2 * p * tok, 2 * tok)
        outputs = split(jnp.concatenate([b[:tok] for b in both], axis=0).T)
        o_hi[:, span], o_lo[:, span] = outputs
        target = jnp.concatenate([b[tok : tok + 1, :tok] for b in both], axis=1).astype(i32)
        words = jnp.concatenate([b[tok + 1 : tok + 2, :tok] for b in both], axis=1).astype(i32)
        logits = dot3(negatives, outputs, NN)
        is_target = columns == target
        live = jnp.bitwise_and(jnp.right_shift(jnp.broadcast_to(words, columns.shape), columns // LANES), 1).astype(f32)
        weight = jnp.where(is_target, beta_weight, live)
        signed = jnp.where(is_target, -logits, logits)
        small = jnp.exp(-jnp.abs(logits))
        loss = loss + jnp.sum(weight * (jnp.maximum(signed, 0.0) + jnp.log1p(small)), axis=0, keepdims=True)
        chance = jnp.where(signed >= 0.0, 1.0, small) / (1.0 + small)
        grad = jnp.where(is_target, -weight, weight) * chance
        g_hi[:, span], g_lo[:, span] = split(grad)
        rows = dot3(split(grad.T), negatives, NN)
        for k in range(2):
            n = 2 * p + k
            target_ref = kept_rows if n < n_seq // 2 else sent_rows
            target_ref[n % (n_seq // 2)] = rows[k * tok : (k + 1) * tok]
    loss_ref[...] = jnp.full((EXTRA, LANES), jnp.sum(loss))
    whole = dot3((o_hi[...], o_lo[...]), (g_hi[...], g_lo[...]), NT)
    if not aligned:
        panel_refs[0][...] = whole
        return
    panel[...] = whole
    n_dim = width // (n_seq * n_item)
    part = n_dim // 2
    for half in range(2):
        for m, r in enumerate(item_orders[half]):
            out = panel_refs[2 * half + m // (n_item // 2)]
            k = m % (n_item // 2)
            for n, q in enumerate(seq_order):
                first = (me ^ q) * (n_item * n_dim) + (item ^ r) * n_dim + half * part
                out[k, n * part : (n + 1) * part] = panel[pl.ds(pl.multiple_of(first, part), part)]


def loss_terms(outputs, negatives, plan, n_neg):
    n_seq, n_item, _, _, aligned = plan
    tok, width = outputs[0].shape[0] - EXTRA, outputs[0].shape[1]
    group_len = tok * n_seq
    vmem = pl.BlockSpec(memory_space=pltpu.VMEM)
    if aligned:
        part = width // (2 * n_item)
        panel = [jax.ShapeDtypeStruct((n_item // 2, part, n_neg), f32)] * 4
    else:
        panel = [jax.ShapeDtypeStruct((width, n_neg), f32)]
    rows = [jax.ShapeDtypeStruct((n_seq // 2, tok, width), f32)] * 2
    out_shape = panel + rows + [jax.ShapeDtypeStruct((EXTRA, LANES), f32)]
    return pl.pallas_call(
        functools.partial(loss_kernel, plan),
        in_specs=[vmem] * (n_seq + len(negatives)),
        out_specs=[vmem] * len(out_shape),
        out_shape=out_shape,
        scratch_shapes=[pltpu.VMEM((n_neg, width), bf16)] * 2
        + [pltpu.VMEM((width, group_len), bf16)] * 2
        + [pltpu.VMEM((n_neg, group_len), bf16)] * 2
        + [pltpu.VMEM((width, n_neg), f32)],
        compiler_params=params,
        cost_estimate=pl.CostEstimate(flops=18 * group_len * width * n_neg, bytes_accessed=16 * n_neg * width, transcendentals=0),
        name="loss_terms",
    )(*outputs, *negatives)


def spread_kernel(order, per_panel, n_item, owner, ids, loss, *refs):
    moved, outs = refs[: len(order)], refs[len(order) :]
    n_dim, n_neg = moved[0].shape
    n_tiles = (outs[0].shape[0] - EXTRA) // n_dim
    me, item = lax.axis_index("seq"), lax.axis_index("item")
    row = lax.broadcasted_iota(i32, (n_tiles * LANES, n_neg), 0)
    spread, owners = [], []
    for p, r in enumerate(order):
        source = me ^ r
        owners.append(owner[source // per_panel])
        hot = jnp.where(row == ids[pl.ds(source, 1), :], 1.0, 0.0).astype(bf16)
        both = dot(jnp.concatenate(split(moved[p][...]), axis=0), hot, NT)
        spread.append(both[:n_dim] + both[n_dim:])
    for r in range(n_item):
        total = jnp.where(owners[0] == item ^ r, spread[0], 0.0)
        for p in range(1, len(order)):
            total = total + jnp.where(owners[p] == item ^ r, spread[p], 0.0)
        for c in range(n_tiles):
            outs[r][c * n_dim : (c + 1) * n_dim] = total[:, c * LANES : (c + 1) * LANES]
        outs[r][n_tiles * n_dim :] = loss[...]


def spread_rows(order, per_panel, owner, moved, ids, loss, n_item, n_rows):
    vmem = pl.BlockSpec(memory_space=pltpu.VMEM)
    smem = pl.BlockSpec(memory_space=pltpu.SMEM)
    n_dim = moved[0].shape[0]
    out = jax.ShapeDtypeStruct((n_rows // LANES * n_dim + EXTRA, LANES), f32)
    return pl.pallas_call(
        functools.partial(spread_kernel, order, per_panel, n_item),
        in_specs=[smem, vmem, vmem] + [vmem] * len(moved),
        out_specs=[vmem] * n_item,
        out_shape=[out] * n_item,
        compiler_params=params,
        cost_estimate=pl.CostEstimate(flops=4 * len(moved) * moved[0].size * n_rows, bytes_accessed=2**21, transcendentals=0),
        name="spread_rows",
    )(owner, ids, loss, *moved)


def assemble_kernel(order, n_item, n_dim, events, *refs):
    groups, (out_ref, loss_ref, quarter) = refs[:-3], refs[-3:]
    n_seq = len(order)
    me, item = lax.axis_index("seq"), lax.axis_index("item")
    cols = n_item * n_dim
    n_tiles = out_ref.shape[0] // LANES
    block = pl.program_id(0)

    def places(k):
        return [(groups[g], m) for g in range(k, len(groups), n_seq) for m in range(groups[g].shape[0])]

    for c in range(n_tiles):
        rows = pl.ds(pl.multiple_of((block * n_tiles + c) * n_dim, n_dim), n_dim)
        for k, q in enumerate(order):
            for r, (group, m) in enumerate(places(k)):
                quarter[pl.ds(pl.multiple_of((item ^ r) * n_dim, n_dim), n_dim)] = group[m, rows]
            place = pl.ds(pl.multiple_of((me ^ q) * cols, cols), cols)
            out_ref[c * LANES : (c + 1) * LANES, place] = quarter[...].T

    @pl.when(block == 0)
    def _():
        total = jnp.zeros((EXTRA, LANES), f32)
        for k in range(n_seq):
            for group, m in places(k):
                total = total + group[m, group.shape[1] - EXTRA :]
        loss_ref[0, 0] = jnp.sum(total) / (EXTRA * LANES * events)


def assemble(table, order, n_item, n_dim, n_rows, events):
    width = n_item * n_dim * len(order)
    step = min(n_rows, 256)
    pieces = sum(table, [])
    return pl.pallas_call(
        functools.partial(assemble_kernel, order, n_item, n_dim, events),
        grid=(n_rows // step,),
        in_specs=[pl.BlockSpec(memory_space=pltpu.VMEM)] * len(pieces),
        out_specs=[pl.BlockSpec((step, width), lambda j: (j, 0)), pl.BlockSpec(memory_space=pltpu.SMEM)],
        out_shape=[jax.ShapeDtypeStruct((n_rows, width), f32), jax.ShapeDtypeStruct((1, 1), f32)],
        scratch_shapes=[pltpu.VMEM((n_item * n_dim, LANES), f32)],
        compiler_params=params,
        cost_estimate=pl.CostEstimate(flops=0, bytes_accessed=8 * n_rows * width, transcendentals=0),
        name="assemble",
    )(*pieces)


def per_device(
    events,
    w_uvqk,
    out_gain,
    w_out,
    item_table,
    user_lengths,
    neg_ids,
    panel_owner,
    block_mask,
    targets,
):
    rows_in = events[0]
    tok, width = rows_in.shape
    n_rows = item_table.shape[0]
    n_seq, n_item = lax.axis_size("seq"), lax.axis_size("item")
    s, i = lax.axis_index("seq").astype(i32), lax.axis_index("item").astype(i32)
    group_len = tok * n_seq
    seq_bits = bits_of(n_seq)
    seq_order = orders(seq_bits)
    bit_lists = two_orders(n_item)
    shared = bit_lists[0][:-2]
    item_orders = [orders(bits) for bits in bit_lists]
    flat_ids = neg_ids.reshape(-1)
    n_neg = flat_ids.shape[0] // n_seq
    per_panel = neg_ids.shape[1] // n_neg
    n_part = n_neg // (2 * n_item)
    n_dim = width // (n_seq * n_item)
    aligned = n_part % 16 == 0 and n_dim % 16 == 0 and (n_item * n_dim) % LANES == 0
    plan = (n_seq, n_item, tuple(seq_order), tuple(tuple(o) for o in item_orders), aligned)

    ids_by_seq = flat_ids.reshape(n_seq, n_neg)
    rel = i ^ jnp.array(item_orders, i32)
    root = panel_owner[s // per_panel]
    if aligned:
        parts = pick_rows(plan, ids_by_seq, item_table)
        parts = [parts[:2], parts[2:]]
    else:
        spot = s * n_neg + rel[:, :, None] * n_part + jnp.arange(n_part, dtype=i32)
        spot = spot + jnp.array([0, n_neg // 2], i32)[:, None, None]
        rows = item_table[flat_ids[spot.reshape(-1)]].reshape(2, n_item, n_part, width)
        parts = [(part[: n_item // 2], part[n_item // 2 :]) for part in rows]
    for step in range(2):
        for half, bits in enumerate(bit_lists):
            bit, (kept, sent) = bits[-1 - step], parts[half]
            other = swap(sent, "item", bit)
            same = ((i ^ root) >> bit) & 1 == 0
            cut = kept.shape[0] if step == 1 else kept.shape[0] // 2
            parts[half] = (jnp.where(same, kept[:cut], other[:cut]), jnp.where(same, kept[cut:], other[cut:]))
    both = jnp.stack([part[0] for part in parts])
    for bit in shared[:0:-1]:
        cut = both.shape[1] // 2
        other = swap(both[:, cut:], "item", bit)
        both = jnp.where(((i ^ root) >> bit) & 1 == 0, both[:, :cut], other)
    other = swap(both, "item", shared[0])
    same = ((i ^ root) >> shared[0]) & 1 == 0
    parts = [
        jnp.where(same, both[half], jnp.concatenate([other[half, 1:], other[half, :1]], axis=0)) for half in range(2)
    ]
    for step in range(1, len(bit_lists[0]) - 1):
        for half, bits in enumerate(bit_lists):
            parts[half] = jnp.concatenate([parts[half], swap(parts[half], "item", bits[step])], axis=0)
    negatives = []
    for half, bits in enumerate(bit_lists):
        negatives += [parts[half], swap(parts[half], "item", bits[-1])]
    if aligned:
        negatives = [n.reshape(-1, width) for n in negatives]
    else:
        negatives = [
            true_order(jnp.concatenate(negatives[2 * half : 2 * half + 2], axis=0), item_orders[half], i)
            for half in range(2)
        ]
        negatives = [jnp.concatenate([n.reshape(-1, width) for n in negatives], axis=0)]

    pieces = gather_pieces(rows_in, "seq", seq_bits)
    gates, queries, vk_hi, vk_lo, wo_hi, wo_lo = prepare(rows_in, w_uvqk, w_out)
    groups = width // LANES
    calls = 2
    attended = [
        attend(user_lengths, pieces, seq_order, queries, vk_hi, vk_lo, c * groups // calls, groups // calls)
        for c in range(calls)
    ]
    own_outputs = project(block_mask, attended, gates, out_gain[None], wo_hi, wo_lo, rows_in, targets)
    outputs = gather_pieces(own_outputs, "seq", seq_bits)

    *panel, kept_rows, sent_rows, loss = loss_terms(outputs, negatives, plan, n_neg)
    if not aligned:
        blocks = panel[0].reshape(n_seq, n_item, 2, n_dim // 2, n_neg).transpose(2, 1, 0, 3, 4)
        panel = []
        for half in range(2):
            mine = blocks[half][rel[half]][:, s ^ jnp.array(seq_order, i32)].reshape(n_item, -1, n_neg)
            panel += [mine[: n_item // 2], mine[n_item // 2 :]]
    event_grad = reduce_steps(kept_rows, sent_rows, "seq", seq_bits[::-1])

    kept, sent = [], []
    for half, bits in enumerate(bit_lists):
        k, t = panel[2 * half], panel[2 * half + 1]
        for bit in bits[:-3:-1]:
            got = swap(t, "item", bit)
            cut = k.shape[0] // 2
            k, t = k[:cut] + got[:cut], k[cut:] + got[cut:]
        kept.append(k)
        sent.append(t)
    total = reduce_steps(jnp.concatenate(kept, axis=1), jnp.concatenate(sent, axis=1), "item", shared[::-1])
    part = n_dim // 2
    halves = total[: n_seq * part], total[n_seq * part :]
    moved = []
    for k, r in enumerate(seq_order):
        block = jnp.concatenate([half[k * part : (k + 1) * part] for half in halves], axis=0)
        moved.append(send(block, "seq", r) if r else block)
    if aligned:
        sent = spread_rows(seq_order, per_panel, panel_owner, moved, ids_by_seq, loss, n_item, n_rows)
    else:
        source = s ^ jnp.array(seq_order, i32)
        ids, owner = ids_by_seq[source], panel_owner[source // per_panel]
        hot = (ids[:, :, None] == jnp.arange(n_rows, dtype=i32)).astype(f32)
        spread = jnp.einsum("pdc,pcr->pdr", jnp.stack(moved), hot, precision=high)
        mine = (owner[None, :] == (i ^ jnp.arange(n_item, dtype=i32))[:, None]).astype(f32)
        sent = jnp.sum(mine[:, :, None, None] * spread[None], axis=1)
        sent = sent.reshape(n_item, n_dim, -1, LANES).transpose(0, 2, 1, 3).reshape(n_item, -1, LANES)
        sent = [jnp.concatenate([sent[r], loss], axis=0) for r in range(n_item)]

    taken = [send(sent[r], "item", r) if r else sent[r] for r in range(n_item)]
    cuts = [0, n_item // 2, 3 * n_item // 4, n_item]
    table = []
    for first, end in zip(cuts, cuts[1:]):
        group = jnp.stack(taken[first:end])
        if first == 0:
            group, event_grad = lax.optimization_barrier((group, event_grad))
        table.append([group, swap(group, "seq", seq_bits[0])])
    for bit in seq_bits[1:]:
        table = [group + [swap(piece, "seq", bit) for piece in group] for group in table]
    if aligned:
        table_grad, mean_loss = assemble(table, seq_order, n_item, n_dim, n_rows, group_len * n_item)
        mean_loss = mean_loss.reshape(())
    else:
        table = jnp.stack([jnp.concatenate(groups, axis=0) for groups in zip(*table)])
        mean_loss = jnp.sum(table[:, :, -1, 0]) / (group_len * n_item)
        table = table[:, :, :-EXTRA].reshape(n_seq, n_item, -1, n_dim, LANES)[:, i ^ jnp.arange(n_item, dtype=i32)]
        table_grad = true_order(table, seq_order, s).transpose(2, 4, 0, 1, 3).reshape(n_rows, width)
    return (mean_loss, event_grad[None], table_grad)


def solution(mesh):
    placed = (
        P("item", "seq", None),
        P(),
        P(),
        P(),
        P("item", None),
        P("item", None),
        P(),
        P(),
        P("item", "seq"),
        P("item", "seq"),
    )
    return jax.shard_map(
        per_device,
        mesh=mesh,
        in_specs=placed,
        out_specs=(P(), P("item", "seq", None), P("item", None)),
        check_vma=False,
    )
```

```python
import functools

import jax
import jax.numpy as jnp
from jax import lax
from jax.experimental import pallas as pl
from jax.experimental.pallas import tpu as pltpu
from jax.sharding import PartitionSpec as P

H = 16
LANES = 128
EXTRA = 8

beta_weight = 0.75
epsilon = 1e-05

f32, bf16, i32 = jnp.float32, jnp.bfloat16, jnp.int32
high = lax.Precision.HIGH
NN, NT = ((1,), (0,)), ((1,), (1,))
params = pltpu.CompilerParams(vmem_limit_bytes=40 * 2**20)
alone = pltpu.CompilerParams(vmem_limit_bytes=62 * 2**20)


def swap(block, axis, bit):
    size = lax.axis_size(axis)
    return lax.ppermute(block, axis, [(i, i ^ (1 << bit)) for i in range(size)])


def send(block, axis, r):
    size = lax.axis_size(axis)
    return lax.ppermute(block, axis, [(i, i ^ r) for i in range(size)])


def bits_of(size):
    return list(range(size.bit_length() - 1))[::-1]


def two_orders(size):
    up = bits_of(size)
    return [up, up[:-2] + up[:-3:-1]]


def orders(bits):
    order = [0]
    for bit in bits:
        order = order + [r ^ (1 << bit) for r in order]
    return order


def gather_pieces(block, axis, bits):
    pieces = [block]
    for bit in bits:
        pieces = pieces + [swap(piece, axis, bit) for piece in pieces]
    return pieces


def reduce_steps(kept, sent, axis, bits):
    for n, bit in enumerate(bits):
        got = swap(sent, axis, bit)
        if n == len(bits) - 1:
            return (kept + got)[0]
        half = kept.shape[0] // 2
        sent = kept[half:] + got[half:]
        kept = kept[:half] + got[:half]


def true_order(stacked, order, index):
    place = [0] * len(order)
    for k, r in enumerate(order):
        place[r] = k
    return stacked[jnp.array(place, i32)[index ^ jnp.arange(len(order), dtype=i32)]]


def split(x):
    top = x.astype(bf16)
    return top, (x - top.astype(f32)).astype(bf16)


def dot(a, b, dims):
    return lax.dot_general(a, b, (dims, ((), ())), preferred_element_type=f32)


def dot3(a, b, dims):
    return dot(a[0], b[0], dims) + (dot(a[0], b[1], dims) + dot(a[1], b[0], dims))


def silu(x):
    return x / (1.0 + jnp.exp(jnp.minimum(-x, 87.0)))


def pick_kernel(plan, ids_hbm, table_hbm, *refs):
    _, n_item, _, item_orders, _ = plan
    outs, (ids, table, picked, sems) = refs[:4], refs[4:]
    n_neg = ids.shape[1]
    n_step, step = table.shape[:2]
    me, item = lax.axis_index("seq"), lax.axis_index("item")
    copies = [pltpu.make_async_copy(ids_hbm, ids, sems.at[n_step])]
    copies += [
        pltpu.make_async_copy(table_hbm.at[pl.ds(k * step, step)], table.at[k], sems.at[k]) for k in range(n_step)
    ]
    for copy in copies:
        copy.start()
    copies[0].wait()
    row = ids[pl.ds(me, 1), :].astype(f32)
    col = jnp.broadcast_to(row, (LANES, n_neg)).T
    lane = lax.broadcasted_iota(i32, (n_neg, LANES), 1)
    for k in range(n_step):
        hot = [
            jnp.where(col == (lane + (k * step + c)).astype(f32), 1.0, 0.0).astype(bf16) for c in range(0, step, LANES)
        ]
        hot = jnp.concatenate(hot, axis=1)
        copies[1 + k].wait()
        t_hi, t_lo = split(table[k])
        part = dot(hot, t_hi, NN) + dot(hot, t_lo, NN)
        picked[...] = part if k == 0 else picked[...] + part
    n_part = n_neg // (2 * n_item)
    for half in range(2):
        for m, r in enumerate(item_orders[half]):
            first = half * (n_neg // 2) + (item ^ r) * n_part
            out = outs[2 * half + m // (n_item // 2)]
            out[m % (n_item // 2)] = picked[pl.ds(pl.multiple_of(first, n_part), n_part)]


def pick_rows(plan, ids, table):
    n_rows, width = table.shape
    n_item, n_neg = plan[1], ids.shape[1]
    step = 256
    out = (n_item // 2, n_neg // (2 * n_item), width)
    return pl.pallas_call(
        functools.partial(pick_kernel, plan),
        in_specs=[pl.BlockSpec(memory_space=pltpu.HBM)] * 2,
        out_specs=[pl.BlockSpec(memory_space=pltpu.VMEM)] * 4,
        out_shape=[jax.ShapeDtypeStruct(out, f32)] * 4,
        scratch_shapes=[
            pltpu.VMEM(ids.shape, i32),
            pltpu.VMEM((n_rows // step, step, width), f32),
            pltpu.VMEM((n_neg, width), f32),
            pltpu.SemaphoreType.DMA((n_rows // step + 1,)),
        ],
        compiler_params=alone,
        cost_estimate=pl.CostEstimate(flops=4 * n_neg * n_rows * width, bytes_accessed=4 * n_rows * width, transcendentals=0),
        name="pick_rows",
    )(ids, table)


def prepare_kernel(x_ref, u_ref, q_ref, gates_ref, queries_ref):
    both = silu(dot3(split(x_ref[...]), split(jnp.concatenate([u_ref[...], q_ref[...]], axis=1)), NN))
    gates_ref[...], queries_ref[...] = both[:, :LANES], both[:, LANES:]


def prepare(rows_in, w_uvqk):
    tok, width = rows_in.shape
    n = width // LANES
    own = pl.BlockSpec((tok, LANES), lambda j: (0, j))
    return pl.pallas_call(
        prepare_kernel,
        grid=(n,),
        in_specs=[
            pl.BlockSpec((tok, width), lambda j: (0, 0)),
            pl.BlockSpec((width, LANES), lambda j: (0, j)),
            pl.BlockSpec((width, LANES), lambda j: (0, 2 * n + j)),
        ],
        out_specs=[own, own],
        out_shape=[jax.ShapeDtypeStruct((tok, width), f32)] * 2,
        compiler_params=params,
        cost_estimate=pl.CostEstimate(flops=12 * tok * width * width, bytes_accessed=2 * width * width * 4, transcendentals=0),
        name="prepare",
    )(rows_in, w_uvqk, w_uvqk)


def attend_kernel(order, n_seq, lengths, *refs):
    x_refs, (q_ref, v_ref, k_ref, out_ref, x_hi, x_lo, allowed) = refs[:n_seq], refs[n_seq:]
    tok = q_ref.shape[0]
    head = x_hi.shape[1] // H

    @pl.when(pl.program_id(0) == 0)
    def _():
        me = lax.axis_index("seq")
        q_pos = me * tok + lax.broadcasted_iota(i32, (tok, tok), 0)
        col = lax.broadcasted_iota(i32, (tok, tok), 1)

        def user(pos):
            ids, end = jnp.zeros_like(pos), 0
            for k in range(lengths.shape[1]):
                end = end + lengths[0, k]
                ids = ids + (pos >= end).astype(i32)
            return ids

        q_user = user(q_pos)
        for n in range(n_seq):
            span = pl.ds(n * tok, tok)
            x_hi[span], x_lo[span] = split(x_refs[n][...])
            k_pos = (me ^ order[n]) * tok + col
            seen = (q_user == user(k_pos)) & (q_pos >= k_pos)
            allowed[:, span] = seen.astype(f32)

    x = (x_hi[...], x_lo[...])
    vk = silu(dot3(x, split(jnp.concatenate([v_ref[...], k_ref[...]], axis=1)), NN))
    v_hi, v_lo = split(vk[:, :LANES])
    k_hi, k_lo = split(vk[:, LANES:])
    k_both = jnp.concatenate([k_hi, k_lo], axis=1)
    v_both = jnp.concatenate([v_hi, v_lo], axis=1)
    queries = q_ref[...]
    n_heads = LANES // head
    of_head = lax.broadcasted_iota(i32, (tok, LANES), 1) // head
    stacked = jnp.concatenate([jnp.where(of_head == h, queries, 0.0) for h in range(n_heads)], axis=0)
    q_hi, q_lo = split(stacked)
    scores = dot(jnp.concatenate([q_hi, q_hi], axis=1), k_both, NT) + dot(q_lo, k_hi, NT)
    seen = allowed[...]
    weights = silu(scores) * jnp.concatenate([seen] * n_heads, axis=0)
    w_hi, w_lo = split(weights)
    wide = dot(w_hi, v_both, NN)
    mine = wide[:, :LANES] + wide[:, LANES:] + dot(w_lo, v_hi, NN)
    total = mine[:tok]
    for h in range(1, n_heads):
        total = jnp.where(of_head == h, mine[h * tok : (h + 1) * tok], total)
    out_ref[...] = total


def attend(lengths, pieces, order, queries, w_uvqk, first, count):
    tok, width = pieces[0].shape
    n_seq = len(pieces)
    whole = pl.BlockSpec((tok, width), lambda j: (0, 0))
    n = width // LANES
    v = pl.BlockSpec((width, LANES), lambda j: (0, n + first + j))
    k = pl.BlockSpec((width, LANES), lambda j: (0, 3 * n + first + j))
    return pl.pallas_call(
        functools.partial(attend_kernel, order, n_seq),
        grid=(count,),
        in_specs=[pl.BlockSpec(memory_space=pltpu.SMEM)]
        + [whole] * n_seq
        + [pl.BlockSpec((tok, LANES), lambda j: (0, first + j)), v, k],
        out_specs=pl.BlockSpec((tok, LANES), lambda j: (0, j)),
        out_shape=jax.ShapeDtypeStruct((tok, count * LANES), f32),
        scratch_shapes=[
            pltpu.VMEM((n_seq * tok, width), bf16),
            pltpu.VMEM((n_seq * tok, width), bf16),
            pltpu.VMEM((tok, n_seq * tok), f32),
        ],
        compiler_params=params,
        cost_estimate=pl.CostEstimate(flops=count * 2000000000, bytes_accessed=2 * width * width * 4, transcendentals=0),
        name="attend",
    )(lengths, *pieces, queries, w_uvqk, w_uvqk)


def project_kernel(n_parts, words, *refs):
    parts, (gates, gain, w_out, rows_in, targets, out_ref) = refs[:n_parts], refs[n_parts:]
    tok, width = rows_in.shape
    attended = jnp.concatenate([p[...] for p in parts], axis=1)
    centered = attended - jnp.mean(attended, axis=1, keepdims=True)
    variance = jnp.mean(centered * centered, axis=1, keepdims=True)
    normed = centered * lax.rsqrt(variance + epsilon) * gain[...]
    gated = split(normed * gates[...])
    out_ref[:tok] = rows_in[...] + dot3(gated, split(w_out[...]), NN)
    out_ref[tok:] = jnp.zeros((EXTRA, width), f32)
    out_ref[tok : tok + 1, :tok] = targets[...].astype(f32)
    for k in range(words.shape[1]):
        out_ref[tok + 1 : tok + 2, k * LANES : (k + 1) * LANES] = jnp.full((1, LANES), words[0, k].astype(f32))


def project(words, parts, gates, gain, w_out, rows_in, targets):
    tok, width = rows_in.shape
    return pl.pallas_call(
        lambda words, *refs: project_kernel(len(parts), words, *refs),
        in_specs=[pl.BlockSpec(memory_space=pltpu.SMEM)] + [pl.BlockSpec(memory_space=pltpu.VMEM)] * (len(parts) + 5),
        out_specs=pl.BlockSpec(memory_space=pltpu.VMEM),
        out_shape=jax.ShapeDtypeStruct((tok + EXTRA, width), f32),
        compiler_params=params,
        cost_estimate=pl.CostEstimate(flops=6 * tok * width * width, bytes_accessed=2 * width * width * 4, transcendentals=0),
        name="project",
    )(words, *parts, gates, gain, w_out, rows_in, targets)


def transpose_kernel(*refs):
    o_refs, (o_hi, o_lo) = refs[:-2], refs[-2:]
    tok = o_refs[0].shape[0] - EXTRA
    for n, o_ref in enumerate(o_refs):
        span = pl.ds(n * tok, tok)
        o_hi[:, span], o_lo[:, span] = split(o_ref[:tok].T)


def transpose_outputs(outputs):
    tok, width = outputs[0].shape[0] - EXTRA, outputs[0].shape[1]
    vmem = pl.BlockSpec(memory_space=pltpu.VMEM)
    return pl.pallas_call(
        transpose_kernel,
        in_specs=[vmem] * len(outputs),
        out_specs=[vmem] * 2,
        out_shape=[jax.ShapeDtypeStruct((width, tok * len(outputs)), bf16)] * 2,
        compiler_params=params,
        cost_estimate=pl.CostEstimate(flops=0, bytes_accessed=2**22, transcendentals=0),
        name="transpose_outputs",
    )(*outputs)


def loss_kernel(plan, o_hi, o_lo, *refs):
    n_seq, n_item, seq_order, item_orders, aligned = plan
    o_refs, refs = refs[:n_seq], refs[n_seq:]
    n_in = 4 if aligned else 1
    n_refs, panel_refs, refs = refs[:n_in], refs[n_in : 2 * n_in], refs[2 * n_in :]
    loss_ref, g_ref, n_hi, n_lo, g_hi, g_lo, panel = refs
    me, item = lax.axis_index("seq"), lax.axis_index("item")
    n_neg, width = n_hi.shape
    tok = o_refs[0].shape[0] - EXTRA

    if aligned:
        n_part = n_neg // (2 * n_item)
        for half in range(2):
            for m, r in enumerate(item_orders[half]):
                source = n_refs[2 * half + m // (n_item // 2)]
                rows = source[pl.ds((m % (n_item // 2)) * n_part, n_part)]
                place = pl.ds(pl.multiple_of(half * (n_neg // 2) + (item ^ r) * n_part, n_part), n_part)
                n_hi[place], n_lo[place] = split(rows)
    else:
        n_hi[...], n_lo[...] = split(n_refs[0][...])

    negatives = (n_hi[...], n_lo[...])
    loss = jnp.zeros((1, 2 * tok), f32)
    columns = me * n_neg + lax.broadcasted_iota(i32, (n_neg, 2 * tok), 0)
    for p in range(n_seq // 2):
        both = o_refs[2 * p], o_refs[2 * p + 1]
        span = pl.ds(2 * p * tok, 2 * tok)
        target = jnp.concatenate([b[tok : tok + 1, :tok] for b in both], axis=1).astype(i32)
        words = jnp.concatenate([b[tok + 1 : tok + 2, :tok] for b in both], axis=1).astype(i32)
        logits = dot3(negatives, (o_hi[:, span], o_lo[:, span]), NN)
        is_target = columns == target
        live = jnp.bitwise_and(jnp.right_shift(jnp.broadcast_to(words, columns.shape), columns // LANES), 1).astype(f32)
        weight = jnp.where(is_target, beta_weight, live)
        signed = jnp.where(is_target, -logits, logits)
        small = jnp.exp(-jnp.abs(logits))
        loss = loss + jnp.sum(weight * (jnp.maximum(signed, 0.0) + jnp.log1p(small)), axis=0, keepdims=True)
        chance = jnp.where(signed >= 0.0, 1.0, small) / (1.0 + small)
        grad = jnp.where(is_target, -weight, weight) * chance
        g_ref[:, span] = grad
        g_hi[:, span], g_lo[:, span] = split(grad)
    loss_ref[...] = jnp.full((EXTRA, LANES), jnp.sum(loss))
    whole = dot3((o_hi[...], o_lo[...]), (g_hi[...], g_lo[...]), NT)
    if not aligned:
        panel_refs[0][...] = whole
        return
    panel[...] = whole
    n_dim = width // (n_seq * n_item)
    part = n_dim // 2
    for half in range(2):
        for m, r in enumerate(item_orders[half]):
            out = panel_refs[2 * half + m // (n_item // 2)]
            k = m % (n_item // 2)
            for n, q in enumerate(seq_order):
                first = (me ^ q) * (n_item * n_dim) + (item ^ r) * n_dim + half * part
                out[k, n * part : (n + 1) * part] = panel[pl.ds(pl.multiple_of(first, part), part)]


def loss_terms(transposed, outputs, negatives, plan, n_neg):
    n_seq, n_item, _, _, aligned = plan
    tok, width = outputs[0].shape[0] - EXTRA, outputs[0].shape[1]
    group_len = tok * n_seq
    vmem = pl.BlockSpec(memory_space=pltpu.VMEM)
    if aligned:
        panel = [jax.ShapeDtypeStruct((n_item // 2, width // (2 * n_item), n_neg), f32)] * 4
    else:
        panel = [jax.ShapeDtypeStruct((width, n_neg), f32)]
    loss = jax.ShapeDtypeStruct((EXTRA, LANES), f32)
    grad = jax.ShapeDtypeStruct((n_neg, group_len), f32)
    parts = [jax.ShapeDtypeStruct((n_neg, width), bf16)] * 2
    out_shape = [*panel, loss, grad, *parts]
    return pl.pallas_call(
        functools.partial(loss_kernel, plan),
        in_specs=[vmem] * (2 + n_seq + len(negatives)),
        out_specs=[vmem] * len(out_shape),
        out_shape=out_shape,
        scratch_shapes=[pltpu.VMEM((n_neg, group_len), bf16)] * 2 + [pltpu.VMEM((width, n_neg), f32)],
        compiler_params=params,
        cost_estimate=pl.CostEstimate(flops=12 * group_len * width * n_neg, bytes_accessed=16 * n_neg * width, transcendentals=0),
        name="loss_terms",
    )(*transposed, *outputs, *negatives)


def rows_kernel(n_seq, grad, n_hi, n_lo, kept_rows, sent_rows):
    tok = grad.shape[1] // n_seq
    negatives = (n_hi[...], n_lo[...])
    for p in range(n_seq // 2):
        rows = dot3(split(grad[:, 2 * p * tok : 2 * (p + 1) * tok].T), negatives, NN)
        for k in range(2):
            n = 2 * p + k
            target_ref = kept_rows if n < n_seq // 2 else sent_rows
            target_ref[n % (n_seq // 2)] = rows[k * tok : (k + 1) * tok]


def event_rows(grad, n_hi, n_lo, n_seq):
    n_neg, group_len = grad.shape
    width = n_hi.shape[1]
    vmem = pl.BlockSpec(memory_space=pltpu.VMEM)
    return pl.pallas_call(
        functools.partial(rows_kernel, n_seq),
        in_specs=[vmem] * 3,
        out_specs=[vmem] * 2,
        out_shape=[jax.ShapeDtypeStruct((n_seq // 2, group_len // n_seq, width), f32)] * 2,
        compiler_params=params,
        cost_estimate=pl.CostEstimate(flops=6 * group_len * width * n_neg, bytes_accessed=8 * n_neg * width, transcendentals=0),
        name="event_rows",
    )(grad, n_hi, n_lo)


def pieces_kernel(spread, owners, which, loss, outs):
    n_dim, n_rows = spread[0].shape
    item = lax.axis_index("item")
    for r, out in zip(which, outs):
        total = jnp.where(owners[0] == item ^ r, spread[0], 0.0)
        for p in range(1, len(owners)):
            total = total + jnp.where(owners[p] == item ^ r, spread[p], 0.0)
        for c in range(n_rows // LANES):
            out[c * n_dim : (c + 1) * n_dim] = total[:, c * LANES : (c + 1) * LANES]
        out[n_rows // LANES * n_dim :] = loss[...]


def owners_of(order, per_panel, owner):
    return [owner[(lax.axis_index("seq") ^ r) // per_panel] for r in order]


def spread_kernel(order, per_panel, which, owner, ids, loss, *refs):
    moved, outs = refs[: len(order)], refs[len(order) :]
    n_dim, n_neg = moved[0].shape
    n_rows = (outs[0].shape[0] - EXTRA) // n_dim * LANES
    row = lax.broadcasted_iota(i32, (n_rows, n_neg), 0)
    spread = []
    for p, r in enumerate(order):
        hot = jnp.where(row == ids[pl.ds(lax.axis_index("seq") ^ r, 1), :], 1.0, 0.0).astype(bf16)
        both = dot(jnp.concatenate(split(moved[p][...]), axis=0), hot, NT)
        spread.append(both[:n_dim] + both[n_dim:])
    pieces_kernel(spread, owners_of(order, per_panel, owner), which, loss, outs)


def spread_rows(order, per_panel, owner, moved, ids, loss, n_item, n_rows):
    vmem = pl.BlockSpec(memory_space=pltpu.VMEM)
    smem = pl.BlockSpec(memory_space=pltpu.SMEM)
    n_dim = moved[0].shape[0]
    out = jax.ShapeDtypeStruct((n_rows // LANES * n_dim + EXTRA, LANES), f32)
    return pl.pallas_call(
        functools.partial(spread_kernel, order, per_panel, tuple(range(n_item))),
        in_specs=[smem, vmem, vmem] + [vmem] * len(moved),
        out_specs=[vmem] * n_item,
        out_shape=[out] * n_item,
        compiler_params=params,
        cost_estimate=pl.CostEstimate(flops=4 * len(moved) * moved[0].size * n_rows, bytes_accessed=2**21, transcendentals=0),
        name="spread_rows",
    )(owner, ids, loss, *moved)


def assemble_kernel(order, members, n_item, n_dim, events, kept, got, *refs):
    groups, (out_ref, loss_ref, event_ref, quarter) = refs[:-4], refs[-4:]
    event_ref[...] = kept[...] + got[...]
    n_seq = len(order)
    me, item = lax.axis_index("seq"), lax.axis_index("item")
    cols = n_item * n_dim
    n_tiles = out_ref.shape[0] // LANES
    block = pl.program_id(0)

    def places(k):
        return [(groups[g], m) for g in range(k, len(groups), n_seq) for m in range(groups[g].shape[0])]

    for c in range(n_tiles):
        rows = pl.ds(pl.multiple_of((block * n_tiles + c) * n_dim, n_dim), n_dim)
        for k, q in enumerate(order):
            for r, (group, m) in zip(members, places(k)):
                quarter[pl.ds(pl.multiple_of((item ^ r) * n_dim, n_dim), n_dim)] = group[m, rows]
            place = pl.ds(pl.multiple_of((me ^ q) * cols, cols), cols)
            out_ref[c * LANES : (c + 1) * LANES, place] = quarter[...].T

    @pl.when(block == 0)
    def _():
        total = jnp.zeros((EXTRA, LANES), f32)
        for k in range(n_seq):
            for group, m in places(k):
                total = total + group[m, group.shape[1] - EXTRA :]
        loss_ref[0, 0] = jnp.sum(total) / (EXTRA * LANES * events)


def assemble(table, kept, got, order, members, n_item, n_dim, n_rows, events):
    width = n_item * n_dim * len(order)
    step = min(n_rows, 256)
    pieces = sum(table, [])
    rows = pl.BlockSpec((1, kept.shape[1] * step // n_rows, width), lambda j: (0, j, 0))
    return pl.pallas_call(
        functools.partial(assemble_kernel, order, members, n_item, n_dim, events),
        grid=(n_rows // step,),
        in_specs=[rows, rows] + [pl.BlockSpec(memory_space=pltpu.VMEM)] * len(pieces),
        out_specs=[pl.BlockSpec((step, width), lambda j: (j, 0)), pl.BlockSpec(memory_space=pltpu.SMEM), rows],
        out_shape=[
            jax.ShapeDtypeStruct((n_rows, width), f32),
            jax.ShapeDtypeStruct((1, 1), f32),
            jax.ShapeDtypeStruct(kept.shape, f32),
        ],
        scratch_shapes=[pltpu.VMEM((n_item * n_dim, LANES), f32)],
        compiler_params=params,
        cost_estimate=pl.CostEstimate(flops=0, bytes_accessed=8 * n_rows * width, transcendentals=0),
        name="assemble",
    )(kept, got, *pieces)


def per_device(
    events,
    w_uvqk,
    out_gain,
    w_out,
    item_table,
    user_lengths,
    neg_ids,
    panel_owner,
    block_mask,
    targets,
):
    rows_in = events[0]
    tok, width = rows_in.shape
    n_rows = item_table.shape[0]
    n_seq, n_item = lax.axis_size("seq"), lax.axis_size("item")
    s, i = lax.axis_index("seq").astype(i32), lax.axis_index("item").astype(i32)
    group_len = tok * n_seq
    seq_bits = bits_of(n_seq)
    seq_order = orders(seq_bits)
    bit_lists = two_orders(n_item)
    shared = bit_lists[0][:-2]
    item_orders = [orders(bits) for bits in bit_lists]
    flat_ids = neg_ids.reshape(-1)
    n_neg = flat_ids.shape[0] // n_seq
    per_panel = neg_ids.shape[1] // n_neg
    n_part = n_neg // (2 * n_item)
    n_dim = width // (n_seq * n_item)
    aligned = n_part % 16 == 0 and n_dim % 16 == 0 and (n_item * n_dim) % LANES == 0
    plan = (n_seq, n_item, tuple(seq_order), tuple(tuple(o) for o in item_orders), aligned)

    ids_by_seq = flat_ids.reshape(n_seq, n_neg)
    rel = i ^ jnp.array(item_orders, i32)
    root = panel_owner[s // per_panel]
    if aligned:
        parts = pick_rows(plan, ids_by_seq, item_table)
        parts = [parts[:2], parts[2:]]
    else:
        spot = s * n_neg + rel[:, :, None] * n_part + jnp.arange(n_part, dtype=i32)
        spot = spot + jnp.array([0, n_neg // 2], i32)[:, None, None]
        rows = item_table[flat_ids[spot.reshape(-1)]].reshape(2, n_item, n_part, width)
        parts = [(part[: n_item // 2], part[n_item // 2 :]) for part in rows]
    pieces = gather_pieces(rows_in, "seq", seq_bits)
    gates, queries = prepare(rows_in, w_uvqk)
    groups = width // LANES
    attended = [
        attend(user_lengths, pieces, seq_order, queries, w_uvqk, first, count)
        for first, count in ((0, groups // 4), (groups // 4, groups - groups // 4))
    ]
    for step in range(2):
        others = [swap(parts[half][1], "item", bits[-1 - step]) for half, bits in enumerate(bit_lists)]
        if step == 1:
            *others, attended[0] = lax.optimization_barrier((*others, attended[0]))
        for half, bits in enumerate(bit_lists):
            kept, other = parts[half][0], others[half]
            same = ((i ^ root) >> bits[-1 - step]) & 1 == 0
            cut = kept.shape[0] if step == 1 else kept.shape[0] // 2
            parts[half] = (jnp.where(same, kept[:cut], other[:cut]), jnp.where(same, kept[cut:], other[cut:]))
    both = jnp.stack([part[0] for part in parts])
    for bit in shared[:0:-1]:
        cut = both.shape[1] // 2
        other = swap(both[:, cut:], "item", bit)
        both = jnp.where(((i ^ root) >> bit) & 1 == 0, both[:, :cut], other)
    other = swap(both, "item", shared[0])
    same = ((i ^ root) >> shared[0]) & 1 == 0
    parts = [
        jnp.where(same, both[half], jnp.concatenate([other[half, 1:], other[half, :1]], axis=0)) for half in range(2)
    ]
    for step in range(1, len(bit_lists[0]) - 1):
        for half, bits in enumerate(bit_lists):
            parts[half] = jnp.concatenate([parts[half], swap(parts[half], "item", bits[step])], axis=0)
    negatives = []
    for half, bits in enumerate(bit_lists):
        negatives += [parts[half], swap(parts[half], "item", bits[-1])]
    if aligned:
        negatives = [n.reshape(-1, width) for n in negatives]
    else:
        negatives = [
            true_order(jnp.concatenate(negatives[2 * half : 2 * half + 2], axis=0), item_orders[half], i)
            for half in range(2)
        ]
        negatives = [jnp.concatenate([n.reshape(-1, width) for n in negatives], axis=0)]

    own_outputs = project(block_mask, attended, gates, out_gain[None], w_out, rows_in, targets)
    outputs = gather_pieces(own_outputs, "seq", seq_bits)

    *panel, loss, grad, n_hi, n_lo = loss_terms(transpose_outputs(outputs), outputs, negatives, plan, n_neg)
    kept_rows, sent_rows = event_rows(grad, n_hi, n_lo, n_seq)
    if not aligned:
        blocks = panel[0].reshape(n_seq, n_item, 2, n_dim // 2, n_neg).transpose(2, 1, 0, 3, 4)
        panel = []
        for half in range(2):
            mine = blocks[half][rel[half]][:, s ^ jnp.array(seq_order, i32)].reshape(n_item, -1, n_neg)
            panel += [mine[: n_item // 2], mine[n_item // 2 :]]

    for step in range(2):
        got = [swap(panel[2 * half + 1], "item", bits[-1 - step]) for half, bits in enumerate(bit_lists)]
        if step == 0:
            *got, kept_rows, sent_rows = lax.optimization_barrier((*got, kept_rows, sent_rows))
        cut = panel[0].shape[0] // 2
        panel = [
            k[:cut] + g[:cut] if part == 0 else k[cut:] + g[cut:]
            for k, g in zip(panel[::2], got)
            for part in range(2)
        ]
    kept, sent = panel[::2], panel[1::2]
    total = reduce_steps(jnp.concatenate(kept, axis=1), jnp.concatenate(sent, axis=1), "item", shared[::-1])
    for n, bit in enumerate(seq_bits[::-1]):
        got_rows = swap(sent_rows, "seq", bit)
        if n < n_seq.bit_length() - 2:
            half = kept_rows.shape[0] // 2
            sent_rows = kept_rows[half:] + got_rows[half:]
            kept_rows = kept_rows[:half] + got_rows[:half]
    part = n_dim // 2
    halves = total[: n_seq * part], total[n_seq * part :]
    moved = []
    for k, r in enumerate(seq_order):
        block = jnp.concatenate([half[k * part : (k + 1) * part] for half in halves], axis=0)
        moved.append(send(block, "seq", r) if r else block)
    if aligned:
        sent = spread_rows(seq_order, per_panel, panel_owner, moved, ids_by_seq, loss, n_item, n_rows)
    else:
        source = s ^ jnp.array(seq_order, i32)
        ids, owner = ids_by_seq[source], panel_owner[source // per_panel]
        hot = (ids[:, :, None] == jnp.arange(n_rows, dtype=i32)).astype(f32)
        spread = jnp.einsum("pdc,pcr->pdr", jnp.stack(moved), hot, precision=high)
        mine = (owner[None, :] == (i ^ jnp.arange(n_item, dtype=i32))[:, None]).astype(f32)
        sent = jnp.sum(mine[:, :, None, None] * spread[None], axis=1)
        sent = sent.reshape(n_item, n_dim, -1, LANES).transpose(0, 2, 1, 3).reshape(n_item, -1, LANES)
        sent = [jnp.concatenate([sent[r], loss], axis=0) for r in range(n_item)]

    taken = [send(sent[r], "item", r) if r else sent[r] for r in range(n_item)]
    near, far = list(range(1, n_item // 2)), list(range(n_item // 2, n_item))
    which = [[0] + far[: len(far) // 2], far[len(far) // 2 :], near]
    table = []
    for members in which:
        group = jnp.stack([taken[r] for r in members])
        if members[0] == 0:
            group, got_rows = lax.optimization_barrier((group, got_rows))
        table.append([group, swap(group, "seq", seq_bits[0])])
    for bit in seq_bits[1:]:
        table = [group + [swap(piece, "seq", bit) for piece in group] for group in table]
    if aligned:
        table_grad, mean_loss, event_grad = assemble(table, kept_rows, got_rows, seq_order, sum(which, []), n_item, n_dim, n_rows, group_len * n_item)
        mean_loss = mean_loss.reshape(())
    else:
        table = jnp.stack([jnp.concatenate(groups, axis=0) for groups in zip(*table)])
        event_grad = kept_rows + got_rows
        mean_loss = jnp.sum(table[:, :, -1, 0]) / (group_len * n_item)
        table = table[:, :, :-EXTRA].reshape(n_seq, n_item, -1, n_dim, LANES)
        table = true_order(table.swapaxes(0, 1), sum(which, []), i).swapaxes(0, 1)
        table_grad = true_order(table, seq_order, s).transpose(2, 4, 0, 1, 3).reshape(n_rows, width)
    return (mean_loss, event_grad, table_grad)


def solution(mesh):
    placed = (
        P("item", "seq", None),
        P(),
        P(),
        P(),
        P("item", None),
        P("item", None),
        P(),
        P(),
        P("item", "seq"),
        P("item", "seq"),
    )
    return jax.shard_map(
        per_device,
        mesh=mesh,
        in_specs=placed,
        out_specs=(P(), P("item", "seq", None), P("item", None)),
        check_vma=False,
    )
```

```python
import functools

import jax
import jax.numpy as jnp
from jax import lax
from jax.experimental import pallas as pl
from jax.experimental.pallas import tpu as pltpu
from jax.sharding import PartitionSpec as P

H = 16
LANES = 128
EXTRA = 8

beta_weight = 0.75
epsilon = 1e-05

f32, bf16, i32 = jnp.float32, jnp.bfloat16, jnp.int32
high = lax.Precision.HIGH
NN, NT = ((1,), (0,)), ((1,), (1,))
params = pltpu.CompilerParams(vmem_limit_bytes=40 * 2**20)
alone = pltpu.CompilerParams(vmem_limit_bytes=62 * 2**20)


def swap(block, axis, bit):
    size = lax.axis_size(axis)
    return lax.ppermute(block, axis, [(i, i ^ (1 << bit)) for i in range(size)])


def send(block, axis, r):
    size = lax.axis_size(axis)
    return lax.ppermute(block, axis, [(i, i ^ r) for i in range(size)])


def bits_of(size):
    return list(range(size.bit_length() - 1))[::-1]


def two_orders(size):
    up = bits_of(size)
    return [up, up[:-2] + up[:-3:-1]]


def orders(bits):
    order = [0]
    for bit in bits:
        order = order + [r ^ (1 << bit) for r in order]
    return order


def gather_pieces(block, axis, bits):
    pieces = [block]
    for bit in bits:
        pieces = pieces + [swap(piece, axis, bit) for piece in pieces]
    return pieces


def reduce_steps(kept, sent, axis, bits):
    for n, bit in enumerate(bits):
        got = swap(sent, axis, bit)
        if n == len(bits) - 1:
            return (kept + got)[0]
        half = kept.shape[0] // 2
        sent = kept[half:] + got[half:]
        kept = kept[:half] + got[:half]


def true_order(stacked, order, index):
    place = [0] * len(order)
    for k, r in enumerate(order):
        place[r] = k
    return stacked[jnp.array(place, i32)[index ^ jnp.arange(len(order), dtype=i32)]]


def split(x):
    top = x.astype(bf16)
    return top, (x - top.astype(f32)).astype(bf16)


def dot(a, b, dims):
    return lax.dot_general(a, b, (dims, ((), ())), preferred_element_type=f32)


def dot3(a, b, dims):
    return dot(a[0], b[0], dims) + (dot(a[0], b[1], dims) + dot(a[1], b[0], dims))


def silu(x):
    return x / (1.0 + jnp.exp(jnp.minimum(-x, 87.0)))


def pick_kernel(plan, ids_hbm, table_hbm, *refs):
    _, n_item, _, item_orders, _ = plan
    outs, (ids, table, picked, sems) = refs[:4], refs[4:]
    n_neg = ids.shape[1]
    n_step, step = table.shape[:2]
    me, item = lax.axis_index("seq"), lax.axis_index("item")
    copies = [pltpu.make_async_copy(ids_hbm, ids, sems.at[n_step])]
    copies += [
        pltpu.make_async_copy(table_hbm.at[pl.ds(k * step, step)], table.at[k], sems.at[k]) for k in range(n_step)
    ]
    for copy in copies:
        copy.start()
    copies[0].wait()
    row = ids[pl.ds(me, 1), :].astype(f32)
    col = jnp.broadcast_to(row, (LANES, n_neg)).T
    lane = lax.broadcasted_iota(i32, (n_neg, LANES), 1)
    for k in range(n_step):
        hot = [
            jnp.where(col == (lane + (k * step + c)).astype(f32), 1.0, 0.0).astype(bf16) for c in range(0, step, LANES)
        ]
        hot = jnp.concatenate(hot, axis=1)
        copies[1 + k].wait()
        t_hi, t_lo = split(table[k])
        part = dot(hot, t_hi, NN) + dot(hot, t_lo, NN)
        picked[...] = part if k == 0 else picked[...] + part
    n_part = n_neg // (2 * n_item)
    for half in range(2):
        for m, r in enumerate(item_orders[half]):
            first = half * (n_neg // 2) + (item ^ r) * n_part
            out = outs[2 * half + m // (n_item // 2)]
            out[m % (n_item // 2)] = picked[pl.ds(pl.multiple_of(first, n_part), n_part)]


def pick_rows(plan, ids, table):
    n_rows, width = table.shape
    n_item, n_neg = plan[1], ids.shape[1]
    step = 256
    out = (n_item // 2, n_neg // (2 * n_item), width)
    return pl.pallas_call(
        functools.partial(pick_kernel, plan),
        in_specs=[pl.BlockSpec(memory_space=pltpu.HBM)] * 2,
        out_specs=[pl.BlockSpec(memory_space=pltpu.VMEM)] * 4,
        out_shape=[jax.ShapeDtypeStruct(out, f32)] * 4,
        scratch_shapes=[
            pltpu.VMEM(ids.shape, i32),
            pltpu.VMEM((n_rows // step, step, width), f32),
            pltpu.VMEM((n_neg, width), f32),
            pltpu.SemaphoreType.DMA((n_rows // step + 1,)),
        ],
        compiler_params=alone,
        cost_estimate=pl.CostEstimate(flops=4 * n_neg * n_rows * width, bytes_accessed=4 * n_rows * width, transcendentals=0),
        name="pick_rows",
    )(ids, table)


def prepare_kernel(x_ref, u_ref, q_ref, gates_ref, queries_ref):
    both = silu(dot3(split(x_ref[...]), split(jnp.concatenate([u_ref[...], q_ref[...]], axis=1)), NN))
    gates_ref[...], queries_ref[...] = both[:, :LANES], both[:, LANES:]


def prepare(rows_in, w_uvqk):
    tok, width = rows_in.shape
    n = width // LANES
    own = pl.BlockSpec((tok, LANES), lambda j: (0, j))
    return pl.pallas_call(
        prepare_kernel,
        grid=(n,),
        in_specs=[
            pl.BlockSpec((tok, width), lambda j: (0, 0)),
            pl.BlockSpec((width, LANES), lambda j: (0, j)),
            pl.BlockSpec((width, LANES), lambda j: (0, 2 * n + j)),
        ],
        out_specs=[own, own],
        out_shape=[jax.ShapeDtypeStruct((tok, width), f32)] * 2,
        compiler_params=params,
        cost_estimate=pl.CostEstimate(flops=12 * tok * width * width, bytes_accessed=2 * width * width * 4, transcendentals=0),
        name="prepare",
    )(rows_in, w_uvqk, w_uvqk)


def attend_kernel(order, n_seq, lengths, *refs):
    x_refs, (q_ref, v_ref, k_ref, out_ref, x_hi, x_lo, allowed) = refs[:n_seq], refs[n_seq:]
    tok = q_ref.shape[0]
    head = x_hi.shape[1] // H

    @pl.when(pl.program_id(0) == 0)
    def _():
        me = lax.axis_index("seq")
        q_pos = me * tok + lax.broadcasted_iota(i32, (tok, tok), 0)
        col = lax.broadcasted_iota(i32, (tok, tok), 1)

        def user(pos):
            ids, end = jnp.zeros_like(pos), 0
            for k in range(lengths.shape[1]):
                end = end + lengths[0, k]
                ids = ids + (pos >= end).astype(i32)
            return ids

        q_user = user(q_pos)
        for n in range(n_seq):
            span = pl.ds(n * tok, tok)
            x_hi[span], x_lo[span] = split(x_refs[n][...])
            k_pos = (me ^ order[n]) * tok + col
            seen = (q_user == user(k_pos)) & (q_pos >= k_pos)
            allowed[:, span] = seen.astype(f32)

    x = (x_hi[...], x_lo[...])
    vk = silu(dot3(x, split(jnp.concatenate([v_ref[...], k_ref[...]], axis=1)), NN))
    v_hi, v_lo = split(vk[:, :LANES])
    k_hi, k_lo = split(vk[:, LANES:])
    k_both = jnp.concatenate([k_hi, k_lo], axis=1)
    v_both = jnp.concatenate([v_hi, v_lo], axis=1)
    queries = q_ref[...]
    n_heads = LANES // head
    of_head = lax.broadcasted_iota(i32, (tok, LANES), 1) // head
    stacked = jnp.concatenate([jnp.where(of_head == h, queries, 0.0) for h in range(n_heads)], axis=0)
    q_hi, q_lo = split(stacked)
    scores = dot(jnp.concatenate([q_hi, q_hi], axis=1), k_both, NT) + dot(q_lo, k_hi, NT)
    seen = allowed[...]
    weights = silu(scores) * jnp.concatenate([seen] * n_heads, axis=0)
    w_hi, w_lo = split(weights)
    wide = dot(w_hi, v_both, NN)
    mine = wide[:, :LANES] + wide[:, LANES:] + dot(w_lo, v_hi, NN)
    total = mine[:tok]
    for h in range(1, n_heads):
        total = jnp.where(of_head == h, mine[h * tok : (h + 1) * tok], total)
    out_ref[...] = total


def attend(lengths, pieces, order, queries, w_uvqk, first, count):
    tok, width = pieces[0].shape
    n_seq = len(pieces)
    whole = pl.BlockSpec((tok, width), lambda j: (0, 0))
    n = width // LANES
    v = pl.BlockSpec((width, LANES), lambda j: (0, n + first + j))
    k = pl.BlockSpec((width, LANES), lambda j: (0, 3 * n + first + j))
    return pl.pallas_call(
        functools.partial(attend_kernel, order, n_seq),
        grid=(count,),
        in_specs=[pl.BlockSpec(memory_space=pltpu.SMEM)]
        + [whole] * n_seq
        + [pl.BlockSpec((tok, LANES), lambda j: (0, first + j)), v, k],
        out_specs=pl.BlockSpec((tok, LANES), lambda j: (0, j)),
        out_shape=jax.ShapeDtypeStruct((tok, count * LANES), f32),
        scratch_shapes=[
            pltpu.VMEM((n_seq * tok, width), bf16),
            pltpu.VMEM((n_seq * tok, width), bf16),
            pltpu.VMEM((tok, n_seq * tok), f32),
        ],
        compiler_params=params,
        cost_estimate=pl.CostEstimate(flops=count * 2000000000, bytes_accessed=2 * width * width * 4, transcendentals=0),
        name="attend",
    )(lengths, *pieces, queries, w_uvqk, w_uvqk)


def project_kernel(n_parts, words, *refs):
    parts, (gates, gain, w_out, rows_in, targets, out_ref) = refs[:n_parts], refs[n_parts:]
    tok, width = rows_in.shape
    attended = jnp.concatenate([p[...] for p in parts], axis=1)
    centered = attended - jnp.mean(attended, axis=1, keepdims=True)
    variance = jnp.mean(centered * centered, axis=1, keepdims=True)
    normed = centered * lax.rsqrt(variance + epsilon) * gain[...]
    gated = split(normed * gates[...])
    out_ref[:tok] = rows_in[...] + dot3(gated, split(w_out[...]), NN)
    out_ref[tok:] = jnp.zeros((EXTRA, width), f32)
    out_ref[tok : tok + 1, :tok] = targets[...].astype(f32)
    for k in range(words.shape[1]):
        out_ref[tok + 1 : tok + 2, k * LANES : (k + 1) * LANES] = jnp.full((1, LANES), words[0, k].astype(f32))


def project(words, parts, gates, gain, w_out, rows_in, targets):
    tok, width = rows_in.shape
    return pl.pallas_call(
        lambda words, *refs: project_kernel(len(parts), words, *refs),
        in_specs=[pl.BlockSpec(memory_space=pltpu.SMEM)] + [pl.BlockSpec(memory_space=pltpu.VMEM)] * (len(parts) + 5),
        out_specs=pl.BlockSpec(memory_space=pltpu.VMEM),
        out_shape=jax.ShapeDtypeStruct((tok + EXTRA, width), f32),
        compiler_params=params,
        cost_estimate=pl.CostEstimate(flops=6 * tok * width * width, bytes_accessed=2 * width * width * 4, transcendentals=0),
        name="project",
    )(words, *parts, gates, gain, w_out, rows_in, targets)


def transpose_kernel(*refs):
    o_refs, (o_hi, o_lo) = refs[:-2], refs[-2:]
    tok = o_refs[0].shape[0] - EXTRA
    for n, o_ref in enumerate(o_refs):
        span = pl.ds(n * tok, tok)
        o_hi[:, span], o_lo[:, span] = split(o_ref[:tok].T)


def transpose_outputs(outputs):
    tok, width = outputs[0].shape[0] - EXTRA, outputs[0].shape[1]
    vmem = pl.BlockSpec(memory_space=pltpu.VMEM)
    return pl.pallas_call(
        transpose_kernel,
        in_specs=[vmem] * len(outputs),
        out_specs=[vmem] * 2,
        out_shape=[jax.ShapeDtypeStruct((width, tok * len(outputs)), bf16)] * 2,
        compiler_params=params,
        cost_estimate=pl.CostEstimate(flops=0, bytes_accessed=2**22, transcendentals=0),
        name="transpose_outputs",
    )(*outputs)


def loss_kernel(plan, o_hi, o_lo, *refs):
    n_seq, n_item, seq_order, item_orders, aligned = plan
    o_refs, refs = refs[:n_seq], refs[n_seq:]
    n_in = 4 if aligned else 1
    n_refs, panel_refs, refs = refs[:n_in], refs[n_in : 2 * n_in], refs[2 * n_in :]
    loss_ref, g_ref, n_hi, n_lo, g_hi, g_lo, panel = refs
    me, item = lax.axis_index("seq"), lax.axis_index("item")
    n_neg, width = n_hi.shape
    tok = o_refs[0].shape[0] - EXTRA

    if aligned:
        n_part = n_neg // (2 * n_item)
        for half in range(2):
            for m, r in enumerate(item_orders[half]):
                source = n_refs[2 * half + m // (n_item // 2)]
                rows = source[pl.ds((m % (n_item // 2)) * n_part, n_part)]
                place = pl.ds(pl.multiple_of(half * (n_neg // 2) + (item ^ r) * n_part, n_part), n_part)
                n_hi[place], n_lo[place] = split(rows)
    else:
        n_hi[...], n_lo[...] = split(n_refs[0][...])

    negatives = (n_hi[...], n_lo[...])
    loss = jnp.zeros((1, 2 * tok), f32)
    columns = me * n_neg + lax.broadcasted_iota(i32, (n_neg, 2 * tok), 0)
    for p in range(n_seq // 2):
        both = o_refs[2 * p], o_refs[2 * p + 1]
        span = pl.ds(2 * p * tok, 2 * tok)
        target = jnp.concatenate([b[tok : tok + 1, :tok] for b in both], axis=1).astype(i32)
        words = jnp.concatenate([b[tok + 1 : tok + 2, :tok] for b in both], axis=1).astype(i32)
        logits = dot3(negatives, (o_hi[:, span], o_lo[:, span]), NN)
        is_target = columns == target
        live = jnp.bitwise_and(jnp.right_shift(jnp.broadcast_to(words, columns.shape), columns // LANES), 1).astype(f32)
        weight = jnp.where(is_target, beta_weight, live)
        signed = jnp.where(is_target, -logits, logits)
        small = jnp.exp(-jnp.abs(logits))
        loss = loss + jnp.sum(weight * (jnp.maximum(signed, 0.0) + jnp.log1p(small)), axis=0, keepdims=True)
        chance = jnp.where(signed >= 0.0, 1.0, small) / (1.0 + small)
        grad = jnp.where(is_target, -weight, weight) * chance
        g_ref[:, span] = grad
        g_hi[:, span], g_lo[:, span] = split(grad)
    loss_ref[...] = jnp.full((EXTRA, LANES), jnp.sum(loss))
    whole = dot3((o_hi[...], o_lo[...]), (g_hi[...], g_lo[...]), NT)
    if not aligned:
        panel_refs[0][...] = whole
        return
    panel[...] = whole
    n_dim = width // (n_seq * n_item)
    part = n_dim // 2
    for half in range(2):
        for m, r in enumerate(item_orders[half]):
            out = panel_refs[2 * half + m // (n_item // 2)]
            k = m % (n_item // 2)
            for n, q in enumerate(seq_order):
                first = (me ^ q) * (n_item * n_dim) + (item ^ r) * n_dim + half * part
                out[k, n * part : (n + 1) * part] = panel[pl.ds(pl.multiple_of(first, part), part)]


def loss_terms(transposed, outputs, negatives, plan, n_neg):
    n_seq, n_item, _, _, aligned = plan
    tok, width = outputs[0].shape[0] - EXTRA, outputs[0].shape[1]
    group_len = tok * n_seq
    vmem = pl.BlockSpec(memory_space=pltpu.VMEM)
    if aligned:
        panel = [jax.ShapeDtypeStruct((n_item // 2, width // (2 * n_item), n_neg), f32)] * 4
    else:
        panel = [jax.ShapeDtypeStruct((width, n_neg), f32)]
    loss = jax.ShapeDtypeStruct((EXTRA, LANES), f32)
    grad = jax.ShapeDtypeStruct((n_neg, group_len), f32)
    parts = [jax.ShapeDtypeStruct((n_neg, width), bf16)] * 2
    out_shape = [*panel, loss, grad, *parts]
    return pl.pallas_call(
        functools.partial(loss_kernel, plan),
        in_specs=[vmem] * (2 + n_seq + len(negatives)),
        out_specs=[vmem] * len(out_shape),
        out_shape=out_shape,
        scratch_shapes=[pltpu.VMEM((n_neg, group_len), bf16)] * 2 + [pltpu.VMEM((width, n_neg), f32)],
        compiler_params=params,
        cost_estimate=pl.CostEstimate(flops=12 * group_len * width * n_neg, bytes_accessed=16 * n_neg * width, transcendentals=0),
        name="loss_terms",
    )(*transposed, *outputs, *negatives)


def rows_kernel(n_seq, grad, n_hi, n_lo, kept_rows, sent_rows):
    tok = grad.shape[1] // n_seq
    negatives = (n_hi[...], n_lo[...])
    for p in range(n_seq // 2):
        rows = dot3(split(grad[:, 2 * p * tok : 2 * (p + 1) * tok].T), negatives, NN)
        for k in range(2):
            n = 2 * p + k
            target_ref = kept_rows if n < n_seq // 2 else sent_rows
            target_ref[n % (n_seq // 2)] = rows[k * tok : (k + 1) * tok]


def event_rows(grad, n_hi, n_lo, n_seq):
    n_neg, group_len = grad.shape
    width = n_hi.shape[1]
    vmem = pl.BlockSpec(memory_space=pltpu.VMEM)
    return pl.pallas_call(
        functools.partial(rows_kernel, n_seq),
        in_specs=[vmem] * 3,
        out_specs=[vmem] * 2,
        out_shape=[jax.ShapeDtypeStruct((n_seq // 2, group_len // n_seq, width), f32)] * 2,
        compiler_params=params,
        cost_estimate=pl.CostEstimate(flops=6 * group_len * width * n_neg, bytes_accessed=8 * n_neg * width, transcendentals=0),
        name="event_rows",
    )(grad, n_hi, n_lo)


def pieces_kernel(spread, owners, which, loss, outs):
    n_dim, n_rows = spread[0].shape
    item = lax.axis_index("item")
    for r, out in zip(which, outs):
        total = jnp.where(owners[0] == item ^ r, spread[0], 0.0)
        for p in range(1, len(owners)):
            total = total + jnp.where(owners[p] == item ^ r, spread[p], 0.0)
        for c in range(n_rows // LANES):
            out[c * n_dim : (c + 1) * n_dim] = total[:, c * LANES : (c + 1) * LANES]
        out[n_rows // LANES * n_dim :] = loss[...]


def owners_of(order, per_panel, owner):
    return [owner[(lax.axis_index("seq") ^ r) // per_panel] for r in order]


def spread_kernel(order, per_panel, which, owner, ids, loss, *refs):
    moved, outs = refs[: len(order)], refs[len(order) :]
    n_dim, n_neg = moved[0].shape
    n_rows = (outs[0].shape[0] - EXTRA) // n_dim * LANES
    row = lax.broadcasted_iota(i32, (n_rows, n_neg), 0)
    spread = []
    for p, r in enumerate(order):
        hot = jnp.where(row == ids[pl.ds(lax.axis_index("seq") ^ r, 1), :], 1.0, 0.0).astype(bf16)
        both = dot(jnp.concatenate(split(moved[p][...]), axis=0), hot, NT)
        spread.append(both[:n_dim] + both[n_dim:])
    pieces_kernel(spread, owners_of(order, per_panel, owner), which, loss, outs)


def spread_rows(order, per_panel, owner, moved, ids, loss, n_item, n_rows):
    vmem = pl.BlockSpec(memory_space=pltpu.VMEM)
    smem = pl.BlockSpec(memory_space=pltpu.SMEM)
    n_dim = moved[0].shape[0]
    out = jax.ShapeDtypeStruct((n_rows // LANES * n_dim + EXTRA, LANES), f32)
    return pl.pallas_call(
        functools.partial(spread_kernel, order, per_panel, tuple(range(n_item))),
        in_specs=[smem, vmem, vmem] + [vmem] * len(moved),
        out_specs=[vmem] * n_item,
        out_shape=[out] * n_item,
        compiler_params=params,
        cost_estimate=pl.CostEstimate(flops=4 * len(moved) * moved[0].size * n_rows, bytes_accessed=2**21, transcendentals=0),
        name="spread_rows",
    )(owner, ids, loss, *moved)


def assemble_kernel(order, members, n_item, n_dim, events, kept, got, *refs):
    groups, (out_ref, loss_ref, event_ref, quarter) = refs[:-4], refs[-4:]
    event_ref[...] = kept[...] + got[...]
    n_seq = len(order)
    me, item = lax.axis_index("seq"), lax.axis_index("item")
    cols = n_item * n_dim
    n_tiles = out_ref.shape[0] // LANES
    block = pl.program_id(0)

    def places(k):
        return [(groups[g], m) for g in range(k, len(groups), n_seq) for m in range(groups[g].shape[0])]

    for c in range(n_tiles):
        first = (block * n_tiles + c) * 2 * n_dim
        for k, q in enumerate(order):
            for r, (group, m) in zip(members, places(k)):
                for chunk in range(2):
                    place = pl.ds(pl.multiple_of((item ^ r ^ (chunk * n_item // 2)) * n_dim, n_dim), n_dim)
                    quarter[place] = group[m, pl.ds(pl.multiple_of(first + chunk * n_dim, n_dim), n_dim)]
            place = pl.ds(pl.multiple_of((me ^ q) * cols, cols), cols)
            out_ref[c * LANES : (c + 1) * LANES, place] = quarter[...].T

    @pl.when(block == 0)
    def _():
        total = jnp.zeros((EXTRA, LANES), f32)
        for k in range(n_seq):
            for group, m in places(k):
                total = total + group[m, group.shape[1] - EXTRA :]
        loss_ref[0, 0] = jnp.sum(total) / (EXTRA * LANES * events)


def assemble(table, kept, got, order, members, n_item, n_dim, n_rows, events):
    width = n_item * n_dim * len(order)
    step = min(n_rows, 256)
    pieces = sum(table, [])
    rows = pl.BlockSpec((1, kept.shape[1] * step // n_rows, width), lambda j: (0, j, 0))
    return pl.pallas_call(
        functools.partial(assemble_kernel, order, members, n_item, n_dim, events),
        grid=(n_rows // step,),
        in_specs=[rows, rows] + [pl.BlockSpec(memory_space=pltpu.VMEM)] * len(pieces),
        out_specs=[pl.BlockSpec((step, width), lambda j: (j, 0)), pl.BlockSpec(memory_space=pltpu.SMEM), rows],
        out_shape=[
            jax.ShapeDtypeStruct((n_rows, width), f32),
            jax.ShapeDtypeStruct((1, 1), f32),
            jax.ShapeDtypeStruct(kept.shape, f32),
        ],
        scratch_shapes=[pltpu.VMEM((n_item * n_dim, LANES), f32)],
        compiler_params=params,
        cost_estimate=pl.CostEstimate(flops=0, bytes_accessed=8 * n_rows * width, transcendentals=0),
        name="assemble",
    )(kept, got, *pieces)


def per_device(
    events,
    w_uvqk,
    out_gain,
    w_out,
    item_table,
    user_lengths,
    neg_ids,
    panel_owner,
    block_mask,
    targets,
):
    rows_in = events[0]
    tok, width = rows_in.shape
    n_rows = item_table.shape[0]
    n_seq, n_item = lax.axis_size("seq"), lax.axis_size("item")
    s, i = lax.axis_index("seq").astype(i32), lax.axis_index("item").astype(i32)
    group_len = tok * n_seq
    seq_bits = bits_of(n_seq)
    seq_order = orders(seq_bits)
    bit_lists = two_orders(n_item)
    shared = bit_lists[0][:-2]
    item_orders = [orders(bits) for bits in bit_lists]
    flat_ids = neg_ids.reshape(-1)
    n_neg = flat_ids.shape[0] // n_seq
    per_panel = neg_ids.shape[1] // n_neg
    n_part = n_neg // (2 * n_item)
    n_dim = width // (n_seq * n_item)
    aligned = n_part % 16 == 0 and n_dim % 16 == 0 and (n_item * n_dim) % LANES == 0
    plan = (n_seq, n_item, tuple(seq_order), tuple(tuple(o) for o in item_orders), aligned)

    ids_by_seq = flat_ids.reshape(n_seq, n_neg)
    rel = i ^ jnp.array(item_orders, i32)
    root = panel_owner[s // per_panel]
    if aligned:
        parts = pick_rows(plan, ids_by_seq, item_table)
        parts = [parts[:2], parts[2:]]
    else:
        spot = s * n_neg + rel[:, :, None] * n_part + jnp.arange(n_part, dtype=i32)
        spot = spot + jnp.array([0, n_neg // 2], i32)[:, None, None]
        rows = item_table[flat_ids[spot.reshape(-1)]].reshape(2, n_item, n_part, width)
        parts = [(part[: n_item // 2], part[n_item // 2 :]) for part in rows]
    pieces = gather_pieces(rows_in, "seq", seq_bits)
    gates, queries = prepare(rows_in, w_uvqk)
    groups = width // LANES
    attended = [
        attend(user_lengths, pieces, seq_order, queries, w_uvqk, first, count)
        for first, count in ((0, groups // 4), (groups // 4, groups - groups // 4))
    ]
    for step in range(2):
        others = [swap(parts[half][1], "item", bits[-1 - step]) for half, bits in enumerate(bit_lists)]
        if step == 1:
            *others, attended[0] = lax.optimization_barrier((*others, attended[0]))
        for half, bits in enumerate(bit_lists):
            kept, other = parts[half][0], others[half]
            same = ((i ^ root) >> bits[-1 - step]) & 1 == 0
            cut = kept.shape[0] if step == 1 else kept.shape[0] // 2
            parts[half] = (jnp.where(same, kept[:cut], other[:cut]), jnp.where(same, kept[cut:], other[cut:]))
    both = jnp.stack([part[0] for part in parts])
    for bit in shared[:0:-1]:
        cut = both.shape[1] // 2
        other = swap(both[:, cut:], "item", bit)
        both = jnp.where(((i ^ root) >> bit) & 1 == 0, both[:, :cut], other)
    other = swap(both, "item", shared[0])
    same = ((i ^ root) >> shared[0]) & 1 == 0
    parts = [
        jnp.where(same, both[half], jnp.concatenate([other[half, 1:], other[half, :1]], axis=0)) for half in range(2)
    ]
    for step in range(1, len(bit_lists[0]) - 1):
        for half, bits in enumerate(bit_lists):
            parts[half] = jnp.concatenate([parts[half], swap(parts[half], "item", bits[step])], axis=0)
    negatives = []
    for half, bits in enumerate(bit_lists):
        negatives += [parts[half], swap(parts[half], "item", bits[-1])]
    if aligned:
        negatives = [n.reshape(-1, width) for n in negatives]
    else:
        negatives = [
            true_order(jnp.concatenate(negatives[2 * half : 2 * half + 2], axis=0), item_orders[half], i)
            for half in range(2)
        ]
        negatives = [jnp.concatenate([n.reshape(-1, width) for n in negatives], axis=0)]

    own_outputs = project(block_mask, attended, gates, out_gain[None], w_out, rows_in, targets)
    outputs = gather_pieces(own_outputs, "seq", seq_bits)

    *panel, loss, grad, n_hi, n_lo = loss_terms(transpose_outputs(outputs), outputs, negatives, plan, n_neg)
    kept_rows, sent_rows = event_rows(grad, n_hi, n_lo, n_seq)
    if not aligned:
        blocks = panel[0].reshape(n_seq, n_item, 2, n_dim // 2, n_neg).transpose(2, 1, 0, 3, 4)
        panel = []
        for half in range(2):
            mine = blocks[half][rel[half]][:, s ^ jnp.array(seq_order, i32)].reshape(n_item, -1, n_neg)
            panel += [mine[: n_item // 2], mine[n_item // 2 :]]

    for step in range(2):
        got = [swap(panel[2 * half + 1], "item", bits[-1 - step]) for half, bits in enumerate(bit_lists)]
        if step == 0:
            *got, kept_rows, sent_rows = lax.optimization_barrier((*got, kept_rows, sent_rows))
        cut = panel[0].shape[0] // 2
        panel = [
            k[:cut] + g[:cut] if part == 0 else k[cut:] + g[cut:]
            for k, g in zip(panel[::2], got)
            for part in range(2)
        ]
    kept, sent = panel[::2], panel[1::2]
    kept, sent = jnp.concatenate(kept, axis=1), jnp.concatenate(sent, axis=1)
    for bit in shared[:0:-1]:
        got = swap(sent, "item", bit)
        cut = kept.shape[0] // 2
        kept, sent = kept[:cut] + got[:cut], kept[cut:] + got[cut:]
    tail = jnp.concatenate([loss] * (n_neg // LANES), axis=1)
    mine = jnp.concatenate([kept[0], sent[0], tail], axis=0)
    other = swap(mine, "item", shared[0])
    for n, bit in enumerate(seq_bits[::-1]):
        got_rows = swap(sent_rows, "seq", bit)
        if n < n_seq.bit_length() - 2:
            half = kept_rows.shape[0] // 2
            sent_rows = kept_rows[half:] + got_rows[half:]
            kept_rows = kept_rows[:half] + got_rows[:half]
    other, got_rows = lax.optimization_barrier((other, got_rows))
    rows = kept.shape[1]
    total = [kept[0] + other[rows : 2 * rows], sent[0] + other[:rows]]
    loss = loss + other[2 * rows :, :LANES]
    part = n_dim // 2
    moved = []
    for k, r in enumerate(seq_order):
        spans = [slice(h * n_seq * part + k * part, h * n_seq * part + (k + 1) * part) for h in range(2)]
        block = jnp.concatenate([chunk[span] for chunk in total for span in spans], axis=0)
        moved.append(send(block, "seq", r) if r else block)
    n_near, top = n_item // 2, 1 << shared[0]
    if aligned:
        sent = spread_rows(seq_order, per_panel, panel_owner, moved, ids_by_seq, loss, n_near, n_rows)
    else:
        source = s ^ jnp.array(seq_order, i32)
        ids, owner = ids_by_seq[source], panel_owner[source // per_panel]
        hot = (ids[:, :, None] == jnp.arange(n_rows, dtype=i32)).astype(f32)
        spread = jnp.einsum("pdc,pcr->pdr", jnp.stack(moved), hot, precision=high)
        mine = (owner[None, :] == (i ^ jnp.arange(n_near, dtype=i32))[:, None]).astype(f32)
        sent = jnp.sum(mine[:, :, None, None] * spread[None], axis=1)
        sent = sent.reshape(n_near, 2 * n_dim, -1, LANES).transpose(0, 2, 1, 3).reshape(n_near, -1, LANES)
        sent = [jnp.concatenate([sent[r], loss], axis=0) for r in range(n_near)]

    sent = list(sent)
    own = sent[0][None]
    own = [own, swap(own, "seq", seq_bits[0])]
    sent[3], own[1] = lax.optimization_barrier((sent[3], own[1]))
    taken = [send(sent[r], "item", r) if r else sent[r] for r in range(n_near)]
    which = [[0], [1, 2], list(range(3, n_near))]
    table = [own]
    for members in which[1:]:
        group = jnp.stack([taken[r] for r in members])
        table.append([group, swap(group, "seq", seq_bits[0])])
    members = sum(which, [])
    for bit in seq_bits[1:]:
        table = [group + [swap(piece, "seq", bit) for piece in group] for group in table]
    if aligned:
        table_grad, mean_loss, event_grad = assemble(table, kept_rows, got_rows, seq_order, members, n_item, n_dim, n_rows, group_len * n_item)
        mean_loss = mean_loss.reshape(())
    else:
        table = jnp.stack([jnp.concatenate(groups, axis=0) for groups in zip(*table)])
        event_grad = kept_rows + got_rows
        mean_loss = jnp.sum(table[:, :, -1, 0]) / (group_len * n_item)
        table = table[:, :, :-EXTRA].reshape(n_seq, n_near, -1, 2, n_dim, LANES).transpose(1, 3, 0, 2, 4, 5)
        table = table.reshape(n_item, n_seq, -1, n_dim, LANES)
        table = true_order(table, [r ^ chunk for r in members for chunk in (0, top)], i).swapaxes(0, 1)
        table_grad = true_order(table, seq_order, s).transpose(2, 4, 0, 1, 3).reshape(n_rows, width)
    return (mean_loss, event_grad, table_grad)


def solution(mesh):
    placed = (
        P("item", "seq", None),
        P(),
        P(),
        P(),
        P("item", None),
        P("item", None),
        P(),
        P(),
        P("item", "seq"),
        P("item", "seq"),
    )
    return jax.shard_map(
        per_device,
        mesh=mesh,
        in_specs=placed,
        out_specs=(P(), P("item", "seq", None), P("item", None)),
        check_vma=False,
    )
```

```python
import functools

import jax
import jax.numpy as jnp
from jax import lax
from jax.experimental import pallas as pl
from jax.experimental.pallas import tpu as pltpu
from jax.sharding import PartitionSpec as P

H = 16
LANES = 128
EXTRA = 8

beta_weight = 0.75
epsilon = 1e-05

f32, bf16, i32 = jnp.float32, jnp.bfloat16, jnp.int32
high = lax.Precision.HIGH
NN, NT = ((1,), (0,)), ((1,), (1,))
params = pltpu.CompilerParams(vmem_limit_bytes=40 * 2**20)
alone = pltpu.CompilerParams(vmem_limit_bytes=62 * 2**20)


def swap(block, axis, bit):
    size = lax.axis_size(axis)
    return lax.ppermute(block, axis, [(i, i ^ (1 << bit)) for i in range(size)])


def send(block, axis, r):
    size = lax.axis_size(axis)
    return lax.ppermute(block, axis, [(i, i ^ r) for i in range(size)])


def bits_of(size):
    return list(range(size.bit_length() - 1))[::-1]


def two_orders(size):
    up = bits_of(size)
    return [up, up[:-2] + up[:-3:-1]]


def orders(bits):
    order = [0]
    for bit in bits:
        order = order + [r ^ (1 << bit) for r in order]
    return order


def gather_pieces(block, axis, bits):
    pieces = [block]
    for bit in bits:
        pieces = pieces + [swap(piece, axis, bit) for piece in pieces]
    return pieces


def reduce_steps(kept, sent, axis, bits):
    for n, bit in enumerate(bits):
        got = swap(sent, axis, bit)
        if n == len(bits) - 1:
            return (kept + got)[0]
        half = kept.shape[0] // 2
        sent = kept[half:] + got[half:]
        kept = kept[:half] + got[:half]


def true_order(stacked, order, index):
    place = [0] * len(order)
    for k, r in enumerate(order):
        place[r] = k
    return stacked[jnp.array(place, i32)[index ^ jnp.arange(len(order), dtype=i32)]]


def split(x):
    top = x.astype(bf16)
    return top, (x - top.astype(f32)).astype(bf16)


def dot(a, b, dims):
    return lax.dot_general(a, b, (dims, ((), ())), preferred_element_type=f32)


def dot3(a, b, dims):
    return dot(a[0], b[0], dims) + (dot(a[0], b[1], dims) + dot(a[1], b[0], dims))


def silu(x):
    return x / (1.0 + jnp.exp(jnp.minimum(-x, 87.0)))


def pick_kernel(plan, ids_hbm, table_hbm, *refs):
    _, n_item, _, item_orders, _ = plan
    outs, (ids, table, picked, sems) = refs[:4], refs[4:]
    n_neg = ids.shape[1]
    n_step, step = table.shape[:2]
    me, item = lax.axis_index("seq"), lax.axis_index("item")
    copies = [pltpu.make_async_copy(ids_hbm, ids, sems.at[n_step])]
    copies += [
        pltpu.make_async_copy(table_hbm.at[pl.ds(k * step, step)], table.at[k], sems.at[k]) for k in range(n_step)
    ]
    for copy in copies:
        copy.start()
    copies[0].wait()
    row = ids[pl.ds(me, 1), :].astype(f32)
    col = jnp.broadcast_to(row, (LANES, n_neg)).T
    lane = lax.broadcasted_iota(i32, (n_neg, LANES), 1)
    for k in range(n_step):
        hot = [
            jnp.where(col == (lane + (k * step + c)).astype(f32), 1.0, 0.0).astype(bf16) for c in range(0, step, LANES)
        ]
        hot = jnp.concatenate(hot, axis=1)
        copies[1 + k].wait()
        t_hi, t_lo = split(table[k])
        part = dot(hot, t_hi, NN) + dot(hot, t_lo, NN)
        picked[...] = part if k == 0 else picked[...] + part
    n_part = n_neg // (2 * n_item)
    for half in range(2):
        for m, r in enumerate(item_orders[half]):
            first = half * (n_neg // 2) + (item ^ r) * n_part
            out = outs[2 * half + m // (n_item // 2)]
            out[m % (n_item // 2)] = picked[pl.ds(pl.multiple_of(first, n_part), n_part)]


def pick_rows(plan, ids, table):
    n_rows, width = table.shape
    n_item, n_neg = plan[1], ids.shape[1]
    step = 256
    out = (n_item // 2, n_neg // (2 * n_item), width)
    return pl.pallas_call(
        functools.partial(pick_kernel, plan),
        in_specs=[pl.BlockSpec(memory_space=pltpu.HBM)] * 2,
        out_specs=[pl.BlockSpec(memory_space=pltpu.VMEM)] * 4,
        out_shape=[jax.ShapeDtypeStruct(out, f32)] * 4,
        scratch_shapes=[
            pltpu.VMEM(ids.shape, i32),
            pltpu.VMEM((n_rows // step, step, width), f32),
            pltpu.VMEM((n_neg, width), f32),
            pltpu.SemaphoreType.DMA((n_rows // step + 1,)),
        ],
        compiler_params=alone,
        cost_estimate=pl.CostEstimate(flops=4 * n_neg * n_rows * width, bytes_accessed=4 * n_rows * width, transcendentals=0),
        name="pick_rows",
    )(ids, table)


def prepare_kernel(x_ref, u_ref, q_ref, gates_ref, queries_ref):
    both = silu(dot3(split(x_ref[...]), split(jnp.concatenate([u_ref[...], q_ref[...]], axis=1)), NN))
    gates_ref[...], queries_ref[...] = both[:, :LANES], both[:, LANES:]


def prepare(rows_in, w_uvqk):
    tok, width = rows_in.shape
    n = width // LANES
    own = pl.BlockSpec((tok, LANES), lambda j: (0, j))
    return pl.pallas_call(
        prepare_kernel,
        grid=(n,),
        in_specs=[
            pl.BlockSpec((tok, width), lambda j: (0, 0)),
            pl.BlockSpec((width, LANES), lambda j: (0, j)),
            pl.BlockSpec((width, LANES), lambda j: (0, 2 * n + j)),
        ],
        out_specs=[own, own],
        out_shape=[jax.ShapeDtypeStruct((tok, width), f32)] * 2,
        compiler_params=params,
        cost_estimate=pl.CostEstimate(flops=12 * tok * width * width, bytes_accessed=2 * width * width * 4, transcendentals=0),
        name="prepare",
    )(rows_in, w_uvqk, w_uvqk)


def attend_kernel(order, n_seq, lengths, *refs):
    x_refs, (q_ref, v_ref, k_ref, out_ref, x_hi, x_lo, allowed) = refs[:n_seq], refs[n_seq:]
    tok = q_ref.shape[0]
    head = x_hi.shape[1] // H

    @pl.when(pl.program_id(0) == 0)
    def _():
        me = lax.axis_index("seq")
        q_pos = me * tok + lax.broadcasted_iota(i32, (tok, tok), 0)
        col = lax.broadcasted_iota(i32, (tok, tok), 1)

        def user(pos):
            ids, end = jnp.zeros_like(pos), 0
            for k in range(lengths.shape[1]):
                end = end + lengths[0, k]
                ids = ids + (pos >= end).astype(i32)
            return ids

        q_user = user(q_pos)
        for n in range(n_seq):
            span = pl.ds(n * tok, tok)
            x_hi[span], x_lo[span] = split(x_refs[n][...])
            k_pos = (me ^ order[n]) * tok + col
            seen = (q_user == user(k_pos)) & (q_pos >= k_pos)
            allowed[:, span] = seen.astype(f32)

    x = (x_hi[...], x_lo[...])
    vk = silu(dot3(x, split(jnp.concatenate([v_ref[...], k_ref[...]], axis=1)), NN))
    v_hi, v_lo = split(vk[:, :LANES])
    k_hi, k_lo = split(vk[:, LANES:])
    k_both = jnp.concatenate([k_hi, k_lo], axis=1)
    v_both = jnp.concatenate([v_hi, v_lo], axis=1)
    queries = q_ref[...]
    n_heads = LANES // head
    of_head = lax.broadcasted_iota(i32, (tok, LANES), 1) // head
    stacked = jnp.concatenate([jnp.where(of_head == h, queries, 0.0) for h in range(n_heads)], axis=0)
    q_hi, q_lo = split(stacked)
    scores = dot(jnp.concatenate([q_hi, q_hi], axis=1), k_both, NT) + dot(q_lo, k_hi, NT)
    seen = allowed[...]
    weights = silu(scores) * jnp.concatenate([seen] * n_heads, axis=0)
    w_hi, w_lo = split(weights)
    wide = dot(w_hi, v_both, NN)
    mine = wide[:, :LANES] + wide[:, LANES:] + dot(w_lo, v_hi, NN)
    total = mine[:tok]
    for h in range(1, n_heads):
        total = jnp.where(of_head == h, mine[h * tok : (h + 1) * tok], total)
    out_ref[...] = total


def attend(lengths, pieces, order, queries, w_uvqk, first, count):
    tok, width = pieces[0].shape
    n_seq = len(pieces)
    whole = pl.BlockSpec((tok, width), lambda j: (0, 0))
    n = width // LANES
    v = pl.BlockSpec((width, LANES), lambda j: (0, n + first + j))
    k = pl.BlockSpec((width, LANES), lambda j: (0, 3 * n + first + j))
    return pl.pallas_call(
        functools.partial(attend_kernel, order, n_seq),
        grid=(count,),
        in_specs=[pl.BlockSpec(memory_space=pltpu.SMEM)]
        + [whole] * n_seq
        + [pl.BlockSpec((tok, LANES), lambda j: (0, first + j)), v, k],
        out_specs=pl.BlockSpec((tok, LANES), lambda j: (0, j)),
        out_shape=jax.ShapeDtypeStruct((tok, count * LANES), f32),
        scratch_shapes=[
            pltpu.VMEM((n_seq * tok, width), bf16),
            pltpu.VMEM((n_seq * tok, width), bf16),
            pltpu.VMEM((tok, n_seq * tok), f32),
        ],
        compiler_params=params,
        cost_estimate=pl.CostEstimate(flops=count * 2000000000, bytes_accessed=2 * width * width * 4, transcendentals=0),
        name="attend",
    )(lengths, *pieces, queries, w_uvqk, w_uvqk)


def project_kernel(n_parts, words, *refs):
    parts, (gates, gain, w_out, rows_in, targets, out_ref) = refs[:n_parts], refs[n_parts:]
    tok, width = rows_in.shape
    attended = jnp.concatenate([p[...] for p in parts], axis=1)
    centered = attended - jnp.mean(attended, axis=1, keepdims=True)
    variance = jnp.mean(centered * centered, axis=1, keepdims=True)
    normed = centered * lax.rsqrt(variance + epsilon) * gain[...]
    gated = split(normed * gates[...])
    out_ref[:tok] = rows_in[...] + dot3(gated, split(w_out[...]), NN)
    out_ref[tok:] = jnp.zeros((EXTRA, width), f32)
    out_ref[tok : tok + 1, :tok] = targets[...].astype(f32)
    for k in range(words.shape[1]):
        out_ref[tok + 1 : tok + 2, k * LANES : (k + 1) * LANES] = jnp.full((1, LANES), words[0, k].astype(f32))


def project(words, parts, gates, gain, w_out, rows_in, targets):
    tok, width = rows_in.shape
    return pl.pallas_call(
        lambda words, *refs: project_kernel(len(parts), words, *refs),
        in_specs=[pl.BlockSpec(memory_space=pltpu.SMEM)] + [pl.BlockSpec(memory_space=pltpu.VMEM)] * (len(parts) + 5),
        out_specs=pl.BlockSpec(memory_space=pltpu.VMEM),
        out_shape=jax.ShapeDtypeStruct((tok + EXTRA, width), f32),
        compiler_params=params,
        cost_estimate=pl.CostEstimate(flops=6 * tok * width * width, bytes_accessed=2 * width * width * 4, transcendentals=0),
        name="project",
    )(words, *parts, gates, gain, w_out, rows_in, targets)


def transpose_kernel(*refs):
    o_refs, (o_hi, o_lo) = refs[:-2], refs[-2:]
    tok = o_refs[0].shape[0] - EXTRA
    for n, o_ref in enumerate(o_refs):
        span = pl.ds(n * tok, tok)
        o_hi[:, span], o_lo[:, span] = split(o_ref[:tok].T)


def transpose_outputs(outputs):
    tok, width = outputs[0].shape[0] - EXTRA, outputs[0].shape[1]
    vmem = pl.BlockSpec(memory_space=pltpu.VMEM)
    return pl.pallas_call(
        transpose_kernel,
        in_specs=[vmem] * len(outputs),
        out_specs=[vmem] * 2,
        out_shape=[jax.ShapeDtypeStruct((width, tok * len(outputs)), bf16)] * 2,
        compiler_params=params,
        cost_estimate=pl.CostEstimate(flops=0, bytes_accessed=2**22, transcendentals=0),
        name="transpose_outputs",
    )(*outputs)


def loss_kernel(plan, o_hi, o_lo, *refs):
    n_seq, n_item, seq_order, item_orders, aligned = plan
    o_refs, refs = refs[:n_seq], refs[n_seq:]
    n_in = 4 if aligned else 1
    n_refs, panel_refs, refs = refs[:n_in], refs[n_in : 2 * n_in], refs[2 * n_in :]
    loss_ref, g_ref, n_hi, n_lo, g_hi, g_lo, panel = refs
    me, item = lax.axis_index("seq"), lax.axis_index("item")
    n_neg, width = n_hi.shape
    tok = o_refs[0].shape[0] - EXTRA

    if aligned:
        n_part = n_neg // (2 * n_item)
        for half in range(2):
            for m, r in enumerate(item_orders[half]):
                source = n_refs[2 * half + m // (n_item // 2)]
                rows = source[pl.ds((m % (n_item // 2)) * n_part, n_part)]
                place = pl.ds(pl.multiple_of(half * (n_neg // 2) + (item ^ r) * n_part, n_part), n_part)
                n_hi[place], n_lo[place] = split(rows)
    else:
        n_hi[...], n_lo[...] = split(n_refs[0][...])

    negatives = (n_hi[...], n_lo[...])
    loss = jnp.zeros((1, 2 * tok), f32)
    columns = me * n_neg + lax.broadcasted_iota(i32, (n_neg, 2 * tok), 0)
    for p in range(n_seq // 2):
        both = o_refs[2 * p], o_refs[2 * p + 1]
        span = pl.ds(2 * p * tok, 2 * tok)
        target = jnp.concatenate([b[tok : tok + 1, :tok] for b in both], axis=1).astype(i32)
        words = jnp.concatenate([b[tok + 1 : tok + 2, :tok] for b in both], axis=1).astype(i32)
        logits = dot3(negatives, (o_hi[:, span], o_lo[:, span]), NN)
        is_target = columns == target
        live = jnp.bitwise_and(jnp.right_shift(jnp.broadcast_to(words, columns.shape), columns // LANES), 1).astype(f32)
        weight = jnp.where(is_target, beta_weight, live)
        signed = jnp.where(is_target, -logits, logits)
        small = jnp.exp(-jnp.abs(logits))
        loss = loss + jnp.sum(weight * (jnp.maximum(signed, 0.0) + jnp.log1p(small)), axis=0, keepdims=True)
        chance = jnp.where(signed >= 0.0, 1.0, small) / (1.0 + small)
        grad = jnp.where(is_target, -weight, weight) * chance
        g_ref[:, span] = grad
        g_hi[:, span], g_lo[:, span] = split(grad)
    loss_ref[...] = jnp.full((EXTRA, LANES), jnp.sum(loss))
    whole = dot3((o_hi[...], o_lo[...]), (g_hi[...], g_lo[...]), NT)
    if not aligned:
        panel_refs[0][...] = whole
        return
    panel[...] = whole
    n_dim = width // (n_seq * n_item)
    part = n_dim // 2
    for half in range(2):
        for m, r in enumerate(item_orders[half]):
            out = panel_refs[2 * half + m // (n_item // 2)]
            k = m % (n_item // 2)
            for n, q in enumerate(seq_order):
                first = (me ^ q) * (n_item * n_dim) + (item ^ r) * n_dim + half * part
                out[k, n * part : (n + 1) * part] = panel[pl.ds(pl.multiple_of(first, part), part)]


def loss_terms(transposed, outputs, negatives, plan, n_neg):
    n_seq, n_item, _, _, aligned = plan
    tok, width = outputs[0].shape[0] - EXTRA, outputs[0].shape[1]
    group_len = tok * n_seq
    vmem = pl.BlockSpec(memory_space=pltpu.VMEM)
    if aligned:
        panel = [jax.ShapeDtypeStruct((n_item // 2, width // (2 * n_item), n_neg), f32)] * 4
    else:
        panel = [jax.ShapeDtypeStruct((width, n_neg), f32)]
    loss = jax.ShapeDtypeStruct((EXTRA, LANES), f32)
    grad = jax.ShapeDtypeStruct((n_neg, group_len), f32)
    parts = [jax.ShapeDtypeStruct((n_neg, width), bf16)] * 2
    out_shape = [*panel, loss, grad, *parts]
    return pl.pallas_call(
        functools.partial(loss_kernel, plan),
        in_specs=[vmem] * (2 + n_seq + len(negatives)),
        out_specs=[vmem] * len(out_shape),
        out_shape=out_shape,
        scratch_shapes=[pltpu.VMEM((n_neg, group_len), bf16)] * 2 + [pltpu.VMEM((width, n_neg), f32)],
        compiler_params=params,
        cost_estimate=pl.CostEstimate(flops=12 * group_len * width * n_neg, bytes_accessed=16 * n_neg * width, transcendentals=0),
        name="loss_terms",
    )(*transposed, *outputs, *negatives)


def rows_kernel(n_seq, grad, n_hi, n_lo, kept_rows, sent_rows):
    tok = grad.shape[1] // n_seq
    negatives = (n_hi[...], n_lo[...])
    for p in range(n_seq // 2):
        rows = dot3(split(grad[:, 2 * p * tok : 2 * (p + 1) * tok].T), negatives, NN)
        for k in range(2):
            n = 2 * p + k
            target_ref = kept_rows if n < n_seq // 2 else sent_rows
            target_ref[n % (n_seq // 2)] = rows[k * tok : (k + 1) * tok]


def event_rows(grad, n_hi, n_lo, n_seq):
    n_neg, group_len = grad.shape
    width = n_hi.shape[1]
    vmem = pl.BlockSpec(memory_space=pltpu.VMEM)
    return pl.pallas_call(
        functools.partial(rows_kernel, n_seq),
        in_specs=[vmem] * 3,
        out_specs=[vmem] * 2,
        out_shape=[jax.ShapeDtypeStruct((n_seq // 2, group_len // n_seq, width), f32)] * 2,
        compiler_params=params,
        cost_estimate=pl.CostEstimate(flops=6 * group_len * width * n_neg, bytes_accessed=8 * n_neg * width, transcendentals=0),
        name="event_rows",
    )(grad, n_hi, n_lo)


def pieces_kernel(spread, owners, which, loss, outs):
    n_dim, n_rows = spread[0].shape
    item = lax.axis_index("item")
    for r, out in zip(which, outs):
        total = jnp.where(owners[0] == item ^ r, spread[0], 0.0)
        for p in range(1, len(owners)):
            total = total + jnp.where(owners[p] == item ^ r, spread[p], 0.0)
        for c in range(n_rows // LANES):
            out[c * n_dim : (c + 1) * n_dim] = total[:, c * LANES : (c + 1) * LANES]
        out[n_rows // LANES * n_dim :] = loss


def owners_of(order, per_panel, owner):
    return [owner[(lax.axis_index("seq") ^ r) // per_panel] for r in order]


def spread_kernel(order, per_panel, which, owner, ids, loss, *refs):
    moved, outs = refs[: len(order)], refs[len(order) :]
    n_dim, n_neg = moved[0].shape
    n_rows = (outs[0].shape[0] - EXTRA) // n_dim * LANES
    row = lax.broadcasted_iota(i32, (n_rows, n_neg), 0)
    spread = []
    for p, r in enumerate(order):
        hot = jnp.where(row == ids[pl.ds(lax.axis_index("seq") ^ r, 1), :], 1.0, 0.0).astype(bf16)
        both = dot(jnp.concatenate(split(moved[p][:n_dim]), axis=0), hot, NT)
        spread.append(both[:n_dim] + both[n_dim:])
    total = loss[...]
    for block in moved:
        if block.shape[0] > n_dim:
            total = total + block[n_dim:, :LANES]
    pieces_kernel(spread, owners_of(order, per_panel, owner), which, total, outs)


def spread_rows(order, per_panel, owner, moved, ids, loss, n_item, n_rows):
    vmem = pl.BlockSpec(memory_space=pltpu.VMEM)
    smem = pl.BlockSpec(memory_space=pltpu.SMEM)
    n_dim = moved[0].shape[0]
    out = jax.ShapeDtypeStruct((n_rows // LANES * n_dim + EXTRA, LANES), f32)
    return pl.pallas_call(
        functools.partial(spread_kernel, order, per_panel, tuple(range(n_item))),
        in_specs=[smem, vmem, vmem] + [vmem] * len(moved),
        out_specs=[vmem] * n_item,
        out_shape=[out] * n_item,
        compiler_params=params,
        cost_estimate=pl.CostEstimate(flops=4 * len(moved) * moved[0].size * n_rows, bytes_accessed=2**21, transcendentals=0),
        name="spread_rows",
    )(owner, ids, loss, *moved)


def assemble_kernel(order, pair, members, n_item, n_dim, events, kept, got, *refs):
    groups, (out_ref, loss_ref, event_ref, quarter) = refs[:-4], refs[-4:]
    event_ref[...] = kept[...] + got[...]
    n_rest = len(order)
    me, item = lax.axis_index("seq"), lax.axis_index("item")
    cols = n_item * n_dim
    n_tiles = out_ref.shape[0] // LANES
    block = pl.program_id(0)

    def places(k):
        return [(groups[g], m) for g in range(k, len(groups), n_rest) for m in range(groups[g].shape[0])]

    for c in range(n_tiles):
        for k, q in enumerate(order):
            for d, across in enumerate(pair):
                first = ((block * n_tiles + c) * 4 + 2 * d) * n_dim
                for r, (group, m) in zip(members, places(k)):
                    for chunk in range(2):
                        place = pl.ds(pl.multiple_of((item ^ r ^ (chunk * n_item // 2)) * n_dim, n_dim), n_dim)
                        quarter[2 * k + d, place] = group[m, pl.ds(pl.multiple_of(first + chunk * n_dim, n_dim), n_dim)]
                place = pl.ds(pl.multiple_of((me ^ q ^ across) * cols, cols), cols)
                out_ref[c * LANES : (c + 1) * LANES, place] = quarter[2 * k + d].T

    @pl.when(block == 0)
    def _():
        total = jnp.zeros((EXTRA, LANES), f32)
        for k in range(n_rest):
            for group, m in places(k):
                total = total + group[m, group.shape[1] - EXTRA :]
        loss_ref[0, 0] = jnp.sum(total) / (EXTRA * LANES * events)


def assemble(table, kept, got, order, pair, members, n_item, n_dim, n_rows, events):
    width = n_item * n_dim * len(order) * len(pair)
    step = min(n_rows, 512)
    pieces = sum(table, [])
    rows = pl.BlockSpec((1, kept.shape[1] * step // n_rows, width), lambda j: (0, j, 0))
    return pl.pallas_call(
        functools.partial(assemble_kernel, order, pair, members, n_item, n_dim, events),
        grid=(n_rows // step,),
        in_specs=[rows, rows] + [pl.BlockSpec(memory_space=pltpu.VMEM)] * len(pieces),
        out_specs=[pl.BlockSpec((step, width), lambda j: (j, 0)), pl.BlockSpec(memory_space=pltpu.SMEM), rows],
        out_shape=[
            jax.ShapeDtypeStruct((n_rows, width), f32),
            jax.ShapeDtypeStruct((1, 1), f32),
            jax.ShapeDtypeStruct(kept.shape, f32),
        ],
        scratch_shapes=[pltpu.VMEM((2 * len(order), n_item * n_dim, LANES), f32)],
        compiler_params=params,
        cost_estimate=pl.CostEstimate(flops=0, bytes_accessed=8 * n_rows * width, transcendentals=0),
        name="assemble",
    )(kept, got, *pieces)


def per_device(
    events,
    w_uvqk,
    out_gain,
    w_out,
    item_table,
    user_lengths,
    neg_ids,
    panel_owner,
    block_mask,
    targets,
):
    rows_in = events[0]
    tok, width = rows_in.shape
    n_rows = item_table.shape[0]
    n_seq, n_item = lax.axis_size("seq"), lax.axis_size("item")
    s, i = lax.axis_index("seq").astype(i32), lax.axis_index("item").astype(i32)
    group_len = tok * n_seq
    seq_bits = bits_of(n_seq)
    seq_order = orders(seq_bits)
    bit_lists = two_orders(n_item)
    shared = bit_lists[0][:-2]
    item_orders = [orders(bits) for bits in bit_lists]
    flat_ids = neg_ids.reshape(-1)
    n_neg = flat_ids.shape[0] // n_seq
    per_panel = neg_ids.shape[1] // n_neg
    n_part = n_neg // (2 * n_item)
    n_dim = width // (n_seq * n_item)
    aligned = n_part % 16 == 0 and n_dim % 16 == 0 and (n_item * n_dim) % LANES == 0
    plan = (n_seq, n_item, tuple(seq_order), tuple(tuple(o) for o in item_orders), aligned)

    ids_by_seq = flat_ids.reshape(n_seq, n_neg)
    rel = i ^ jnp.array(item_orders, i32)
    root = panel_owner[s // per_panel]
    if aligned:
        parts = pick_rows(plan, ids_by_seq, item_table)
        parts = [parts[:2], parts[2:]]
    else:
        spot = s * n_neg + rel[:, :, None] * n_part + jnp.arange(n_part, dtype=i32)
        spot = spot + jnp.array([0, n_neg // 2], i32)[:, None, None]
        rows = item_table[flat_ids[spot.reshape(-1)]].reshape(2, n_item, n_part, width)
        parts = [(part[: n_item // 2], part[n_item // 2 :]) for part in rows]
    pieces = gather_pieces(rows_in, "seq", seq_bits)
    gates, queries = prepare(rows_in, w_uvqk)
    groups = width // LANES
    attended = [
        attend(user_lengths, pieces, seq_order, queries, w_uvqk, first, count)
        for first, count in ((0, groups // 4), (groups // 4, groups - groups // 4))
    ]
    for step in range(2):
        others = [swap(parts[half][1], "item", bits[-1 - step]) for half, bits in enumerate(bit_lists)]
        if step == 1:
            *others, attended[0] = lax.optimization_barrier((*others, attended[0]))
        for half, bits in enumerate(bit_lists):
            kept, other = parts[half][0], others[half]
            same = ((i ^ root) >> bits[-1 - step]) & 1 == 0
            cut = kept.shape[0] if step == 1 else kept.shape[0] // 2
            parts[half] = (jnp.where(same, kept[:cut], other[:cut]), jnp.where(same, kept[cut:], other[cut:]))
    both = jnp.stack([part[0] for part in parts])
    for bit in shared[:0:-1]:
        cut = both.shape[1] // 2
        other = swap(both[:, cut:], "item", bit)
        both = jnp.where(((i ^ root) >> bit) & 1 == 0, both[:, :cut], other)
    other = swap(both, "item", shared[0])
    same = ((i ^ root) >> shared[0]) & 1 == 0
    parts = [
        jnp.where(same, both[half], jnp.concatenate([other[half, 1:], other[half, :1]], axis=0)) for half in range(2)
    ]
    for step in range(1, len(bit_lists[0]) - 1):
        for half, bits in enumerate(bit_lists):
            parts[half] = jnp.concatenate([parts[half], swap(parts[half], "item", bits[step])], axis=0)
    negatives = []
    for half, bits in enumerate(bit_lists):
        negatives += [parts[half], swap(parts[half], "item", bits[-1])]
    if aligned:
        negatives = [n.reshape(-1, width) for n in negatives]
    else:
        negatives = [
            true_order(jnp.concatenate(negatives[2 * half : 2 * half + 2], axis=0), item_orders[half], i)
            for half in range(2)
        ]
        negatives = [jnp.concatenate([n.reshape(-1, width) for n in negatives], axis=0)]

    own_outputs = project(block_mask, attended, gates, out_gain[None], w_out, rows_in, targets)
    outputs = gather_pieces(own_outputs, "seq", seq_bits)

    *panel, loss, grad, n_hi, n_lo = loss_terms(transpose_outputs(outputs), outputs, negatives, plan, n_neg)
    kept_rows, sent_rows = event_rows(grad, n_hi, n_lo, n_seq)
    if not aligned:
        blocks = panel[0].reshape(n_seq, n_item, 2, n_dim // 2, n_neg).transpose(2, 1, 0, 3, 4)
        panel = []
        for half in range(2):
            mine = blocks[half][rel[half]][:, s ^ jnp.array(seq_order, i32)].reshape(n_item, -1, n_neg)
            panel += [mine[: n_item // 2], mine[n_item // 2 :]]

    for step in range(2):
        got = [swap(panel[2 * half + 1], "item", bits[-1 - step]) for half, bits in enumerate(bit_lists)]
        if step == 0:
            *got, kept_rows, sent_rows = lax.optimization_barrier((*got, kept_rows, sent_rows))
        cut = panel[0].shape[0] // 2
        panel = [
            k[:cut] + g[:cut] if part == 0 else k[cut:] + g[cut:]
            for k, g in zip(panel[::2], got)
            for part in range(2)
        ]
    kept, sent = panel[::2], panel[1::2]
    kept, sent = jnp.concatenate(kept, axis=1), jnp.concatenate(sent, axis=1)
    for bit in shared[:0:-1]:
        got = swap(sent, "item", bit)
        cut = kept.shape[0] // 2
        kept, sent = kept[:cut] + got[:cut], kept[cut:] + got[cut:]
    tail = jnp.concatenate([loss] * (n_neg // LANES), axis=1)
    mine = jnp.concatenate([kept[0], sent[0], tail], axis=0)
    other = swap(mine, "item", shared[0])
    for n, bit in enumerate(seq_bits[::-1]):
        got_rows = swap(sent_rows, "seq", bit)
        if n < n_seq.bit_length() - 2:
            half = kept_rows.shape[0] // 2
            sent_rows = kept_rows[half:] + got_rows[half:]
            kept_rows = kept_rows[:half] + got_rows[:half]
    other, got_rows = lax.optimization_barrier((other, got_rows))
    rows = kept.shape[1]
    total = [kept[0] + other[rows : 2 * rows], sent[0] + other[:rows]]
    loss = loss + other[2 * rows :, :LANES]
    part = n_dim // 2
    pair = (0, 1 << seq_bits[0])
    moved = []
    for r in seq_order:
        block = []
        for d in pair:
            k = seq_order.index(r ^ d)
            spans = [slice(h * n_seq * part + k * part, h * n_seq * part + (k + 1) * part) for h in range(2)]
            block += [chunk[span] for chunk in total for span in spans]
        if r == pair[1]:
            block.append(jnp.concatenate([loss] * (n_neg // LANES), axis=1))
        block = jnp.concatenate(block, axis=0)
        moved.append(send(block, "seq", r) if r else block)
    n_near, top = n_item // 2, 1 << shared[0]
    if aligned:
        sent = spread_rows(seq_order, per_panel, panel_owner, moved, ids_by_seq, loss, n_near, n_rows)
    else:
        source = s ^ jnp.array(seq_order, i32)
        ids, owner = ids_by_seq[source], panel_owner[source // per_panel]
        hot = (ids[:, :, None] == jnp.arange(n_rows, dtype=i32)).astype(f32)
        loss = loss + moved[seq_order.index(pair[1])][4 * n_dim :, :LANES]
        moved = jnp.stack([block[: 4 * n_dim] for block in moved])
        spread = jnp.einsum("pdc,pcr->pdr", moved, hot, precision=high)
        mine = (owner[None, :] == (i ^ jnp.arange(n_near, dtype=i32))[:, None]).astype(f32)
        sent = jnp.sum(mine[:, :, None, None] * spread[None], axis=1)
        sent = sent.reshape(n_near, 4 * n_dim, -1, LANES).transpose(0, 2, 1, 3).reshape(n_near, -1, LANES)
        sent = [jnp.concatenate([sent[r], loss], axis=0) for r in range(n_near)]

    taken = [send(sent[r], "item", r) if r else sent[r] for r in range(n_near)]
    which = [[0], [1], [2], list(range(3, n_near))]
    table = [gather_pieces(jnp.stack([taken[r] for r in members]), "seq", seq_bits[1:]) for members in which]
    members, rest_order = sum(which, []), orders(seq_bits[1:])
    if aligned:
        table_grad, mean_loss, event_grad = assemble(table, kept_rows, got_rows, rest_order, pair, members, n_item, n_dim, n_rows, group_len * n_item)
        mean_loss = mean_loss.reshape(())
    else:
        table = jnp.stack([jnp.concatenate(groups, axis=0) for groups in zip(*table)])
        event_grad = kept_rows + got_rows
        mean_loss = jnp.sum(table[:, :, -1, 0]) / (group_len * n_item)
        table = table[:, :, :-EXTRA].reshape(len(rest_order), n_near, -1, 2, 2, n_dim, LANES).transpose(1, 4, 0, 3, 2, 5, 6)
        table = table.reshape(n_item, n_seq, -1, n_dim, LANES)
        table = true_order(table, [r ^ chunk for r in members for chunk in (0, top)], i).swapaxes(0, 1)
        table = true_order(table, [r ^ d for r in rest_order for d in pair], s)
        table_grad = table.transpose(2, 4, 0, 1, 3).reshape(n_rows, width)
    return (mean_loss, event_grad, table_grad)


def solution(mesh):
    placed = (
        P("item", "seq", None),
        P(),
        P(),
        P(),
        P("item", None),
        P("item", None),
        P(),
        P(),
        P("item", "seq"),
        P("item", "seq"),
    )
    return jax.shard_map(
        per_device,
        mesh=mesh,
        in_specs=placed,
        out_specs=(P(), P("item", "seq", None), P("item", None)),
        check_vma=False,
    )
```

```python
import functools

import jax
import jax.numpy as jnp
from jax import lax
from jax.experimental import pallas as pl
from jax.experimental.pallas import tpu as pltpu
from jax.sharding import PartitionSpec as P

H = 16
LANES = 128
EXTRA = 8

beta_weight = 0.75
epsilon = 1e-05

f32, bf16, i32 = jnp.float32, jnp.bfloat16, jnp.int32
high = lax.Precision.HIGH
NN, NT = ((1,), (0,)), ((1,), (1,))
params = pltpu.CompilerParams(vmem_limit_bytes=40 * 2**20)
alone = pltpu.CompilerParams(vmem_limit_bytes=62 * 2**20)


def swap(block, axis, bit):
    size = lax.axis_size(axis)
    return lax.ppermute(block, axis, [(i, i ^ (1 << bit)) for i in range(size)])


def send(block, axis, r):
    size = lax.axis_size(axis)
    return lax.ppermute(block, axis, [(i, i ^ r) for i in range(size)])


def bits_of(size):
    return list(range(size.bit_length() - 1))[::-1]


def two_orders(size):
    up = bits_of(size)
    return [up, up[:-2] + up[:-3:-1]]


def orders(bits):
    order = [0]
    for bit in bits:
        order = order + [r ^ (1 << bit) for r in order]
    return order


def gather_pieces(block, axis, bits):
    pieces = [block]
    for bit in bits:
        pieces = pieces + [swap(piece, axis, bit) for piece in pieces]
    return pieces


def reduce_steps(kept, sent, axis, bits):
    for n, bit in enumerate(bits):
        got = swap(sent, axis, bit)
        if n == len(bits) - 1:
            return (kept + got)[0]
        half = kept.shape[0] // 2
        sent = kept[half:] + got[half:]
        kept = kept[:half] + got[:half]


def true_order(stacked, order, index):
    place = [0] * len(order)
    for k, r in enumerate(order):
        place[r] = k
    return stacked[jnp.array(place, i32)[index ^ jnp.arange(len(order), dtype=i32)]]


def split(x):
    top = x.astype(bf16)
    return top, (x - top.astype(f32)).astype(bf16)


def dot(a, b, dims):
    return lax.dot_general(a, b, (dims, ((), ())), preferred_element_type=f32)


def dot3(a, b, dims):
    return dot(a[0], b[0], dims) + (dot(a[0], b[1], dims) + dot(a[1], b[0], dims))


def silu(x):
    return x / (1.0 + jnp.exp(jnp.minimum(-x, 87.0)))


def pick_kernel(plan, ids_hbm, table_hbm, *refs):
    _, n_item, _, item_orders, _ = plan
    outs, (ids, table, picked, sems) = refs[:4], refs[4:]
    n_neg = ids.shape[1]
    n_step, step = table.shape[:2]
    me, item = lax.axis_index("seq"), lax.axis_index("item")
    copies = [pltpu.make_async_copy(ids_hbm, ids, sems.at[n_step])]
    copies += [
        pltpu.make_async_copy(table_hbm.at[pl.ds(k * step, step)], table.at[k], sems.at[k]) for k in range(n_step)
    ]
    for copy in copies:
        copy.start()
    copies[0].wait()
    row = ids[pl.ds(me, 1), :].astype(f32)
    col = jnp.broadcast_to(row, (LANES, n_neg)).T
    lane = lax.broadcasted_iota(i32, (n_neg, LANES), 1)
    for k in range(n_step):
        hot = [
            jnp.where(col == (lane + (k * step + c)).astype(f32), 1.0, 0.0).astype(bf16) for c in range(0, step, LANES)
        ]
        hot = jnp.concatenate(hot, axis=1)
        copies[1 + k].wait()
        t_hi, t_lo = split(table[k])
        part = dot(hot, t_hi, NN) + dot(hot, t_lo, NN)
        picked[...] = part if k == 0 else picked[...] + part
    n_part = n_neg // (2 * n_item)
    for half in range(2):
        for m, r in enumerate(item_orders[half]):
            first = half * (n_neg // 2) + (item ^ r) * n_part
            out = outs[2 * half + m // (n_item // 2)]
            out[m % (n_item // 2)] = picked[pl.ds(pl.multiple_of(first, n_part), n_part)]


def pick_rows(plan, ids, table):
    n_rows, width = table.shape
    n_item, n_neg = plan[1], ids.shape[1]
    step = 256
    out = (n_item // 2, n_neg // (2 * n_item), width)
    return pl.pallas_call(
        functools.partial(pick_kernel, plan),
        in_specs=[pl.BlockSpec(memory_space=pltpu.HBM)] * 2,
        out_specs=[pl.BlockSpec(memory_space=pltpu.VMEM)] * 4,
        out_shape=[jax.ShapeDtypeStruct(out, f32)] * 4,
        scratch_shapes=[
            pltpu.VMEM(ids.shape, i32),
            pltpu.VMEM((n_rows // step, step, width), f32),
            pltpu.VMEM((n_neg, width), f32),
            pltpu.SemaphoreType.DMA((n_rows // step + 1,)),
        ],
        compiler_params=alone,
        cost_estimate=pl.CostEstimate(flops=4 * n_neg * n_rows * width, bytes_accessed=4 * n_rows * width, transcendentals=0),
        name="pick_rows",
    )(ids, table)


def prepare_kernel(x_ref, u_ref, q_ref, gates_ref, queries_ref):
    both = silu(dot3(split(x_ref[...]), split(jnp.concatenate([u_ref[...], q_ref[...]], axis=1)), NN))
    gates_ref[...], queries_ref[...] = both[:, :LANES], both[:, LANES:]


def prepare(rows_in, w_uvqk):
    tok, width = rows_in.shape
    n = width // LANES
    own = pl.BlockSpec((tok, LANES), lambda j: (0, j))
    return pl.pallas_call(
        prepare_kernel,
        grid=(n,),
        in_specs=[
            pl.BlockSpec((tok, width), lambda j: (0, 0)),
            pl.BlockSpec((width, LANES), lambda j: (0, j)),
            pl.BlockSpec((width, LANES), lambda j: (0, 2 * n + j)),
        ],
        out_specs=[own, own],
        out_shape=[jax.ShapeDtypeStruct((tok, width), f32)] * 2,
        compiler_params=params,
        cost_estimate=pl.CostEstimate(flops=12 * tok * width * width, bytes_accessed=2 * width * width * 4, transcendentals=0),
        name="prepare",
    )(rows_in, w_uvqk, w_uvqk)


def attend_kernel(order, n_seq, lengths, *refs):
    x_refs, (q_ref, v_ref, k_ref, out_ref, x_hi, x_lo, allowed) = refs[:n_seq], refs[n_seq:]
    tok = q_ref.shape[0]
    head = x_hi.shape[1] // H

    @pl.when(pl.program_id(0) == 0)
    def _():
        me = lax.axis_index("seq")
        q_pos = me * tok + lax.broadcasted_iota(i32, (tok, tok), 0)
        col = lax.broadcasted_iota(i32, (tok, tok), 1)

        def user(pos):
            ids, end = jnp.zeros_like(pos), 0
            for k in range(lengths.shape[1]):
                end = end + lengths[0, k]
                ids = ids + (pos >= end).astype(i32)
            return ids

        q_user = user(q_pos)
        for n in range(n_seq):
            span = pl.ds(n * tok, tok)
            x_hi[span], x_lo[span] = split(x_refs[n][...])
            k_pos = (me ^ order[n]) * tok + col
            seen = (q_user == user(k_pos)) & (q_pos >= k_pos)
            allowed[:, span] = seen.astype(f32)

    x = (x_hi[...], x_lo[...])
    vk = silu(dot3(x, split(jnp.concatenate([v_ref[...], k_ref[...]], axis=1)), NN))
    v_hi, v_lo = split(vk[:, :LANES])
    k_hi, k_lo = split(vk[:, LANES:])
    k_both = jnp.concatenate([k_hi, k_lo], axis=1)
    v_both = jnp.concatenate([v_hi, v_lo], axis=1)
    queries = q_ref[...]
    n_heads = LANES // head
    of_head = lax.broadcasted_iota(i32, (tok, LANES), 1) // head
    stacked = jnp.concatenate([jnp.where(of_head == h, queries, 0.0) for h in range(n_heads)], axis=0)
    q_hi, q_lo = split(stacked)
    scores = dot(jnp.concatenate([q_hi, q_hi], axis=1), k_both, NT) + dot(q_lo, k_hi, NT)
    seen = allowed[...]
    weights = silu(scores) * jnp.concatenate([seen] * n_heads, axis=0)
    w_hi, w_lo = split(weights)
    wide = dot(w_hi, v_both, NN)
    mine = wide[:, :LANES] + wide[:, LANES:] + dot(w_lo, v_hi, NN)
    total = mine[:tok]
    for h in range(1, n_heads):
        total = jnp.where(of_head == h, mine[h * tok : (h + 1) * tok], total)
    out_ref[...] = total


def attend(lengths, pieces, order, queries, w_uvqk, first, count):
    tok, width = pieces[0].shape
    n_seq = len(pieces)
    whole = pl.BlockSpec((tok, width), lambda j: (0, 0))
    n = width // LANES
    v = pl.BlockSpec((width, LANES), lambda j: (0, n + first + j))
    k = pl.BlockSpec((width, LANES), lambda j: (0, 3 * n + first + j))
    return pl.pallas_call(
        functools.partial(attend_kernel, order, n_seq),
        grid=(count,),
        in_specs=[pl.BlockSpec(memory_space=pltpu.SMEM)]
        + [whole] * n_seq
        + [pl.BlockSpec((tok, LANES), lambda j: (0, first + j)), v, k],
        out_specs=pl.BlockSpec((tok, LANES), lambda j: (0, j)),
        out_shape=jax.ShapeDtypeStruct((tok, count * LANES), f32),
        scratch_shapes=[
            pltpu.VMEM((n_seq * tok, width), bf16),
            pltpu.VMEM((n_seq * tok, width), bf16),
            pltpu.VMEM((tok, n_seq * tok), f32),
        ],
        compiler_params=params,
        cost_estimate=pl.CostEstimate(flops=count * 2000000000, bytes_accessed=2 * width * width * 4, transcendentals=0),
        name="attend",
    )(lengths, *pieces, queries, w_uvqk, w_uvqk)


def project_kernel(n_parts, words, *refs):
    parts, (gates, gain, w_out, rows_in, targets, out_ref) = refs[:n_parts], refs[n_parts:]
    tok, width = rows_in.shape
    attended = jnp.concatenate([p[...] for p in parts], axis=1)
    centered = attended - jnp.mean(attended, axis=1, keepdims=True)
    variance = jnp.mean(centered * centered, axis=1, keepdims=True)
    normed = centered * lax.rsqrt(variance + epsilon) * gain[...]
    gated = split(normed * gates[...])
    out_ref[:tok] = rows_in[...] + dot3(gated, split(w_out[...]), NN)
    out_ref[tok:] = jnp.zeros((EXTRA, width), f32)
    out_ref[tok : tok + 1, :tok] = targets[...].astype(f32)
    for k in range(words.shape[1]):
        out_ref[tok + 1 : tok + 2, k * LANES : (k + 1) * LANES] = jnp.full((1, LANES), words[0, k].astype(f32))


def project(words, parts, gates, gain, w_out, rows_in, targets):
    tok, width = rows_in.shape
    return pl.pallas_call(
        lambda words, *refs: project_kernel(len(parts), words, *refs),
        in_specs=[pl.BlockSpec(memory_space=pltpu.SMEM)] + [pl.BlockSpec(memory_space=pltpu.VMEM)] * (len(parts) + 5),
        out_specs=pl.BlockSpec(memory_space=pltpu.VMEM),
        out_shape=jax.ShapeDtypeStruct((tok + EXTRA, width), f32),
        compiler_params=params,
        cost_estimate=pl.CostEstimate(flops=6 * tok * width * width, bytes_accessed=2 * width * width * 4, transcendentals=0),
        name="project",
    )(words, *parts, gates, gain, w_out, rows_in, targets)


def transpose_kernel(*refs):
    o_refs, (o_hi, o_lo) = refs[:-2], refs[-2:]
    tok = o_refs[0].shape[0] - EXTRA
    for n, o_ref in enumerate(o_refs):
        span = pl.ds(n * tok, tok)
        o_hi[:, span], o_lo[:, span] = split(o_ref[:tok].T)


def transpose_outputs(outputs):
    tok, width = outputs[0].shape[0] - EXTRA, outputs[0].shape[1]
    vmem = pl.BlockSpec(memory_space=pltpu.VMEM)
    return pl.pallas_call(
        transpose_kernel,
        in_specs=[vmem] * len(outputs),
        out_specs=[vmem] * 2,
        out_shape=[jax.ShapeDtypeStruct((width, tok * len(outputs)), bf16)] * 2,
        compiler_params=params,
        cost_estimate=pl.CostEstimate(flops=0, bytes_accessed=2**22, transcendentals=0),
        name="transpose_outputs",
    )(*outputs)


def loss_kernel(plan, o_hi, o_lo, *refs):
    n_seq, n_item, seq_order, item_orders, aligned = plan
    o_refs, refs = refs[:n_seq], refs[n_seq:]
    n_in = 4 if aligned else 1
    n_refs, panel_refs, refs = refs[:n_in], refs[n_in : 2 * n_in], refs[2 * n_in :]
    loss_ref, g_ref, n_hi, n_lo, g_hi, g_lo, panel = refs
    me, item = lax.axis_index("seq"), lax.axis_index("item")
    n_neg, width = n_hi.shape
    tok = o_refs[0].shape[0] - EXTRA

    if aligned:
        n_part = n_neg // (2 * n_item)
        for half in range(2):
            for m, r in enumerate(item_orders[half]):
                source = n_refs[2 * half + m // (n_item // 2)]
                rows = source[pl.ds((m % (n_item // 2)) * n_part, n_part)]
                place = pl.ds(pl.multiple_of(half * (n_neg // 2) + (item ^ r) * n_part, n_part), n_part)
                n_hi[place], n_lo[place] = split(rows)
    else:
        n_hi[...], n_lo[...] = split(n_refs[0][...])

    negatives = (n_hi[...], n_lo[...])
    loss = jnp.zeros((1, 2 * tok), f32)
    columns = me * n_neg + lax.broadcasted_iota(i32, (n_neg, 2 * tok), 0)
    for p in range(n_seq // 2):
        both = o_refs[2 * p], o_refs[2 * p + 1]
        span = pl.ds(2 * p * tok, 2 * tok)
        target = jnp.concatenate([b[tok : tok + 1, :tok] for b in both], axis=1).astype(i32)
        words = jnp.concatenate([b[tok + 1 : tok + 2, :tok] for b in both], axis=1).astype(i32)
        logits = dot3(negatives, (o_hi[:, span], o_lo[:, span]), NN)
        is_target = columns == target
        live = jnp.bitwise_and(jnp.right_shift(jnp.broadcast_to(words, columns.shape), columns // LANES), 1).astype(f32)
        weight = jnp.where(is_target, beta_weight, live)
        signed = jnp.where(is_target, -logits, logits)
        small = jnp.exp(-jnp.abs(logits))
        loss = loss + jnp.sum(weight * (jnp.maximum(signed, 0.0) + jnp.log1p(small)), axis=0, keepdims=True)
        chance = jnp.where(signed >= 0.0, 1.0, small) / (1.0 + small)
        grad = jnp.where(is_target, -weight, weight) * chance
        g_ref[:, span] = grad
        g_hi[:, span], g_lo[:, span] = split(grad)
    loss_ref[...] = jnp.full((EXTRA, LANES), jnp.sum(loss))
    whole = dot3((o_hi[...], o_lo[...]), (g_hi[...], g_lo[...]), NT)
    if not aligned:
        panel_refs[0][...] = whole
        return
    panel[...] = whole
    n_dim = width // (n_seq * n_item)
    part = n_dim // 2
    for half in range(2):
        for m, r in enumerate(item_orders[half]):
            out = panel_refs[2 * half + m // (n_item // 2)]
            k = m % (n_item // 2)
            for n, q in enumerate(seq_order):
                first = (me ^ q) * (n_item * n_dim) + (item ^ r) * n_dim + half * part
                out[k, n * part : (n + 1) * part] = panel[pl.ds(pl.multiple_of(first, part), part)]


def loss_terms(transposed, outputs, negatives, plan, n_neg):
    n_seq, n_item, _, _, aligned = plan
    tok, width = outputs[0].shape[0] - EXTRA, outputs[0].shape[1]
    group_len = tok * n_seq
    vmem = pl.BlockSpec(memory_space=pltpu.VMEM)
    if aligned:
        panel = [jax.ShapeDtypeStruct((n_item // 2, width // (2 * n_item), n_neg), f32)] * 4
    else:
        panel = [jax.ShapeDtypeStruct((width, n_neg), f32)]
    loss = jax.ShapeDtypeStruct((EXTRA, LANES), f32)
    grad = jax.ShapeDtypeStruct((n_neg, group_len), f32)
    parts = [jax.ShapeDtypeStruct((n_neg, width), bf16)] * 2
    out_shape = [*panel, loss, grad, *parts]
    return pl.pallas_call(
        functools.partial(loss_kernel, plan),
        in_specs=[vmem] * (2 + n_seq + len(negatives)),
        out_specs=[vmem] * len(out_shape),
        out_shape=out_shape,
        scratch_shapes=[pltpu.VMEM((n_neg, group_len), bf16)] * 2 + [pltpu.VMEM((width, n_neg), f32)],
        compiler_params=params,
        cost_estimate=pl.CostEstimate(flops=12 * group_len * width * n_neg, bytes_accessed=16 * n_neg * width, transcendentals=0),
        name="loss_terms",
    )(*transposed, *outputs, *negatives)


def rows_kernel(n_seq, grad, n_hi, n_lo, kept_rows, sent_rows):
    tok = grad.shape[1] // n_seq
    negatives = (n_hi[...], n_lo[...])
    for p in range(n_seq // 2):
        rows = dot3(split(grad[:, 2 * p * tok : 2 * (p + 1) * tok].T), negatives, NN)
        for k in range(2):
            n = 2 * p + k
            target_ref = kept_rows if n < n_seq // 2 else sent_rows
            target_ref[n % (n_seq // 2)] = rows[k * tok : (k + 1) * tok]


def event_rows(grad, n_hi, n_lo, n_seq):
    n_neg, group_len = grad.shape
    width = n_hi.shape[1]
    vmem = pl.BlockSpec(memory_space=pltpu.VMEM)
    return pl.pallas_call(
        functools.partial(rows_kernel, n_seq),
        in_specs=[vmem] * 3,
        out_specs=[vmem] * 2,
        out_shape=[jax.ShapeDtypeStruct((n_seq // 2, group_len // n_seq, width), f32)] * 2,
        compiler_params=params,
        cost_estimate=pl.CostEstimate(flops=6 * group_len * width * n_neg, bytes_accessed=8 * n_neg * width, transcendentals=0),
        name="event_rows",
    )(grad, n_hi, n_lo)


def pieces_kernel(spread, owners, which, loss, outs):
    n_dim, n_rows = spread[0].shape
    item = lax.axis_index("item")
    for r, out in zip(which, outs):
        total = jnp.where(owners[0] == item ^ r, spread[0], 0.0)
        for p in range(1, len(owners)):
            total = total + jnp.where(owners[p] == item ^ r, spread[p], 0.0)
        for c in range(n_rows // LANES):
            out[c * n_dim : (c + 1) * n_dim] = total[:, c * LANES : (c + 1) * LANES]
        out[n_rows // LANES * n_dim :] = loss


def owners_of(order, per_panel, owner):
    return [owner[(lax.axis_index("seq") ^ r) // per_panel] for r in order]


def hot_kernel(order, ids, out_ref):
    _, n_rows, n_neg = out_ref.shape
    row = lax.broadcasted_iota(i32, (n_rows, n_neg), 0)
    for p, r in enumerate(order):
        out_ref[p] = jnp.where(row == ids[pl.ds(lax.axis_index("seq") ^ r, 1), :], 1.0, 0.0).astype(bf16)


def hot_rows(order, ids, n_rows):
    vmem = pl.BlockSpec(memory_space=pltpu.VMEM)
    return pl.pallas_call(
        functools.partial(hot_kernel, order),
        in_specs=[vmem],
        out_specs=vmem,
        out_shape=jax.ShapeDtypeStruct((len(order), n_rows, ids.shape[1]), bf16),
        compiler_params=params,
        cost_estimate=pl.CostEstimate(flops=0, bytes_accessed=2**22, transcendentals=0),
        name="hot_rows",
    )(ids)


def spread_kernel(order, per_panel, which, owner, hot, loss, *refs):
    moved, outs = refs[: len(order)], refs[len(order) :]
    n_dim = moved[0].shape[0]
    spread = []
    for p in range(len(order)):
        both = dot(jnp.concatenate(split(moved[p][:n_dim]), axis=0), hot[p], NT)
        spread.append(both[:n_dim] + both[n_dim:])
    total = loss[...]
    for block in moved:
        if block.shape[0] > n_dim:
            total = total + block[n_dim:, :LANES]
    pieces_kernel(spread, owners_of(order, per_panel, owner), which, total, outs)


def spread_rows(order, per_panel, owner, moved, hot, loss, n_item, n_rows):
    vmem = pl.BlockSpec(memory_space=pltpu.VMEM)
    smem = pl.BlockSpec(memory_space=pltpu.SMEM)
    n_dim = moved[0].shape[0]
    out = jax.ShapeDtypeStruct((n_rows // LANES * n_dim + EXTRA, LANES), f32)
    return pl.pallas_call(
        functools.partial(spread_kernel, order, per_panel, tuple(range(n_item))),
        in_specs=[smem, vmem, vmem] + [vmem] * len(moved),
        out_specs=[vmem] * n_item,
        out_shape=[out] * n_item,
        compiler_params=params,
        cost_estimate=pl.CostEstimate(flops=4 * len(moved) * moved[0].size * n_rows, bytes_accessed=2**21, transcendentals=0),
        name="spread_rows",
    )(owner, hot, loss, *moved)


def assemble_kernel(order, pair, members, n_item, n_dim, events, kept, got, *refs):
    groups, (out_ref, loss_ref, event_ref, quarter) = refs[:-4], refs[-4:]
    event_ref[...] = kept[...] + got[...]
    n_rest = len(order)
    me, item = lax.axis_index("seq"), lax.axis_index("item")
    cols = n_item * n_dim
    n_tiles = out_ref.shape[0] // LANES
    block = pl.program_id(0)

    def places(k):
        return [(groups[g], m) for g in range(k, len(groups), n_rest) for m in range(groups[g].shape[0])]

    for c in range(n_tiles):
        for k, q in enumerate(order):
            for d, across in enumerate(pair):
                first = ((block * n_tiles + c) * 4 + 2 * d) * n_dim
                for r, (group, m) in zip(members, places(k)):
                    for chunk in range(2):
                        place = pl.ds(pl.multiple_of((item ^ r ^ (chunk * n_item // 2)) * n_dim, n_dim), n_dim)
                        quarter[2 * k + d, place] = group[m, pl.ds(pl.multiple_of(first + chunk * n_dim, n_dim), n_dim)]
                place = pl.ds(pl.multiple_of((me ^ q ^ across) * cols, cols), cols)
                out_ref[c * LANES : (c + 1) * LANES, place] = quarter[2 * k + d].T

    @pl.when(block == 0)
    def _():
        total = jnp.zeros((EXTRA, LANES), f32)
        for k in range(n_rest):
            for group, m in places(k):
                total = total + group[m, group.shape[1] - EXTRA :]
        loss_ref[0, 0] = jnp.sum(total) / (EXTRA * LANES * events)


def assemble(table, kept, got, order, pair, members, n_item, n_dim, n_rows, events):
    width = n_item * n_dim * len(order) * len(pair)
    step = min(n_rows, 512)
    pieces = sum(table, [])
    rows = pl.BlockSpec((1, kept.shape[1] * step // n_rows, width), lambda j: (0, j, 0))
    return pl.pallas_call(
        functools.partial(assemble_kernel, order, pair, members, n_item, n_dim, events),
        grid=(n_rows // step,),
        in_specs=[rows, rows] + [pl.BlockSpec(memory_space=pltpu.VMEM)] * len(pieces),
        out_specs=[pl.BlockSpec((step, width), lambda j: (j, 0)), pl.BlockSpec(memory_space=pltpu.SMEM), rows],
        out_shape=[
            jax.ShapeDtypeStruct((n_rows, width), f32),
            jax.ShapeDtypeStruct((1, 1), f32),
            jax.ShapeDtypeStruct(kept.shape, f32),
        ],
        scratch_shapes=[pltpu.VMEM((2 * len(order), n_item * n_dim, LANES), f32)],
        compiler_params=params,
        cost_estimate=pl.CostEstimate(flops=0, bytes_accessed=8 * n_rows * width, transcendentals=0),
        name="assemble",
    )(kept, got, *pieces)


def per_device(
    events,
    w_uvqk,
    out_gain,
    w_out,
    item_table,
    user_lengths,
    neg_ids,
    panel_owner,
    block_mask,
    targets,
):
    rows_in = events[0]
    tok, width = rows_in.shape
    n_rows = item_table.shape[0]
    n_seq, n_item = lax.axis_size("seq"), lax.axis_size("item")
    s, i = lax.axis_index("seq").astype(i32), lax.axis_index("item").astype(i32)
    group_len = tok * n_seq
    seq_bits = bits_of(n_seq)
    seq_order = orders(seq_bits)
    bit_lists = two_orders(n_item)
    shared = bit_lists[0][:-2]
    item_orders = [orders(bits) for bits in bit_lists]
    flat_ids = neg_ids.reshape(-1)
    n_neg = flat_ids.shape[0] // n_seq
    per_panel = neg_ids.shape[1] // n_neg
    n_part = n_neg // (2 * n_item)
    n_dim = width // (n_seq * n_item)
    aligned = n_part % 16 == 0 and n_dim % 16 == 0 and (n_item * n_dim) % LANES == 0
    plan = (n_seq, n_item, tuple(seq_order), tuple(tuple(o) for o in item_orders), aligned)

    ids_by_seq = flat_ids.reshape(n_seq, n_neg)
    rel = i ^ jnp.array(item_orders, i32)
    root = panel_owner[s // per_panel]
    if aligned:
        parts = pick_rows(plan, ids_by_seq, item_table)
        parts = [parts[:2], parts[2:]]
    else:
        spot = s * n_neg + rel[:, :, None] * n_part + jnp.arange(n_part, dtype=i32)
        spot = spot + jnp.array([0, n_neg // 2], i32)[:, None, None]
        rows = item_table[flat_ids[spot.reshape(-1)]].reshape(2, n_item, n_part, width)
        parts = [(part[: n_item // 2], part[n_item // 2 :]) for part in rows]
    pieces = gather_pieces(rows_in, "seq", seq_bits)
    gates, queries = prepare(rows_in, w_uvqk)
    groups = width // LANES
    attended = [
        attend(user_lengths, pieces, seq_order, queries, w_uvqk, first, count)
        for first, count in ((0, groups // 4), (groups // 4, groups - groups // 4))
    ]
    for step in range(2):
        others = [swap(parts[half][1], "item", bits[-1 - step]) for half, bits in enumerate(bit_lists)]
        if step == 1:
            *others, attended[0] = lax.optimization_barrier((*others, attended[0]))
        for half, bits in enumerate(bit_lists):
            kept, other = parts[half][0], others[half]
            same = ((i ^ root) >> bits[-1 - step]) & 1 == 0
            cut = kept.shape[0] if step == 1 else kept.shape[0] // 2
            parts[half] = (jnp.where(same, kept[:cut], other[:cut]), jnp.where(same, kept[cut:], other[cut:]))
    both = jnp.stack([part[0] for part in parts])
    for bit in shared[:0:-1]:
        cut = both.shape[1] // 2
        other = swap(both[:, cut:], "item", bit)
        both = jnp.where(((i ^ root) >> bit) & 1 == 0, both[:, :cut], other)
    other = swap(both, "item", shared[0])
    same = ((i ^ root) >> shared[0]) & 1 == 0
    parts = [
        jnp.where(same, both[half], jnp.concatenate([other[half, 1:], other[half, :1]], axis=0)) for half in range(2)
    ]
    for step in range(1, len(bit_lists[0]) - 1):
        for half, bits in enumerate(bit_lists):
            parts[half] = jnp.concatenate([parts[half], swap(parts[half], "item", bits[step])], axis=0)
    negatives = []
    for half, bits in enumerate(bit_lists):
        negatives += [parts[half], swap(parts[half], "item", bits[-1])]
    if aligned:
        negatives = [n.reshape(-1, width) for n in negatives]
    else:
        negatives = [
            true_order(jnp.concatenate(negatives[2 * half : 2 * half + 2], axis=0), item_orders[half], i)
            for half in range(2)
        ]
        negatives = [jnp.concatenate([n.reshape(-1, width) for n in negatives], axis=0)]

    own_outputs = project(block_mask, attended, gates, out_gain[None], w_out, rows_in, targets)
    outputs = gather_pieces(own_outputs, "seq", seq_bits)

    *panel, loss, grad, n_hi, n_lo = loss_terms(transpose_outputs(outputs), outputs, negatives, plan, n_neg)
    kept_rows, sent_rows = event_rows(grad, n_hi, n_lo, n_seq)
    if not aligned:
        blocks = panel[0].reshape(n_seq, n_item, 2, n_dim // 2, n_neg).transpose(2, 1, 0, 3, 4)
        panel = []
        for half in range(2):
            mine = blocks[half][rel[half]][:, s ^ jnp.array(seq_order, i32)].reshape(n_item, -1, n_neg)
            panel += [mine[: n_item // 2], mine[n_item // 2 :]]

    for step in range(2):
        got = [swap(panel[2 * half + 1], "item", bits[-1 - step]) for half, bits in enumerate(bit_lists)]
        if step == 0:
            *got, kept_rows, sent_rows = lax.optimization_barrier((*got, kept_rows, sent_rows))
        cut = panel[0].shape[0] // 2
        panel = [
            k[:cut] + g[:cut] if part == 0 else k[cut:] + g[cut:]
            for k, g in zip(panel[::2], got)
            for part in range(2)
        ]
    kept, sent = panel[::2], panel[1::2]
    kept, sent = jnp.concatenate(kept, axis=1), jnp.concatenate(sent, axis=1)
    for bit in shared[:0:-1]:
        got = swap(sent, "item", bit)
        cut = kept.shape[0] // 2
        kept, sent = kept[:cut] + got[:cut], kept[cut:] + got[cut:]
    tail = jnp.concatenate([loss] * (n_neg // LANES), axis=1)
    mine = jnp.concatenate([kept[0], sent[0], tail], axis=0)
    other = swap(mine, "item", shared[0])
    for n, bit in enumerate(seq_bits[::-1]):
        got_rows = swap(sent_rows, "seq", bit)
        if n < n_seq.bit_length() - 2:
            half = kept_rows.shape[0] // 2
            sent_rows = kept_rows[half:] + got_rows[half:]
            kept_rows = kept_rows[:half] + got_rows[:half]
    hot = hot_rows(tuple(seq_order), ids_by_seq, n_rows) if aligned else ids_by_seq
    other, got_rows, hot = lax.optimization_barrier((other, got_rows, hot))
    rows = kept.shape[1]
    total = [kept[0] + other[rows : 2 * rows], sent[0] + other[:rows]]
    loss = loss + other[2 * rows :, :LANES]
    part = n_dim // 2
    pair = (0, 1 << seq_bits[0])
    moved = []
    for r in seq_order:
        block = []
        for d in pair:
            k = seq_order.index(r ^ d)
            spans = [slice(h * n_seq * part + k * part, h * n_seq * part + (k + 1) * part) for h in range(2)]
            block += [chunk[span] for chunk in total for span in spans]
        if r == pair[1]:
            block.append(jnp.concatenate([loss] * (n_neg // LANES), axis=1))
        block = jnp.concatenate(block, axis=0)
        moved.append(send(block, "seq", r) if r else block)
    n_near, top = n_item // 2, 1 << shared[0]
    if aligned:
        sent = spread_rows(seq_order, per_panel, panel_owner, moved, hot, loss, n_near, n_rows)
    else:
        source = s ^ jnp.array(seq_order, i32)
        ids, owner = ids_by_seq[source], panel_owner[source // per_panel]
        hot = (ids[:, :, None] == jnp.arange(n_rows, dtype=i32)).astype(f32)
        loss = loss + moved[seq_order.index(pair[1])][4 * n_dim :, :LANES]
        moved = jnp.stack([block[: 4 * n_dim] for block in moved])
        spread = jnp.einsum("pdc,pcr->pdr", moved, hot, precision=high)
        mine = (owner[None, :] == (i ^ jnp.arange(n_near, dtype=i32))[:, None]).astype(f32)
        sent = jnp.sum(mine[:, :, None, None] * spread[None], axis=1)
        sent = sent.reshape(n_near, 4 * n_dim, -1, LANES).transpose(0, 2, 1, 3).reshape(n_near, -1, LANES)
        sent = [jnp.concatenate([sent[r], loss], axis=0) for r in range(n_near)]

    taken = [send(sent[r], "item", r) if r else sent[r] for r in range(n_near)]
    which = [[0], [1], [2], list(range(3, n_near))]
    table = [gather_pieces(jnp.stack([taken[r] for r in members]), "seq", seq_bits[1:]) for members in which]
    members, rest_order = sum(which, []), orders(seq_bits[1:])
    if aligned:
        table_grad, mean_loss, event_grad = assemble(table, kept_rows, got_rows, rest_order, pair, members, n_item, n_dim, n_rows, group_len * n_item)
        mean_loss = mean_loss.reshape(())
    else:
        table = jnp.stack([jnp.concatenate(groups, axis=0) for groups in zip(*table)])
        event_grad = kept_rows + got_rows
        mean_loss = jnp.sum(table[:, :, -1, 0]) / (group_len * n_item)
        table = table[:, :, :-EXTRA].reshape(len(rest_order), n_near, -1, 2, 2, n_dim, LANES).transpose(1, 4, 0, 3, 2, 5, 6)
        table = table.reshape(n_item, n_seq, -1, n_dim, LANES)
        table = true_order(table, [r ^ chunk for r in members for chunk in (0, top)], i).swapaxes(0, 1)
        table = true_order(table, [r ^ d for r in rest_order for d in pair], s)
        table_grad = table.transpose(2, 4, 0, 1, 3).reshape(n_rows, width)
    return (mean_loss, event_grad, table_grad)


def solution(mesh):
    placed = (
        P("item", "seq", None),
        P(),
        P(),
        P(),
        P("item", None),
        P("item", None),
        P(),
        P(),
        P("item", "seq"),
        P("item", "seq"),
    )
    return jax.shard_map(
        per_device,
        mesh=mesh,
        in_specs=placed,
        out_specs=(P(), P("item", "seq", None), P("item", None)),
        check_vma=False,
    )
```

```python
import functools

import jax
import jax.numpy as jnp
from jax import lax
from jax.experimental import pallas as pl
from jax.experimental.pallas import tpu as pltpu
from jax.sharding import PartitionSpec as P

H = 16
LANES = 128
EXTRA = 8

beta_weight = 0.75
epsilon = 1e-05

f32, bf16, i32 = jnp.float32, jnp.bfloat16, jnp.int32
high = lax.Precision.HIGH
NN, NT = ((1,), (0,)), ((1,), (1,))
params = pltpu.CompilerParams(vmem_limit_bytes=40 * 2**20)
alone = pltpu.CompilerParams(vmem_limit_bytes=62 * 2**20)


def swap(block, axis, bit):
    size = lax.axis_size(axis)
    return lax.ppermute(block, axis, [(i, i ^ (1 << bit)) for i in range(size)])


def send(block, axis, r):
    size = lax.axis_size(axis)
    return lax.ppermute(block, axis, [(i, i ^ r) for i in range(size)])


def bits_of(size):
    return list(range(size.bit_length() - 1))[::-1]


def two_orders(size):
    up = bits_of(size)
    return [up, up[:-2] + up[:-3:-1]]


def orders(bits):
    order = [0]
    for bit in bits:
        order = order + [r ^ (1 << bit) for r in order]
    return order


def gather_pieces(block, axis, bits):
    pieces = [block]
    for bit in bits:
        pieces = pieces + [swap(piece, axis, bit) for piece in pieces]
    return pieces


def reduce_steps(kept, sent, axis, bits):
    for n, bit in enumerate(bits):
        got = swap(sent, axis, bit)
        if n == len(bits) - 1:
            return (kept + got)[0]
        half = kept.shape[0] // 2
        sent = kept[half:] + got[half:]
        kept = kept[:half] + got[:half]


def true_order(stacked, order, index):
    place = [0] * len(order)
    for k, r in enumerate(order):
        place[r] = k
    return stacked[jnp.array(place, i32)[index ^ jnp.arange(len(order), dtype=i32)]]


def split(x):
    top = x.astype(bf16)
    return top, (x - top.astype(f32)).astype(bf16)


def dot(a, b, dims):
    return lax.dot_general(a, b, (dims, ((), ())), preferred_element_type=f32)


def dot3(a, b, dims):
    return dot(a[0], b[0], dims) + (dot(a[0], b[1], dims) + dot(a[1], b[0], dims))


def silu(x):
    return x / (1.0 + jnp.exp(jnp.minimum(-x, 87.0)))


def pick_kernel(plan, ids_hbm, table_hbm, *refs):
    _, n_item, _, item_orders, _ = plan
    outs, (ids, table, picked, sems) = refs[:4], refs[4:]
    n_neg = ids.shape[1]
    n_step, step = table.shape[:2]
    me, item = lax.axis_index("seq"), lax.axis_index("item")
    copies = [pltpu.make_async_copy(ids_hbm, ids, sems.at[n_step])]
    copies += [
        pltpu.make_async_copy(table_hbm.at[pl.ds(k * step, step)], table.at[k], sems.at[k]) for k in range(n_step)
    ]
    for copy in copies:
        copy.start()
    copies[0].wait()
    row = ids[pl.ds(me, 1), :].astype(f32)
    col = jnp.broadcast_to(row, (LANES, n_neg)).T
    lane = lax.broadcasted_iota(i32, (n_neg, LANES), 1)
    for k in range(n_step):
        hot = [
            jnp.where(col == (lane + (k * step + c)).astype(f32), 1.0, 0.0).astype(bf16) for c in range(0, step, LANES)
        ]
        hot = jnp.concatenate(hot, axis=1)
        copies[1 + k].wait()
        t_hi, t_lo = split(table[k])
        part = dot(hot, t_hi, NN) + dot(hot, t_lo, NN)
        picked[...] = part if k == 0 else picked[...] + part
    n_part = n_neg // (2 * n_item)
    for half in range(2):
        for m, r in enumerate(item_orders[half]):
            first = half * (n_neg // 2) + (item ^ r) * n_part
            out = outs[2 * half + m // (n_item // 2)]
            out[m % (n_item // 2)] = picked[pl.ds(pl.multiple_of(first, n_part), n_part)]


def pick_rows(plan, ids, table):
    n_rows, width = table.shape
    n_item, n_neg = plan[1], ids.shape[1]
    step = 512
    out = (n_item // 2, n_neg // (2 * n_item), width)
    return pl.pallas_call(
        functools.partial(pick_kernel, plan),
        in_specs=[pl.BlockSpec(memory_space=pltpu.HBM)] * 2,
        out_specs=[pl.BlockSpec(memory_space=pltpu.VMEM)] * 4,
        out_shape=[jax.ShapeDtypeStruct(out, f32)] * 4,
        scratch_shapes=[
            pltpu.VMEM(ids.shape, i32),
            pltpu.VMEM((n_rows // step, step, width), f32),
            pltpu.VMEM((n_neg, width), f32),
            pltpu.SemaphoreType.DMA((n_rows // step + 1,)),
        ],
        compiler_params=alone,
        cost_estimate=pl.CostEstimate(flops=4 * n_neg * n_rows * width, bytes_accessed=4 * n_rows * width, transcendentals=0),
        name="pick_rows",
    )(ids, table)


def prepare_kernel(x_ref, u_ref, q_ref, gates_ref, queries_ref):
    both = silu(dot3(split(x_ref[...]), split(jnp.concatenate([u_ref[...], q_ref[...]], axis=1)), NN))
    gates_ref[...], queries_ref[...] = both[:, :LANES], both[:, LANES:]


def prepare(rows_in, w_uvqk):
    tok, width = rows_in.shape
    n = width // LANES
    own = pl.BlockSpec((tok, LANES), lambda j: (0, j))
    return pl.pallas_call(
        prepare_kernel,
        grid=(n,),
        in_specs=[
            pl.BlockSpec((tok, width), lambda j: (0, 0)),
            pl.BlockSpec((width, LANES), lambda j: (0, j)),
            pl.BlockSpec((width, LANES), lambda j: (0, 2 * n + j)),
        ],
        out_specs=[own, own],
        out_shape=[jax.ShapeDtypeStruct((tok, width), f32)] * 2,
        compiler_params=params,
        cost_estimate=pl.CostEstimate(flops=12 * tok * width * width, bytes_accessed=2 * width * width * 4, transcendentals=0),
        name="prepare",
    )(rows_in, w_uvqk, w_uvqk)


def attend_kernel(order, n_seq, lengths, *refs):
    x_refs, (q_ref, v_ref, k_ref, out_ref, x_hi, x_lo, allowed) = refs[:n_seq], refs[n_seq:]
    tok = q_ref.shape[0]
    head = x_hi.shape[1] // H

    @pl.when(pl.program_id(0) == 0)
    def _():
        me = lax.axis_index("seq")
        q_pos = me * tok + lax.broadcasted_iota(i32, (tok, tok), 0)
        col = lax.broadcasted_iota(i32, (tok, tok), 1)

        def user(pos):
            ids, end = jnp.zeros_like(pos), 0
            for k in range(lengths.shape[1]):
                end = end + lengths[0, k]
                ids = ids + (pos >= end).astype(i32)
            return ids

        q_user = user(q_pos)
        for n in range(n_seq):
            span = pl.ds(n * tok, tok)
            x_hi[span], x_lo[span] = split(x_refs[n][...])
            k_pos = (me ^ order[n]) * tok + col
            seen = (q_user == user(k_pos)) & (q_pos >= k_pos)
            allowed[:, span] = seen.astype(f32)

    x = (x_hi[...], x_lo[...])
    vk = silu(dot3(x, split(jnp.concatenate([v_ref[...], k_ref[...]], axis=1)), NN))
    v_hi, v_lo = split(vk[:, :LANES])
    k_hi, k_lo = split(vk[:, LANES:])
    k_both = jnp.concatenate([k_hi, k_lo], axis=1)
    v_both = jnp.concatenate([v_hi, v_lo], axis=1)
    queries = q_ref[...]
    n_heads = LANES // head
    of_head = lax.broadcasted_iota(i32, (tok, LANES), 1) // head
    stacked = jnp.concatenate([jnp.where(of_head == h, queries, 0.0) for h in range(n_heads)], axis=0)
    q_hi, q_lo = split(stacked)
    scores = dot(jnp.concatenate([q_hi, q_hi], axis=1), k_both, NT) + dot(q_lo, k_hi, NT)
    seen = allowed[...]
    weights = silu(scores) * jnp.concatenate([seen] * n_heads, axis=0)
    w_hi, w_lo = split(weights)
    wide = dot(w_hi, v_both, NN)
    mine = wide[:, :LANES] + wide[:, LANES:] + dot(w_lo, v_hi, NN)
    total = mine[:tok]
    for h in range(1, n_heads):
        total = jnp.where(of_head == h, mine[h * tok : (h + 1) * tok], total)
    out_ref[...] = total


def attend(lengths, pieces, order, queries, w_uvqk, first, count):
    tok, width = pieces[0].shape
    n_seq = len(pieces)
    whole = pl.BlockSpec((tok, width), lambda j: (0, 0))
    n = width // LANES
    v = pl.BlockSpec((width, LANES), lambda j: (0, n + first + j))
    k = pl.BlockSpec((width, LANES), lambda j: (0, 3 * n + first + j))
    return pl.pallas_call(
        functools.partial(attend_kernel, order, n_seq),
        grid=(count,),
        in_specs=[pl.BlockSpec(memory_space=pltpu.SMEM)]
        + [whole] * n_seq
        + [pl.BlockSpec((tok, LANES), lambda j: (0, first + j)), v, k],
        out_specs=pl.BlockSpec((tok, LANES), lambda j: (0, j)),
        out_shape=jax.ShapeDtypeStruct((tok, count * LANES), f32),
        scratch_shapes=[
            pltpu.VMEM((n_seq * tok, width), bf16),
            pltpu.VMEM((n_seq * tok, width), bf16),
            pltpu.VMEM((tok, n_seq * tok), f32),
        ],
        compiler_params=params,
        cost_estimate=pl.CostEstimate(flops=count * 2000000000, bytes_accessed=2 * width * width * 4, transcendentals=0),
        name="attend",
    )(lengths, *pieces, queries, w_uvqk, w_uvqk)


def project_kernel(n_parts, words, *refs):
    parts, (gates, gain, w_out, rows_in, targets, out_ref) = refs[:n_parts], refs[n_parts:]
    tok, width = rows_in.shape
    attended = jnp.concatenate([p[...] for p in parts], axis=1)
    centered = attended - jnp.mean(attended, axis=1, keepdims=True)
    variance = jnp.mean(centered * centered, axis=1, keepdims=True)
    normed = centered * lax.rsqrt(variance + epsilon) * gain[...]
    gated = split(normed * gates[...])
    out_ref[:tok] = rows_in[...] + dot3(gated, split(w_out[...]), NN)
    out_ref[tok:] = jnp.zeros((EXTRA, width), f32)
    out_ref[tok : tok + 1, :tok] = targets[...].astype(f32)
    for k in range(words.shape[1]):
        out_ref[tok + 1 : tok + 2, k * LANES : (k + 1) * LANES] = jnp.full((1, LANES), words[0, k].astype(f32))


def project(words, parts, gates, gain, w_out, rows_in, targets):
    tok, width = rows_in.shape
    return pl.pallas_call(
        lambda words, *refs: project_kernel(len(parts), words, *refs),
        in_specs=[pl.BlockSpec(memory_space=pltpu.SMEM)] + [pl.BlockSpec(memory_space=pltpu.VMEM)] * (len(parts) + 5),
        out_specs=pl.BlockSpec(memory_space=pltpu.VMEM),
        out_shape=jax.ShapeDtypeStruct((tok + EXTRA, width), f32),
        compiler_params=params,
        cost_estimate=pl.CostEstimate(flops=6 * tok * width * width, bytes_accessed=2 * width * width * 4, transcendentals=0),
        name="project",
    )(words, *parts, gates, gain, w_out, rows_in, targets)


def transpose_kernel(*refs):
    o_refs, (o_hi, o_lo) = refs[:-2], refs[-2:]
    tok = o_refs[0].shape[0] - EXTRA
    for n, o_ref in enumerate(o_refs):
        span = pl.ds(n * tok, tok)
        o_hi[:, span], o_lo[:, span] = split(o_ref[:tok].T)


def transpose_outputs(outputs):
    tok, width = outputs[0].shape[0] - EXTRA, outputs[0].shape[1]
    vmem = pl.BlockSpec(memory_space=pltpu.VMEM)
    return pl.pallas_call(
        transpose_kernel,
        in_specs=[vmem] * len(outputs),
        out_specs=[vmem] * 2,
        out_shape=[jax.ShapeDtypeStruct((width, tok * len(outputs)), bf16)] * 2,
        compiler_params=params,
        cost_estimate=pl.CostEstimate(flops=0, bytes_accessed=2**22, transcendentals=0),
        name="transpose_outputs",
    )(*outputs)


def loss_kernel(plan, o_hi, o_lo, *refs):
    n_seq, n_item, seq_order, item_orders, aligned = plan
    o_refs, refs = refs[:n_seq], refs[n_seq:]
    n_in = 4 if aligned else 1
    n_refs, panel_refs, refs = refs[:n_in], refs[n_in : 2 * n_in], refs[2 * n_in :]
    loss_ref, g_ref, n_hi, n_lo, g_hi, g_lo, panel = refs
    me, item = lax.axis_index("seq"), lax.axis_index("item")
    n_neg, width = n_hi.shape
    tok = o_refs[0].shape[0] - EXTRA

    if aligned:
        n_part = n_neg // (2 * n_item)
        for half in range(2):
            for m, r in enumerate(item_orders[half]):
                source = n_refs[2 * half + m // (n_item // 2)]
                rows = source[pl.ds((m % (n_item // 2)) * n_part, n_part)]
                place = pl.ds(pl.multiple_of(half * (n_neg // 2) + (item ^ r) * n_part, n_part), n_part)
                n_hi[place], n_lo[place] = split(rows)
    else:
        n_hi[...], n_lo[...] = split(n_refs[0][...])

    negatives = (n_hi[...], n_lo[...])
    loss = jnp.zeros((1, 2 * tok), f32)
    columns = me * n_neg + lax.broadcasted_iota(i32, (n_neg, 2 * tok), 0)
    for p in range(n_seq // 2):
        both = o_refs[2 * p], o_refs[2 * p + 1]
        span = pl.ds(2 * p * tok, 2 * tok)
        target = jnp.concatenate([b[tok : tok + 1, :tok] for b in both], axis=1).astype(i32)
        words = jnp.concatenate([b[tok + 1 : tok + 2, :tok] for b in both], axis=1).astype(i32)
        logits = dot3(negatives, (o_hi[:, span], o_lo[:, span]), NN)
        is_target = columns == target
        live = jnp.bitwise_and(jnp.right_shift(jnp.broadcast_to(words, columns.shape), columns // LANES), 1).astype(f32)
        weight = jnp.where(is_target, beta_weight, live)
        signed = jnp.where(is_target, -logits, logits)
        small = jnp.exp(-jnp.abs(logits))
        loss = loss + jnp.sum(weight * (jnp.maximum(signed, 0.0) + jnp.log1p(small)), axis=0, keepdims=True)
        chance = jnp.where(signed >= 0.0, 1.0, small) / (1.0 + small)
        grad = jnp.where(is_target, -weight, weight) * chance
        g_ref[:, span] = grad
        g_hi[:, span], g_lo[:, span] = split(grad)
    loss_ref[...] = jnp.full((EXTRA, LANES), jnp.sum(loss))
    whole = dot3((o_hi[...], o_lo[...]), (g_hi[...], g_lo[...]), NT)
    if not aligned:
        panel_refs[0][...] = whole
        return
    panel[...] = whole
    n_dim = width // (n_seq * n_item)
    part = n_dim // 2
    for half in range(2):
        for m, r in enumerate(item_orders[half]):
            out = panel_refs[2 * half + m // (n_item // 2)]
            k = m % (n_item // 2)
            for n, q in enumerate(seq_order):
                first = (me ^ q) * (n_item * n_dim) + (item ^ r) * n_dim + half * part
                out[k, n * part : (n + 1) * part] = panel[pl.ds(pl.multiple_of(first, part), part)]


def loss_terms(transposed, outputs, negatives, plan, n_neg):
    n_seq, n_item, _, _, aligned = plan
    tok, width = outputs[0].shape[0] - EXTRA, outputs[0].shape[1]
    group_len = tok * n_seq
    vmem = pl.BlockSpec(memory_space=pltpu.VMEM)
    if aligned:
        panel = [jax.ShapeDtypeStruct((n_item // 2, width // (2 * n_item), n_neg), f32)] * 4
    else:
        panel = [jax.ShapeDtypeStruct((width, n_neg), f32)]
    loss = jax.ShapeDtypeStruct((EXTRA, LANES), f32)
    grad = jax.ShapeDtypeStruct((n_neg, group_len), f32)
    parts = [jax.ShapeDtypeStruct((n_neg, width), bf16)] * 2
    out_shape = [*panel, loss, grad, *parts]
    return pl.pallas_call(
        functools.partial(loss_kernel, plan),
        in_specs=[vmem] * (2 + n_seq + len(negatives)),
        out_specs=[vmem] * len(out_shape),
        out_shape=out_shape,
        scratch_shapes=[pltpu.VMEM((n_neg, group_len), bf16)] * 2 + [pltpu.VMEM((width, n_neg), f32)],
        compiler_params=params,
        cost_estimate=pl.CostEstimate(flops=12 * group_len * width * n_neg, bytes_accessed=16 * n_neg * width, transcendentals=0),
        name="loss_terms",
    )(*transposed, *outputs, *negatives)


def rows_kernel(n_seq, grad, n_hi, n_lo, kept_rows, sent_rows):
    tok = grad.shape[1] // n_seq
    negatives = (n_hi[...], n_lo[...])
    for p in range(n_seq // 2):
        rows = dot3(split(grad[:, 2 * p * tok : 2 * (p + 1) * tok].T), negatives, NN)
        for k in range(2):
            n = 2 * p + k
            target_ref = kept_rows if n < n_seq // 2 else sent_rows
            target_ref[n % (n_seq // 2)] = rows[k * tok : (k + 1) * tok]


def event_rows(grad, n_hi, n_lo, n_seq):
    n_neg, group_len = grad.shape
    width = n_hi.shape[1]
    vmem = pl.BlockSpec(memory_space=pltpu.VMEM)
    return pl.pallas_call(
        functools.partial(rows_kernel, n_seq),
        in_specs=[vmem] * 3,
        out_specs=[vmem] * 2,
        out_shape=[jax.ShapeDtypeStruct((n_seq // 2, group_len // n_seq, width), f32)] * 2,
        compiler_params=params,
        cost_estimate=pl.CostEstimate(flops=6 * group_len * width * n_neg, bytes_accessed=8 * n_neg * width, transcendentals=0),
        name="event_rows",
    )(grad, n_hi, n_lo)


def pieces_kernel(spread, owners, which, loss, outs):
    n_dim, n_rows = spread[0].shape
    item = lax.axis_index("item")
    for r, out in zip(which, outs):
        total = jnp.where(owners[0] == item ^ r, spread[0], 0.0)
        for p in range(1, len(owners)):
            total = total + jnp.where(owners[p] == item ^ r, spread[p], 0.0)
        for c in range(n_rows // LANES):
            out[c * n_dim : (c + 1) * n_dim] = total[:, c * LANES : (c + 1) * LANES]
        out[n_rows // LANES * n_dim :] = loss


def owners_of(order, per_panel, owner):
    return [owner[(lax.axis_index("seq") ^ r) // per_panel] for r in order]


def spread_kernel(order, per_panel, which, owner, ids, loss, *refs):
    moved, outs = refs[: len(order)], refs[len(order) :]
    n_dim, n_neg = moved[0].shape
    n_rows = (outs[0].shape[0] - EXTRA) // n_dim * LANES
    row = lax.broadcasted_iota(i32, (n_rows, n_neg), 0)
    spread = []
    for p, r in enumerate(order):
        hot = jnp.where(row == ids[pl.ds(lax.axis_index("seq") ^ r, 1), :], 1.0, 0.0).astype(bf16)
        both = dot(jnp.concatenate(split(moved[p][:n_dim]), axis=0), hot, NT)
        spread.append(both[:n_dim] + both[n_dim:])
    total = loss[...]
    for block in moved:
        if block.shape[0] > n_dim:
            total = total + block[n_dim:, :LANES]
    pieces_kernel(spread, owners_of(order, per_panel, owner), which, total, outs)


def spread_rows(order, per_panel, owner, moved, ids, loss, n_item, n_rows):
    vmem = pl.BlockSpec(memory_space=pltpu.VMEM)
    smem = pl.BlockSpec(memory_space=pltpu.SMEM)
    n_dim = moved[0].shape[0]
    out = jax.ShapeDtypeStruct((n_rows // LANES * n_dim + EXTRA, LANES), f32)
    return pl.pallas_call(
        functools.partial(spread_kernel, order, per_panel, tuple(range(n_item))),
        in_specs=[smem, vmem, vmem] + [vmem] * len(moved),
        out_specs=[vmem] * n_item,
        out_shape=[out] * n_item,
        compiler_params=params,
        cost_estimate=pl.CostEstimate(flops=4 * len(moved) * moved[0].size * n_rows, bytes_accessed=2**21, transcendentals=0),
        name="spread_rows",
    )(owner, ids, loss, *moved)


def assemble_kernel(order, pair, members, n_item, n_dim, events, kept, got, *refs):
    groups, (out_ref, loss_ref, event_ref, quarter) = refs[:-4], refs[-4:]
    event_ref[...] = kept[...] + got[...]
    n_rest = len(order)
    me, item = lax.axis_index("seq"), lax.axis_index("item")
    cols = n_item * n_dim
    n_tiles = out_ref.shape[0] // LANES
    block = pl.program_id(0)

    def places(k):
        return [(groups[g], m) for g in range(k, len(groups), n_rest) for m in range(groups[g].shape[0])]

    for c in range(n_tiles):
        for k, q in enumerate(order):
            for d, across in enumerate(pair):
                first = ((block * n_tiles + c) * 4 + 2 * d) * n_dim
                for r, (group, m) in zip(members, places(k)):
                    for chunk in range(2):
                        place = pl.ds(pl.multiple_of((item ^ r ^ (chunk * n_item // 2)) * n_dim, n_dim), n_dim)
                        quarter[2 * k + d, place] = group[m, pl.ds(pl.multiple_of(first + chunk * n_dim, n_dim), n_dim)]
                place = pl.ds(pl.multiple_of((me ^ q ^ across) * cols, cols), cols)
                out_ref[c * LANES : (c + 1) * LANES, place] = quarter[2 * k + d].T

    @pl.when(block == 0)
    def _():
        total = jnp.zeros((EXTRA, LANES), f32)
        for k in range(n_rest):
            for group, m in places(k):
                total = total + group[m, group.shape[1] - EXTRA :]
        loss_ref[0, 0] = jnp.sum(total) / (EXTRA * LANES * events)


def assemble(table, kept, got, order, pair, members, n_item, n_dim, n_rows, events):
    width = n_item * n_dim * len(order) * len(pair)
    step = min(n_rows, 512)
    pieces = sum(table, [])
    rows = pl.BlockSpec((1, kept.shape[1] * step // n_rows, width), lambda j: (0, j, 0))
    return pl.pallas_call(
        functools.partial(assemble_kernel, order, pair, members, n_item, n_dim, events),
        grid=(n_rows // step,),
        in_specs=[rows, rows] + [pl.BlockSpec(memory_space=pltpu.VMEM)] * len(pieces),
        out_specs=[pl.BlockSpec((step, width), lambda j: (j, 0)), pl.BlockSpec(memory_space=pltpu.SMEM), rows],
        out_shape=[
            jax.ShapeDtypeStruct((n_rows, width), f32),
            jax.ShapeDtypeStruct((1, 1), f32),
            jax.ShapeDtypeStruct(kept.shape, f32),
        ],
        scratch_shapes=[pltpu.VMEM((2 * len(order), n_item * n_dim, LANES), f32)],
        compiler_params=params,
        cost_estimate=pl.CostEstimate(flops=0, bytes_accessed=8 * n_rows * width, transcendentals=0),
        name="assemble",
    )(kept, got, *pieces)


def per_device(
    events,
    w_uvqk,
    out_gain,
    w_out,
    item_table,
    user_lengths,
    neg_ids,
    panel_owner,
    block_mask,
    targets,
):
    rows_in = events[0]
    tok, width = rows_in.shape
    n_rows = item_table.shape[0]
    n_seq, n_item = lax.axis_size("seq"), lax.axis_size("item")
    s, i = lax.axis_index("seq").astype(i32), lax.axis_index("item").astype(i32)
    group_len = tok * n_seq
    seq_bits = bits_of(n_seq)
    seq_order = orders(seq_bits)
    bit_lists = two_orders(n_item)
    shared = bit_lists[0][:-2]
    item_orders = [orders(bits) for bits in bit_lists]
    flat_ids = neg_ids.reshape(-1)
    n_neg = flat_ids.shape[0] // n_seq
    per_panel = neg_ids.shape[1] // n_neg
    n_part = n_neg // (2 * n_item)
    n_dim = width // (n_seq * n_item)
    aligned = n_part % 16 == 0 and n_dim % 16 == 0 and (n_item * n_dim) % LANES == 0
    plan = (n_seq, n_item, tuple(seq_order), tuple(tuple(o) for o in item_orders), aligned)

    ids_by_seq = flat_ids.reshape(n_seq, n_neg)
    rel = i ^ jnp.array(item_orders, i32)
    root = panel_owner[s // per_panel]
    if aligned:
        parts = pick_rows(plan, ids_by_seq, item_table)
        parts = [parts[:2], parts[2:]]
    else:
        spot = s * n_neg + rel[:, :, None] * n_part + jnp.arange(n_part, dtype=i32)
        spot = spot + jnp.array([0, n_neg // 2], i32)[:, None, None]
        rows = item_table[flat_ids[spot.reshape(-1)]].reshape(2, n_item, n_part, width)
        parts = [(part[: n_item // 2], part[n_item // 2 :]) for part in rows]
    pieces = gather_pieces(rows_in, "seq", seq_bits)
    gates, queries = prepare(rows_in, w_uvqk)
    groups = width // LANES
    attended = [
        attend(user_lengths, pieces, seq_order, queries, w_uvqk, first, count)
        for first, count in ((0, groups // 4), (groups // 4, groups - groups // 4))
    ]
    for step in range(2):
        others = [swap(parts[half][1], "item", bits[-1 - step]) for half, bits in enumerate(bit_lists)]
        if step == 1:
            *others, attended[0] = lax.optimization_barrier((*others, attended[0]))
        for half, bits in enumerate(bit_lists):
            kept, other = parts[half][0], others[half]
            same = ((i ^ root) >> bits[-1 - step]) & 1 == 0
            cut = kept.shape[0] if step == 1 else kept.shape[0] // 2
            parts[half] = (jnp.where(same, kept[:cut], other[:cut]), jnp.where(same, kept[cut:], other[cut:]))
    both = jnp.stack([part[0] for part in parts])
    for bit in shared[:0:-1]:
        cut = both.shape[1] // 2
        other = swap(both[:, cut:], "item", bit)
        both = jnp.where(((i ^ root) >> bit) & 1 == 0, both[:, :cut], other)
    other = swap(both, "item", shared[0])
    same = ((i ^ root) >> shared[0]) & 1 == 0
    parts = [
        jnp.where(same, both[half], jnp.concatenate([other[half, 1:], other[half, :1]], axis=0)) for half in range(2)
    ]
    for step in range(1, len(bit_lists[0]) - 1):
        for half, bits in enumerate(bit_lists):
            parts[half] = jnp.concatenate([parts[half], swap(parts[half], "item", bits[step])], axis=0)
    negatives = []
    for half, bits in enumerate(bit_lists):
        negatives += [parts[half], swap(parts[half], "item", bits[-1])]
    if aligned:
        negatives = [n.reshape(-1, width) for n in negatives]
    else:
        negatives = [
            true_order(jnp.concatenate(negatives[2 * half : 2 * half + 2], axis=0), item_orders[half], i)
            for half in range(2)
        ]
        negatives = [jnp.concatenate([n.reshape(-1, width) for n in negatives], axis=0)]

    own_outputs = project(block_mask, attended, gates, out_gain[None], w_out, rows_in, targets)
    outputs = gather_pieces(own_outputs, "seq", seq_bits)

    *panel, loss, grad, n_hi, n_lo = loss_terms(transpose_outputs(outputs), outputs, negatives, plan, n_neg)
    kept_rows, sent_rows = event_rows(grad, n_hi, n_lo, n_seq)
    if not aligned:
        blocks = panel[0].reshape(n_seq, n_item, 2, n_dim // 2, n_neg).transpose(2, 1, 0, 3, 4)
        panel = []
        for half in range(2):
            mine = blocks[half][rel[half]][:, s ^ jnp.array(seq_order, i32)].reshape(n_item, -1, n_neg)
            panel += [mine[: n_item // 2], mine[n_item // 2 :]]

    for step in range(2):
        got = [swap(panel[2 * half + 1], "item", bits[-1 - step]) for half, bits in enumerate(bit_lists)]
        if step == 0:
            *got, kept_rows, sent_rows = lax.optimization_barrier((*got, kept_rows, sent_rows))
        cut = panel[0].shape[0] // 2
        panel = [
            k[:cut] + g[:cut] if part == 0 else k[cut:] + g[cut:]
            for k, g in zip(panel[::2], got)
            for part in range(2)
        ]
    kept, sent = panel[::2], panel[1::2]
    kept, sent = jnp.concatenate(kept, axis=1), jnp.concatenate(sent, axis=1)
    for bit in shared[:0:-1]:
        got = swap(sent, "item", bit)
        cut = kept.shape[0] // 2
        kept, sent = kept[:cut] + got[:cut], kept[cut:] + got[cut:]
    tail = jnp.concatenate([loss] * (n_neg // LANES), axis=1)
    mine = jnp.concatenate([kept[0], sent[0], tail], axis=0)
    other = swap(mine, "item", shared[0])
    for n, bit in enumerate(seq_bits[::-1]):
        got_rows = swap(sent_rows, "seq", bit)
        if n < n_seq.bit_length() - 2:
            half = kept_rows.shape[0] // 2
            sent_rows = kept_rows[half:] + got_rows[half:]
            kept_rows = kept_rows[:half] + got_rows[:half]
    other, got_rows = lax.optimization_barrier((other, got_rows))
    rows = kept.shape[1]
    total = [kept[0] + other[rows : 2 * rows], sent[0] + other[:rows]]
    loss = loss + other[2 * rows :, :LANES]
    part = n_dim // 2
    pair = (0, 1 << seq_bits[0])
    moved = []
    for r in seq_order:
        block = []
        for d in pair:
            k = seq_order.index(r ^ d)
            spans = [slice(h * n_seq * part + k * part, h * n_seq * part + (k + 1) * part) for h in range(2)]
            block += [chunk[span] for chunk in total for span in spans]
        if r == pair[1]:
            block.append(jnp.concatenate([loss] * (n_neg // LANES), axis=1))
        block = jnp.concatenate(block, axis=0)
        moved.append(send(block, "seq", r) if r else block)
    n_near, top = n_item // 2, 1 << shared[0]
    if aligned:
        sent = spread_rows(seq_order, per_panel, panel_owner, moved, ids_by_seq, loss, n_near, n_rows)
    else:
        source = s ^ jnp.array(seq_order, i32)
        ids, owner = ids_by_seq[source], panel_owner[source // per_panel]
        hot = (ids[:, :, None] == jnp.arange(n_rows, dtype=i32)).astype(f32)
        loss = loss + moved[seq_order.index(pair[1])][4 * n_dim :, :LANES]
        moved = jnp.stack([block[: 4 * n_dim] for block in moved])
        spread = jnp.einsum("pdc,pcr->pdr", moved, hot, precision=high)
        mine = (owner[None, :] == (i ^ jnp.arange(n_near, dtype=i32))[:, None]).astype(f32)
        sent = jnp.sum(mine[:, :, None, None] * spread[None], axis=1)
        sent = sent.reshape(n_near, 4 * n_dim, -1, LANES).transpose(0, 2, 1, 3).reshape(n_near, -1, LANES)
        sent = [jnp.concatenate([sent[r], loss], axis=0) for r in range(n_near)]

    taken = [send(sent[r], "item", r) if r else sent[r] for r in range(n_near)]
    which = [[0], [1], [2], list(range(3, n_near))]
    table = [gather_pieces(jnp.stack([taken[r] for r in members]), "seq", seq_bits[1:]) for members in which]
    members, rest_order = sum(which, []), orders(seq_bits[1:])
    if aligned:
        table_grad, mean_loss, event_grad = assemble(table, kept_rows, got_rows, rest_order, pair, members, n_item, n_dim, n_rows, group_len * n_item)
        mean_loss = mean_loss.reshape(())
    else:
        table = jnp.stack([jnp.concatenate(groups, axis=0) for groups in zip(*table)])
        event_grad = kept_rows + got_rows
        mean_loss = jnp.sum(table[:, :, -1, 0]) / (group_len * n_item)
        table = table[:, :, :-EXTRA].reshape(len(rest_order), n_near, -1, 2, 2, n_dim, LANES).transpose(1, 4, 0, 3, 2, 5, 6)
        table = table.reshape(n_item, n_seq, -1, n_dim, LANES)
        table = true_order(table, [r ^ chunk for r in members for chunk in (0, top)], i).swapaxes(0, 1)
        table = true_order(table, [r ^ d for r in rest_order for d in pair], s)
        table_grad = table.transpose(2, 4, 0, 1, 3).reshape(n_rows, width)
    return (mean_loss, event_grad, table_grad)


def solution(mesh):
    placed = (
        P("item", "seq", None),
        P(),
        P(),
        P(),
        P("item", None),
        P("item", None),
        P(),
        P(),
        P("item", "seq"),
        P("item", "seq"),
    )
    return jax.shard_map(
        per_device,
        mesh=mesh,
        in_specs=placed,
        out_specs=(P(), P("item", "seq", None), P("item", None)),
        check_vma=False,
    )
```
